256 devices in a mesh: band: 4 (over x), space: 64 (over z, y, core).
Axes of the slice: x: 4, y: 4, z: 8, core: 2. Of those that a mesh axis runs over, the one named last changes fastest.
Arguments:
- lanczos_now: float32 [2, 4, 1048576], P(None, 'band', 'space'), may hold values from -16 to 16
- lanczos_prev: float32 [2, 4, 1048576], P(None, 'band', 'space'), may hold values from -6 to 6
- beta_prev: float32 [1], replicated, may hold values from 0.5 to 1.5
- orbitals: float32 [2, 4, 192, 192, 192], P(None, 'band', 'space'), may hold values from -6 to 6
- band_energy: float32 [4], P('band'), may hold values from -2 to -0.5
- occupied: float32 [2, 64, 1048576], P(None, 'band', 'space'), may hold values from -0.0034526698 to 0.0034526698
- local_pot: float32 [192, 192, 192], P('space'), may hold values from -1 to 1
- xc_kernel: float32 [192, 192, 192], P('space'), may hold values from -1.5 to -0.3
- miller: int32 [3, 1048576], P(None, 'space'), may hold values from 0 to 191, as said below
Outputs:
- lanczos_next: float32 [2, 4, 1048576], P(None, 'band', 'space')
- coefficients: float32 [1, 2], replicated
- potential: float32 [192, 192, 192], P('space')
The draws below stay inside these ranges and needn't reach their ends.
Inputs may be any that keep to these rules, and one draw needn't show every extreme that they name: `miller`: each column is a distinct grid point; the plane waves of the k-th block of 16384 columns have their second index in [k * 192 / 64, (k + 1) * 192 / 64).
All inputs are finite; a program needn't handle non-finite values.
Results may differ from the reference program's by a relative error of at most 0.0001.
Values sent between devices are 32-bit elements; how exact they have to be, the bound alone decides.
A program may use at most 64 MiB of HBM per device.

```python
import jax
import jax.numpy as jnp
from jax import lax

N = 192
NPW_DEV = 16384
STEPS = 1
WIN = 4
NOCC = 64
NPW = 1048576
N_SPACE = 64


def occupied_basis(key):
    values = jax.random.normal(key, (2, NOCC, NPW), jnp.float32)
    return jnp.clip(values, -5.0, 5.0) * (2.0 * NPW) ** (-0.5)


def draw_occupied(key, part):
    basis = occupied_basis(key)
    return basis


def draw_lanczos_now(key, part):
    basis = occupied_basis(key)
    key = jax.random.fold_in(key, 13)
    noise_key, pick_key, sign_key, weight_key = jax.random.split(key, 4)
    picked = 4
    chosen = jax.random.randint(pick_key, (WIN, picked), 0, NOCC)
    signs = (2 * jax.random.randint(sign_key, (WIN, picked), 0, 2) - 1).astype(jnp.float32)
    magnitudes = jax.random.uniform(weight_key, (WIN, picked), jnp.float32, 0.5, 1.5)
    weights = signs * magnitudes * 0.5
    scaled = basis * (2.0 * NPW) ** 0.5
    combined = jnp.zeros((2, WIN, NPW), jnp.float32)
    for column in range(picked):
        combined = combined + weights[None, :, column, None] * scaled[:, chosen[:, column], :]
    noise = 0.6 * jnp.clip(jax.random.normal(noise_key, (2, WIN, NPW), jnp.float32), -5.0, 5.0)
    return noise + 0.8 * combined


def draw_miller(key, part):
    key = jax.random.fold_in(key, 5)
    planes = N // N_SPACE
    subkeys = jax.random.split(key, N_SPACE)

    def choose_points(subkey):
        return jax.random.permutation(subkey, planes * N * N)[:NPW_DEV]
    local_points = jax.vmap(choose_points)(subkeys).astype(jnp.int32)
    owners = jnp.arange(N_SPACE, dtype=jnp.int32)[:, None]
    first_index = local_points // (planes * N)
    second_index = owners * planes + local_points // N % planes
    third_index = local_points % N
    return jnp.stack([first_index.reshape(-1), second_index.reshape(-1), third_index.reshape(-1)], axis=0)


def level_of(key, shape, cuts, smallest, largest):
    factor_of = 1.0
    for axis_at, shards_of in cuts:
        heights = jax.random.uniform(jax.random.fold_in(jax.random.fold_in(key, 6), axis_at), (shards_of,), jnp.float32, smallest / len(cuts), largest / len(cuts))
        factor_of = factor_of * jnp.repeat(jnp.exp(heights), shape[axis_at] // shards_of).reshape((-1,) + (1,) * (len(shape) - 1 - axis_at))
    return factor_of


def gaussian(key, shape, deviation, reach, cuts=(), held_as=jnp.bfloat16):
    values = deviation * jax.random.normal(key, shape, jnp.float32)
    if cuts:
        values = values * level_of(key, shape, cuts, -0.22, 0.18)
    return jnp.clip(values, -reach, reach).astype(held_as)


def setup_inputs(seed: int = 0) -> dict:
    arg_keys = jax.random.split(jax.random.key(seed), 10)
    lanczos_now = draw_lanczos_now(jax.random.fold_in(arg_keys[9], 71), 0)
    lanczos_prev = gaussian(arg_keys[1], (2, WIN, NPW), 1.0, 6.0, ((1, 4), (2, 64)), jnp.float32)
    beta_prev = jnp.clip(jax.random.uniform(arg_keys[2], (1,), jnp.float32, 0.5, 1.5), 0.5, 1.5)
    orbitals = gaussian(arg_keys[3], (2, WIN, N, N, N), 1.0, 6.0, ((1, 4), (2, 64)), jnp.float32)
    band_energy = jnp.clip(-2.0 + 1.5 * jax.random.uniform(arg_keys[4], (WIN,), jnp.float32) ** level_of(arg_keys[4], (WIN,), ((0, 4),), -0.2, 0.2), -2.0, -0.5)
    occupied = draw_occupied(jax.random.fold_in(arg_keys[9], 71), 0)
    local_pot = jnp.clip(jax.random.uniform(arg_keys[6], (N, N, N), jnp.float32, -1.0, 1.0) * level_of(arg_keys[6], (N, N, N), ((0, 64),), -0.4, 0.0), -1.0, 1.0)
    xc_kernel = jnp.clip(-1.5 + 1.2 * jax.random.uniform(arg_keys[7], (N, N, N), jnp.float32) ** level_of(arg_keys[7], (N, N, N), ((0, 64),), -0.2, 0.2), -1.5, -0.3)
    miller = draw_miller(jax.random.fold_in(arg_keys[9], 71), 0)
    return dict(lanczos_now=lanczos_now, lanczos_prev=lanczos_prev, beta_prev=beta_prev, orbitals=orbitals, band_energy=band_energy, occupied=occupied, local_pot=local_pot, xc_kernel=xc_kernel, miller=miller)


HIGH = lax.Precision.HIGHEST
KINETIC = 8.0
HARTREE = 4.0

def signed(indices):
    return jnp.where(indices < N // 2, indices, indices - N)

def reference(lanczos_now, lanczos_prev, beta_prev, orbitals, band_energy, occupied, local_pot, xc_kernel, miller):
    first_index = miller[0]
    second_index = miller[1]
    third_index = miller[2]
    squared_wave = signed(first_index) * signed(first_index) + signed(second_index) * signed(second_index) + signed(third_index) * signed(third_index)
    kinetic = KINETIC * squared_wave.astype(jnp.float32) / float(N * N)
    axis_values = signed(jnp.arange(N, dtype=jnp.int32))
    squared_grid = axis_values[:, None, None] * axis_values[:, None, None] + axis_values[None, :, None] * axis_values[None, :, None] + axis_values[None, None, :] * axis_values[None, None, :]
    coulomb = jnp.where(squared_grid > 0, HARTREE / jnp.maximum(squared_grid, 1).astype(jnp.float32), 0.0)
    complex_orbitals = orbitals[0] + 1j * orbitals[1]
    complex_occupied = occupied[0] + 1j * occupied[1]
    entries = float(2 * WIN * NPW)

    def operate(current):
        coeffs = current[0] + 1j * current[1]

        def to_real(values):
            placed = jnp.zeros((N, N, N), coeffs.dtype).at[first_index, second_index, third_index].set(values)
            return jnp.fft.ifftn(placed, norm='ortho')
        fields = lax.map(to_real, coeffs)
        density = 2.0 * lax.optimization_barrier(jnp.sum(jnp.real(jnp.conj(complex_orbitals) * fields), axis=0))
        hartree = jnp.real(jnp.fft.ifftn(coulomb * jnp.fft.fftn(density, norm='ortho'), norm='ortho'))
        potential = hartree + xc_kernel * density

        def to_waves(operands):
            values = local_pot * operands[0] + potential * operands[1]
            return jnp.fft.fftn(values, norm='ortho')[first_index, second_index, third_index]
        waves = lax.map(to_waves, (fields, complex_orbitals))
        lifted = (kinetic[None, :] - band_energy[:, None]) * coeffs + waves
        intersection = jnp.matmul(jnp.conj(complex_occupied), lifted.T, precision=HIGH)
        result = lifted - jnp.matmul(intersection.T, complex_occupied, precision=HIGH)
        image = jnp.stack([jnp.real(result), jnp.imag(result)]).astype(current.dtype)
        return (image, potential.astype(current.dtype))
    current = lanczos_now
    previous = lanczos_prev
    beta_value = beta_prev[0]
    rows_out = []
    potential = local_pot
    for iteration in range(STEPS):
        image, potential = operate(current)
        alpha_value = jnp.sum(current * image) / entries
        rest = image - alpha_value * current - beta_value * previous
        beta_new = jnp.sqrt(jnp.sum(rest * rest) / entries)
        previous = current
        current = rest / beta_new
        beta_value = beta_new
        rows_out.append(jnp.stack([alpha_value, beta_new]))
    return (current, jnp.stack(rows_out), potential)
```

```python
import math

import jax
import jax.numpy as jnp
import ml_dtypes
import numpy as np
from jax import lax
from jax.experimental import pallas as pl
from jax.experimental.pallas import tpu as pltpu
from jax.sharding import PartitionSpec as P

MESH = pl.DeviceIdType.MESH
F32 = jnp.float32
BF16 = jnp.bfloat16
KINETIC = 8.0
HARTREE = 4.0
N = 192
S = 64
G = 4
PL = 3
CELL = 9
HROWS = 4
QUART = N // G
HL = 512
TILE = 64
WAVES = 16384
PLACE = 2048
READ = 1024
BLOCK = 4096
STRIDE = 29
ENTRIES = float(2 * G * WAVES * S)


def split_np(table):
    high = table.astype(np.float32).astype(ml_dtypes.bfloat16)
    low = (table - high.astype(np.float64)).astype(np.float32).astype(ml_dtypes.bfloat16)
    return high, low


def left_table(table):
    high, low = split_np(table)
    return np.concatenate([high, high, low], axis=1)


def right_table(table):
    high, low = split_np(table)
    return np.concatenate([high, high, low], axis=0)


def make_tables():
    index = np.arange(N)
    angle = 2.0 * np.pi * (np.outer(index, index) % N) / N
    cosine = np.cos(angle) / math.sqrt(N)
    sine = np.sin(angle) / math.sqrt(N)
    order = np.concatenate([np.arange(S) * PL + part for part in range(PL)])
    re_lane = index // TILE * 128 + index % TILE
    im_lane = re_lane + TILE

    def lanes(sign):
        table = np.zeros((2 * N, 2 * N))
        table[np.ix_(re_lane, re_lane)] = cosine
        table[np.ix_(im_lane, re_lane)] = -sign * sine
        table[np.ix_(re_lane, im_lane)] = sign * sine
        table[np.ix_(im_lane, im_lane)] = cosine
        return table

    def rows(sign, row_order, column_order):
        both = [
            cosine[row_order][:, column_order],
            sign * sine[row_order][:, column_order],
        ]
        return left_table(np.concatenate(both, axis=1))

    cas = cosine + sine
    cas_in = np.zeros((2 * N, N))
    cas_in[re_lane] = cas
    cas_in[im_lane] = cas
    plus = lanes(1.0)
    return (
        np.stack([right_table(plus[t * 128 : (t + 1) * 128]) for t in range(3)]),
        right_table(lanes(-1.0)),
        rows(1.0, order, index),
        rows(1.0, index, order),
        rows(-1.0, order, index),
        rows(-1.0, index, order),
        right_table(cas_in),
        right_table(cas_in.T),
        left_table(cas[order]),
        left_table(cas[:, order]),
    )


def split(values):
    high = values.astype(BF16)
    low = (values - high.astype(F32)).astype(BF16)
    return high, low


def left(table_ref, values):
    high, low = split(values)
    stacked = jnp.concatenate([high, low, high], axis=0)
    return jnp.dot(table_ref[...], stacked, preferred_element_type=F32)


def right(values, table):
    high, low = split(values)
    stacked = jnp.concatenate([high, low, high], axis=1)
    return jnp.dot(stacked, table, preferred_element_type=F32)


def times_i(values):
    lane = lax.broadcasted_iota(jnp.int32, (values.shape[0], 128), 1)
    tiles = []
    for t in range(values.shape[1] // 128):
        turned = pltpu.roll(values[:, t * 128 : (t + 1) * 128], TILE, axis=1)
        tiles.append(jnp.where(lane < TILE, -turned, turned))
    return jnp.concatenate(tiles, axis=1)


def left_complex(table_ref, values):
    return left(table_ref, jnp.concatenate([values, times_i(values)], axis=0))


def signed(indices):
    return jnp.where(indices < N // 2, indices, indices - N)


def doubled(values):
    tiles = []
    for t in range(3):
        part = values[:, t * TILE : (t + 1) * TILE]
        tiles += [part, part]
    return jnp.concatenate(tiles, axis=1)


def body(*refs):
    now_ref, miller_ref, beta_ref, energy_ref = refs[:4]
    later = refs[4:19]
    rest_ref, scalars_ref, pot_ref = refs[19:22]
    held = refs[22:37]
    (
        prev_ref,
        orbit_ref,
        occ_ref,
        local_ref,
        xc_ref,
        lane_plus,
        lane_minus,
        a_plus,
        b_plus,
        b_minus,
        a_minus,
        cas_in,
        cas_out,
        cas_rows,
        cas_cols,
    ) = held
    (
        hot,
        acc,
        send1,
        recv1,
        fields,
        packed,
        w_send,
        w_recv,
        d_all,
        h_all,
        h_send1,
        h_recv1,
        h_send2,
        h_recv2,
        send2,
        recv2,
        table,
        lifted,
        over_send,
        over_recv,
        corr,
        corr_recv,
        sum_send1,
        sum_recv1,
        sum_send2,
        sum_recv2,
        sems,
        load_sems,
    ) = refs[37:]
    me = lax.axis_index("space")
    group = lax.axis_index("band")
    start = me * PL

    def load(at):
        return pltpu.make_async_copy(later[at], held[at], load_sems.at[at])

    for at in range(len(later)):
        load(at).start()

    barrier = pltpu.get_barrier_semaphore()

    def greet(step, carry):
        pl.semaphore_signal(
            barrier, inc=1, device_id={"space": lax.rem(me + step, S)}, device_id_type=MESH
        )
        return carry

    lax.fori_loop(1, S, greet, 0)
    for step in range(1, G):
        pl.semaphore_signal(
            barrier, inc=1, device_id={"band": lax.rem(group + step, G)}, device_id_type=MESH
        )

    def space_send(phase, source, target):
        def one(step, carry):
            peer = lax.rem(me + step * STRIDE, S)
            pltpu.make_async_remote_copy(
                src_ref=source(peer),
                dst_ref=target(me),
                send_sem=sems.at[phase, 0],
                recv_sem=sems.at[phase, 1],
                device_id={"space": peer},
                device_id_type=MESH,
            ).start()
            return carry

        lax.fori_loop(1, S, one, 0)

    def band_send(phase, source, target):
        for step in range(1, G):
            peer = lax.rem(group + step, G)
            pltpu.make_async_remote_copy(
                src_ref=source(peer),
                dst_ref=target(group),
                send_sem=sems.at[phase, 0],
                recv_sem=sems.at[phase, 1],
                device_id={"band": peer},
                device_id_type=MESH,
            ).start()

    def wait(phase, side, region):
        pltpu.make_async_copy(region, region, sems.at[phase, side]).wait()

    def part_chunk(ref, part):
        return lambda at: ref.at[pl.ds(part * S * CELL + at * CELL, CELL)]

    def chunk(ref):
        return lambda at: ref.at[pl.ds(at * HROWS, HROWS)]

    def keep(source, target, first, rows):
        own = pl.ds(first + me * rows, rows)
        target[own, :] = source[own, :]

    def cell_rows(part, m):
        return pl.ds(part * S * CELL + m, S, stride=CELL)

    def columns_at(step, size):
        return pl.ds(pl.multiple_of(step * size, size), size)

    def place(tile):
        def one(step, carry):
            columns = columns_at(step, PLACE)
            if tile == 0:
                row = (miller_ref[1:2, columns] - start) * N + miller_ref[0:1, columns]
                where = lax.broadcasted_iota(jnp.int16, (PL * N, PLACE), 0)
                hot[:, columns] = jnp.where(
                    where == row.astype(jnp.int16), BF16(1), BF16(0)
                )
            third = (miller_ref[2:3, columns] - tile * TILE).astype(jnp.int16)
            mask = lax.broadcasted_iota(jnp.int16, (TILE, PLACE), 0) == third
            parts = [jnp.where(mask, value, BF16(0)) for value in values_of(columns)]
            product = lax.dot_general(
                hot[:, columns],
                jnp.concatenate(parts, axis=0),
                (((1,), (1,)), ((), ())),
                preferred_element_type=F32,
            )
            acc[...] += product
            return carry

        acc[...] = jnp.zeros_like(acc)
        lax.fori_loop(0, WAVES // PLACE, one, 0)

    def values_of(columns):
        re_high, re_low = split(now_ref[0, 0:1, columns])
        im_high, im_low = split(now_ref[1, 0:1, columns])
        return re_high, im_high, re_low, im_low

    for t in range(3):
        place(t)
        placed = acc[:, 0:128] + acc[:, 128:256]
        if t == 0:
            load(7).wait()
        result = left_complex(
            a_plus, jnp.concatenate([placed[b * N : (b + 1) * N] for b in range(PL)], axis=1)
        )
        for r in range(PL):
            for b in range(PL):
                send1[cell_rows(t, r * PL + b), :] = result[
                    r * S : (r + 1) * S, b * 128 : (b + 1) * 128
                ]
        if t == 0:
            pl.semaphore_wait(barrier, S - 1 + G - 1)
        space_send(t, part_chunk(send1, t), part_chunk(recv1, t))
        keep(send1, recv1, t * S * CELL, CELL)

    for at in range(len(later)):
        if at != 7:
            load(at).wait()

    for r in range(PL):
        re = orbit_ref[0, 0, r]
        im = orbit_ref[1, 0, r]
        pieces = []
        for t in range(3):
            pieces += [re[:, t * TILE : (t + 1) * TILE], im[:, t * TILE : (t + 1) * TILE]]
        packed[r * N : (r + 1) * N] = jnp.concatenate(pieces, axis=1)

    every_chunk = pl.ds(0, (S - 1) * CELL)
    for t in range(3):
        wait(t, 1, recv1.at[every_chunk])
        values = jnp.concatenate(
            [
                jnp.concatenate([recv1[cell_rows(t, r * PL + b), :] for r in range(PL)], axis=1)
                for b in range(PL)
            ],
            axis=0,
        )
        result = left_complex(b_plus, values)
        result = jnp.concatenate([result[:, r * 128 : (r + 1) * 128] for r in range(PL)], axis=0)
        result = right(result, lane_plus[t])
        if t == 0:
            fields[...] = result
        else:
            fields[...] += result

    columns_of = right(2.0 * fields[...] * packed[...], cas_in[...])
    columns_of = [left(cas_rows, columns_of[r * N : (r + 1) * N]) for r in range(PL)]

    for g in range(G):
        pieces = []
        for r in range(PL):
            for b in range(PL):
                pieces.append(columns_of[r][b * S : (b + 1) * S, g * QUART : (g + 1) * QUART])
        pieces.append(jnp.zeros((S, HL - PL * PL * QUART), F32))
        w_send[g] = jnp.concatenate(pieces, axis=1)

    band_send(3, lambda peer: w_send.at[peer], lambda mine: w_recv.at[mine])
    w_recv[group] = w_send[group]
    wait(3, 1, w_recv.at[pl.ds(0, G - 1)])
    total = w_recv[0] + w_recv[1] + w_recv[2] + w_recv[3]
    d_all[group] = total
    for t in range(4):
        h_send1[pl.ds(t, S, stride=HROWS), :] = total[:, t * 128 : (t + 1) * 128]
    space_send(4, chunk(h_send1), chunk(h_recv1))
    band_send(5, lambda peer: d_all.at[group], lambda mine: d_all.at[mine])
    keep(h_send1, h_recv1, 0, HROWS)

    lane = lax.broadcasted_iota(jnp.int32, (N, PL * QUART), 1)
    first = signed(lax.broadcasted_iota(jnp.int32, (N, PL * QUART), 0))
    plane = jnp.where(lane >= QUART, 1, 0) + jnp.where(lane >= 2 * QUART, 1, 0)
    second = signed(plane + start)
    third = signed(lane - plane * QUART + group * QUART)
    squared = first * first + second * second + third * third
    coulomb = jnp.where(squared > 0, HARTREE / jnp.maximum(squared, 1).astype(F32), 0.0)

    wait(4, 1, h_recv1.at[pl.ds(0, (S - 1) * HROWS)])
    wide = jnp.concatenate([h_recv1[pl.ds(t, S, stride=HROWS), :] for t in range(4)], axis=1)
    tall = jnp.concatenate(
        [wide[:, r * PL * QUART : (r + 1) * PL * QUART] for r in range(PL)], axis=0
    )
    tall = left(cas_rows, coulomb * left(cas_cols, tall))
    wide = jnp.concatenate(
        [tall[r * S : (r + 1) * S] for r in range(PL)]
        + [jnp.zeros((S, HL - PL * PL * QUART), F32)],
        axis=1,
    )
    for t in range(4):
        h_send2[pl.ds(t, S, stride=HROWS), :] = wide[:, t * 128 : (t + 1) * 128]
    space_send(6, chunk(h_send2), chunk(h_recv2))
    keep(h_send2, h_recv2, 0, HROWS)

    def grid_values(ref):
        planes = []
        for r in range(PL):
            values = jnp.concatenate(
                [
                    jnp.concatenate(
                        [
                            ref[g][:, (r * PL + b) * QUART : (r * PL + b + 1) * QUART]
                            for g in range(G)
                        ],
                        axis=1,
                    )
                    for b in range(PL)
                ],
                axis=0,
            )
            planes.append(left(cas_cols, values))
        return right(jnp.concatenate(planes, axis=0), cas_out[...])

    wait(5, 0, d_all.at[pl.ds(0, G - 1)])
    wait(5, 1, d_all.at[pl.ds(0, G - 1)])
    xc_part = jnp.concatenate([doubled(xc_ref[r]) for r in range(PL)], axis=0)
    xc_part = xc_part * grid_values(d_all)
    acc[:, 0:128] = xc_part[:, 0:128]
    acc[:, 128:256] = xc_part[:, 128:256]
    acc_tail = xc_part[:, 256:384]

    wait(6, 1, h_recv2.at[pl.ds(0, (S - 1) * HROWS)])
    h_all[group] = jnp.concatenate(
        [h_recv2[pl.ds(t, S, stride=HROWS), :] for t in range(4)], axis=1
    )
    band_send(7, lambda peer: h_all.at[group], lambda mine: h_all.at[mine])
    wait(7, 0, h_all.at[pl.ds(0, G - 1)])
    wait(7, 1, h_all.at[pl.ds(0, G - 1)])

    potential = grid_values(h_all) + jnp.concatenate([acc[...], acc_tail], axis=1)
    local = jnp.concatenate([doubled(local_ref[r]) for r in range(PL)], axis=0)
    mixed = right(local * fields[...] + potential * packed[...], lane_minus[...])
    result = left_complex(
        b_minus, jnp.concatenate([mixed[r * N : (r + 1) * N] for r in range(PL)], axis=1)
    )
    for b in range(PL):
        for r in range(PL):
            for t in range(3):
                send2[cell_rows(b, r * PL + t), :] = result[
                    b * S : (b + 1) * S, (r * 3 + t) * 128 : (r * 3 + t + 1) * 128
                ]
        space_send(8 + b, part_chunk(send2, b), part_chunk(recv2, b))
        keep(send2, recv2, b * S * CELL, CELL)
    for r in range(PL):
        pot_ref[r] = jnp.concatenate(
            [potential[r * N : (r + 1) * N, t * 128 : t * 128 + TILE] for t in range(3)], axis=1
        )

    energy = energy_ref[0]

    def read_waves(b, columns):
        seen = hot[b * N : (b + 1) * N, columns]
        found = jnp.dot(
            table[...], jnp.concatenate([seen, seen], axis=0), preferred_element_type=F32
        )
        mask = lax.broadcasted_iota(jnp.int32, (N, READ), 0) == miller_ref[2:3, columns]
        sums = []
        for half in range(2):
            total = None
            for t in range(3):
                at = t * 128 + half * TILE
                kept = jnp.where(
                    mask[t * TILE : (t + 1) * TILE], found[at : at + TILE], 0.0
                )
                total = kept if total is None else total + kept
            sums.append(jnp.sum(total, axis=0, keepdims=True))
        if b > 0:
            sums = [sums[half] + lifted[group, half : half + 1, columns] for half in range(2)]
        if b == PL - 1:
            first = signed(miller_ref[0:1, columns])
            second = signed(miller_ref[1:2, columns])
            third = signed(miller_ref[2:3, columns])
            squared = first * first + second * second + third * third
            diagonal = KINETIC * squared.astype(F32) / float(N * N) - energy
            sums = [sums[half] + diagonal * now_ref[half, 0:1, columns] for half in range(2)]
        for half in range(2):
            lifted[group, half : half + 1, columns] = sums[half]

    blocks = WAVES // BLOCK
    per_block = BLOCK // READ

    def block(ref, at, n):
        return ref.at[at, :, pl.ds(n * BLOCK, BLOCK)]

    for b in range(PL):
        wait(8 + b, 1, recv2.at[every_chunk])
        values = jnp.concatenate(
            [
                jnp.concatenate([recv2[cell_rows(b, r * PL + t), :] for t in range(3)], axis=1)
                for r in range(PL)
            ],
            axis=0,
        )
        result = left_complex(a_minus, values)
        high = result.astype(BF16).astype(F32)
        table[...] = jnp.transpose(jnp.concatenate([high, result - high], axis=0)).astype(BF16)

        def one(step, carry):
            read_waves(b, columns_at(step, READ))
            return carry

        for n in range(blocks):
            lax.fori_loop(n * per_block, (n + 1) * per_block, one, 0)
            if b == PL - 1:
                band_send(
                    11 + n,
                    lambda peer: block(lifted, group, n),
                    lambda mine: block(lifted, mine, n),
                )

    def columns_of_tile(step):
        return pl.ds(pl.multiple_of(step * 128, 128), 128)

    def overlap(step, sums):
        columns = columns_of_tile(step)
        occ_re = occ_ref[0, :, columns]
        occ_im = occ_ref[1, :, columns]
        out = []
        for v in range(G):
            re = lifted[v, 0:1, columns]
            im = lifted[v, 1:2, columns]
            out.append(sums[2 * v] + (occ_re * re + occ_im * im))
            out.append(sums[2 * v + 1] + (occ_re * im - occ_im * re))
        return tuple(out)

    def three(ref, n):
        return ref.at[pl.ds(0, G - 1), :, pl.ds(n * BLOCK, BLOCK)]

    tiles = BLOCK // 128
    sums = tuple(jnp.zeros((16, 128), F32) for _ in range(2 * G))
    for n in range(blocks):
        wait(11 + n, 0, three(lifted, n))
        wait(11 + n, 1, three(lifted, n))
        sums = lax.fori_loop(n * tiles, (n + 1) * tiles, overlap, sums)
    lane = lax.broadcasted_iota(jnp.int32, (16, 128), 1)
    band_of = lane // 16
    own_row = (lane % 16) == lax.broadcasted_iota(jnp.int32, (16, 128), 0)
    matrix = jnp.zeros((16, 128), F32)
    for row in range(2 * G):
        column = jnp.sum(sums[row], axis=1, keepdims=True)
        matrix = jnp.where(band_of == row, column, matrix)
    over_send[0] = jnp.sum(jnp.where(own_row, matrix, 0.0), axis=0, keepdims=True)
    space_send(15, lambda peer: over_send.at[0], lambda mine: over_recv.at[mine])
    over_recv[me] = over_send[0]
    wait(15, 1, over_recv.at[pl.ds(0, S - 1)])
    row_sum = jnp.sum(over_recv[...], axis=0)
    spread = jnp.where(own_row, jnp.broadcast_to(row_sum, (16, 128)), 0.0)
    weights = []
    for row in range(2 * G):
        column = jnp.sum(jnp.where(band_of == row, spread, 0.0), axis=1, keepdims=True)
        weights.append(jnp.broadcast_to(column, (16, 128)))

    def correct(step, carry):
        columns = columns_of_tile(step)
        occ_re = occ_ref[0, :, columns]
        occ_im = occ_ref[1, :, columns]
        for v in range(G):
            w_re, w_im = weights[2 * v], weights[2 * v + 1]
            corr[v, 0:1, columns] = jnp.sum(occ_re * w_re - occ_im * w_im, axis=0, keepdims=True)
            corr[v, 1:2, columns] = jnp.sum(occ_re * w_im + occ_im * w_re, axis=0, keepdims=True)
        return carry

    for n in range(blocks):
        lax.fori_loop(n * tiles, (n + 1) * tiles, correct, 0)
        band_send(
            16 + n, lambda peer: block(corr, peer, n), lambda mine: block(corr_recv, mine, n)
        )

    corr_recv[group] = corr[group]
    beta_old = beta_ref[0]
    partial = [jnp.zeros((1, 1), F32) for _ in range(4)]
    for n in range(blocks):
        wait(16 + n, 1, three(corr_recv, n))
        columns = pl.ds(n * BLOCK, BLOCK)
        for part in range(2):
            removed = (
                corr_recv[0, part : part + 1, columns]
                + corr_recv[1, part : part + 1, columns]
                + corr_recv[2, part : part + 1, columns]
                + corr_recv[3, part : part + 1, columns]
            )
            q = now_ref[part, 0:1, columns]
            p = prev_ref[part, 0:1, columns]
            u = lifted[group, part : part + 1, columns] - removed - beta_old * p
            rest_ref[part, 0:1, columns] = u
            for slot, product in enumerate((u * u, q * u, q * p, q * q)):
                partial[slot] = partial[slot] + jnp.sum(product, axis=1, keepdims=True)
    lane = lax.broadcasted_iota(jnp.int32, (1, 128), 1)
    row = jnp.zeros((1, 128), F32)
    for slot in range(4):
        row = jnp.where(lane == slot, partial[slot], row)
    sum_send1[0] = row
    band_send(20, lambda peer: sum_send1.at[0], lambda mine: sum_recv1.at[mine])
    sum_recv1[group] = sum_send1[0]
    wait(20, 1, sum_recv1.at[pl.ds(0, G - 1)])
    sum_send2[0] = jnp.sum(sum_recv1[...], axis=0)
    space_send(21, lambda peer: sum_send2.at[0], lambda mine: sum_recv2.at[mine])
    sum_recv2[me] = sum_send2[0]

    for part in range(3):
        wait(part, 0, send1.at[every_chunk])
        wait(8 + part, 0, send2.at[every_chunk])
    wait(3, 0, w_send.at[pl.ds(0, G - 1)])
    wait(4, 0, h_send1.at[pl.ds(0, (S - 1) * HROWS)])
    wait(6, 0, h_send2.at[pl.ds(0, (S - 1) * HROWS)])
    wait(15, 0, over_recv.at[pl.ds(0, S - 1)])
    for n in range(blocks):
        wait(16 + n, 0, three(corr, n))
    wait(20, 0, sum_recv1.at[pl.ds(0, G - 1)])

    wait(21, 0, sum_recv2.at[pl.ds(0, S - 1)])
    wait(21, 1, sum_recv2.at[pl.ds(0, S - 1)])
    row = jnp.sum(sum_recv2[...], axis=0)

    def pick(slot):
        return jnp.sum(jnp.where(lane == slot, row, 0.0), axis=1, keepdims=True)

    norm_u, q_u, q_p, norm_q = [pick(slot) for slot in range(4)]
    alpha = (q_u + beta_old * q_p) / ENTRIES
    square = norm_u - 2.0 * alpha * q_u + alpha * alpha * norm_q
    beta_new = jnp.sqrt(square / ENTRIES)
    scalars_ref[...] = jnp.where(lane == 0, alpha, beta_new)


def finish(rest_ref, now_ref, scalars_ref, pot_in, next_ref, coef_ref, pot_ref):
    alpha = scalars_ref[0:1, 0:1]
    beta_new = scalars_ref[0:1, 1:2]
    inverse = 1.0 / beta_new
    for part in range(2):
        next_ref[part] = (rest_ref[part] - alpha * now_ref[part]) * inverse
    coef_ref[...] = scalars_ref[0:1, 0:2]
    pot_ref[...] = pot_in[...]


def per_device(
    lanczos_now,
    lanczos_prev,
    beta_prev,
    orbitals,
    band_energy,
    occupied,
    local_pot,
    xc_kernel,
    miller,
):
    later = [lanczos_prev, orbitals, occupied, local_pot, xc_kernel]
    later += [jnp.asarray(table) for table in make_tables()]
    vmem = pl.BlockSpec(memory_space=pltpu.VMEM)
    smem = pl.BlockSpec(memory_space=pltpu.SMEM)
    anywhere = pl.BlockSpec(memory_space=pl.ANY)
    wide = pltpu.VMEM((3 * S * CELL, 128), F32)
    narrow = pltpu.VMEM((S * HROWS, 128), F32)
    quarter = pltpu.VMEM((G, S, HL), F32)
    band_waves = pltpu.VMEM((G, 2, WAVES), F32)
    real_grid = jax.ShapeDtypeStruct((PL, N, N), F32)
    waves = jax.ShapeDtypeStruct((2, 1, WAVES), F32)
    rest, scalars, potential = pl.pallas_call(
        body,
        out_shape=(waves, jax.ShapeDtypeStruct((1, 128), F32), real_grid),
        in_specs=[vmem, vmem, smem, smem] + [anywhere] * len(later),
        out_specs=(vmem, vmem, vmem),
        scratch_shapes=[pltpu.VMEM(array.shape, array.dtype) for array in later]
        + [
            pltpu.VMEM((PL * N, WAVES), BF16),
            pltpu.VMEM((PL * N, 256), F32),
            wide,
            wide,
            pltpu.VMEM((PL * N, 384), F32),
            pltpu.VMEM((PL * N, 384), F32),
            quarter,
            quarter,
            quarter,
            quarter,
            narrow,
            narrow,
            narrow,
            narrow,
            wide,
            wide,
            pltpu.VMEM((384, 2 * N), BF16),
            band_waves,
            pltpu.VMEM((1, 1, 128), F32),
            pltpu.VMEM((S, 1, 128), F32),
            band_waves,
            band_waves,
            pltpu.VMEM((1, 1, 128), F32),
            pltpu.VMEM((G, 1, 128), F32),
            pltpu.VMEM((1, 1, 128), F32),
            pltpu.VMEM((S, 1, 128), F32),
            pltpu.SemaphoreType.DMA((22, 2)),
            pltpu.SemaphoreType.DMA((len(later),)),
        ],
        compiler_params=pltpu.CompilerParams(
            collective_id=0, has_side_effects=True, vmem_limit_bytes=60 * 1024 * 1024
        ),
    )(lanczos_now, miller, beta_prev, band_energy, *later)
    return pl.pallas_call(
        finish,
        out_shape=(waves, jax.ShapeDtypeStruct((1, 2), F32), real_grid),
        in_specs=[vmem] * 4,
        out_specs=(vmem,) * 3,
    )(rest, lanczos_now, scalars, potential)


def solution(mesh):
    return jax.shard_map(
        per_device,
        mesh=mesh,
        in_specs=(
            P(None, "band", "space"),
            P(None, "band", "space"),
            P(),
            P(None, "band", "space", None, None),
            P("band"),
            P(None, "band", "space"),
            P("space", None, None),
            P("space", None, None),
            P(None, "space"),
        ),
        out_specs=(P(None, "band", "space"), P(), P("space", None, None)),
        check_vma=False,
    )
```

```python
import math

import jax
import jax.numpy as jnp
import ml_dtypes
import numpy as np
from jax import lax
from jax.experimental import pallas as pl
from jax.experimental.pallas import tpu as pltpu
from jax.sharding import PartitionSpec as P

MESH = pl.DeviceIdType.MESH
F32 = jnp.float32
BF16 = jnp.bfloat16
KINETIC = 8.0
HARTREE = 4.0
N = 192
S = 64
G = 4
PL = 3
CELL = 9
HROWS = 4
QUART = N // G
HL = 512
TILE = 64
WAVES = 16384
PLACE = 2048
READ = 1024
BLOCK = 4096
STRIDE = 29
ENTRIES = float(2 * G * WAVES * S)


def split_np(table):
    high = table.astype(np.float32).astype(ml_dtypes.bfloat16)
    low = (table - high.astype(np.float64)).astype(np.float32).astype(ml_dtypes.bfloat16)
    return high, low


def left_table(table):
    high, low = split_np(table)
    return np.concatenate([high, high, low], axis=1)


def right_table(table):
    high, low = split_np(table)
    return np.concatenate([high, high, low], axis=0)


def make_tables():
    index = np.arange(N)
    angle = 2.0 * np.pi * (np.outer(index, index) % N) / N
    cosine = np.cos(angle) / math.sqrt(N)
    sine = np.sin(angle) / math.sqrt(N)
    order = np.concatenate([np.arange(S) * PL + part for part in range(PL)])
    re_lane = index // TILE * 128 + index % TILE
    im_lane = re_lane + TILE

    def lanes(sign):
        table = np.zeros((2 * N, 2 * N))
        table[np.ix_(re_lane, re_lane)] = cosine
        table[np.ix_(im_lane, re_lane)] = -sign * sine
        table[np.ix_(re_lane, im_lane)] = sign * sine
        table[np.ix_(im_lane, im_lane)] = cosine
        return table

    def rows(sign, row_order, column_order):
        both = [
            cosine[row_order][:, column_order],
            sign * sine[row_order][:, column_order],
        ]
        return left_table(np.concatenate(both, axis=1))

    cas = cosine + sine
    cas_in = np.zeros((2 * N, N))
    cas_in[re_lane] = cas
    cas_in[im_lane] = cas
    plus = lanes(1.0)
    return (
        np.stack([right_table(plus[t * 128 : (t + 1) * 128]) for t in range(3)]),
        right_table(lanes(-1.0)),
        rows(1.0, order, index),
        rows(1.0, index, order),
        rows(-1.0, order, index),
        rows(-1.0, index, order),
        right_table(cas_in),
        right_table(cas_in.T),
        left_table(cas[order]),
        left_table(cas[:, order]),
    )


def split(values):
    high = values.astype(BF16)
    low = (values - high.astype(F32)).astype(BF16)
    return high, low


def left(table_ref, values):
    high, low = split(values)
    stacked = jnp.concatenate([high, low, high], axis=0)
    return jnp.dot(table_ref[...], stacked, preferred_element_type=F32)


def right(values, table):
    high, low = split(values)
    stacked = jnp.concatenate([high, low, high], axis=1)
    return jnp.dot(stacked, table, preferred_element_type=F32)


def times_i(values):
    lane = lax.broadcasted_iota(jnp.int32, (values.shape[0], 128), 1)
    tiles = []
    for t in range(values.shape[1] // 128):
        turned = pltpu.roll(values[:, t * 128 : (t + 1) * 128], TILE, axis=1)
        tiles.append(jnp.where(lane < TILE, -turned, turned))
    return jnp.concatenate(tiles, axis=1)


def left_complex(table_ref, values):
    return left(table_ref, jnp.concatenate([values, times_i(values)], axis=0))


def signed(indices):
    return jnp.where(indices < N // 2, indices, indices - N)


def doubled(values):
    tiles = []
    for t in range(3):
        part = values[:, t * TILE : (t + 1) * TILE]
        tiles += [part, part]
    return jnp.concatenate(tiles, axis=1)


def body(*refs):
    now_ref, miller_ref = refs[:2]
    later = refs[2:19]
    rest_ref, scalars_ref, pot_ref = refs[19:22]
    held = refs[22:39]
    (
        prev_ref,
        orbit_ref,
        occ_ref,
        local_ref,
        xc_ref,
        lane_plus,
        lane_minus,
        a_plus,
        b_plus,
        b_minus,
        a_minus,
        cas_in,
        cas_out,
        cas_rows,
        cas_cols,
        beta_ref,
        energy_ref,
    ) = held
    (
        hot,
        acc,
        send1,
        recv1,
        fields,
        packed,
        xc_part,
        w_send,
        w_recv,
        d_all,
        h_all,
        h_send1,
        h_recv1,
        h_send2,
        h_recv2,
        send2,
        recv2,
        table,
        lifted,
        over_send,
        over_recv,
        corr,
        corr_recv,
        sum_send1,
        sum_recv1,
        sum_send2,
        sum_recv2,
        sems,
        load_sems,
    ) = refs[39:]
    me = lax.axis_index("space")
    group = lax.axis_index("band")
    start = me * PL

    def load(at):
        return pltpu.make_async_copy(later[at], held[at], load_sems.at[at])

    for at in range(len(later)):
        load(at).start()

    barrier = pltpu.get_barrier_semaphore()

    def greet(turn, carry):
        for step in range(7):
            peer = lax.rem(me + (turn * 7 + step + 1) * STRIDE, S)
            pl.semaphore_signal(barrier, inc=1, device_id={"space": peer}, device_id_type=MESH)
        return carry

    lax.fori_loop(0, (S - 1) // 7, greet, 0)
    for step in range(1, G):
        pl.semaphore_signal(
            barrier, inc=1, device_id={"band": lax.rem(group + step, G)}, device_id_type=MESH
        )

    def space_send(phase, source, target):
        def one(turn, carry):
            for step in range(7):
                peer = lax.rem(me + (turn * 7 + step + 1) * STRIDE, S)
                pltpu.make_async_remote_copy(
                    src_ref=source(peer),
                    dst_ref=target(me),
                    send_sem=sems.at[phase, 0],
                    recv_sem=sems.at[phase, 1],
                    device_id={"space": peer},
                    device_id_type=MESH,
                ).start()
            return carry

        lax.fori_loop(0, (S - 1) // 7, one, 0)

    def band_send(phase, source, target):
        for step in (2, 1, 3):
            peer = lax.rem(group + step, G)
            pltpu.make_async_remote_copy(
                src_ref=source(peer),
                dst_ref=target(group),
                send_sem=sems.at[phase, 0],
                recv_sem=sems.at[phase, 1],
                device_id={"band": peer},
                device_id_type=MESH,
            ).start()

    def wait(phase, side, region):
        pltpu.make_async_copy(region, region, sems.at[phase, side]).wait()

    def part_chunk(ref, part):
        return lambda at: ref.at[pl.ds(part * S * CELL + at * CELL, CELL)]

    def chunk(ref):
        return lambda at: ref.at[pl.ds(at * HROWS, HROWS)]

    def keep(source, target, first, rows):
        own = pl.ds(first + me * rows, rows)
        target[own, :] = source[own, :]

    def cell_rows(part, m):
        return pl.ds(part * S * CELL + m, S, stride=CELL)

    def columns_at(step, size):
        return pl.ds(pl.multiple_of(step * size, size), size)

    def place(tile):
        def one(step, carry):
            columns = columns_at(step, PLACE)
            if tile == 0:
                row = (miller_ref[1:2, columns] - start) * N + miller_ref[0:1, columns]
                where = lax.broadcasted_iota(jnp.int16, (PL * N, PLACE), 0)
                hot[:, columns] = jnp.where(
                    where == row.astype(jnp.int16), BF16(1), BF16(0)
                )
            third = (miller_ref[2:3, columns] - tile * TILE).astype(jnp.int16)
            mask = lax.broadcasted_iota(jnp.int16, (TILE, PLACE), 0) == third
            parts = [jnp.where(mask, value, BF16(0)) for value in values_of(columns)]
            product = lax.dot_general(
                hot[:, columns],
                jnp.concatenate(parts, axis=0),
                (((1,), (1,)), ((), ())),
                preferred_element_type=F32,
            )
            acc[...] += product
            return carry

        acc[...] = jnp.zeros_like(acc)
        lax.fori_loop(0, WAVES // PLACE, one, 0, unroll=2)

    def values_of(columns):
        re_high, re_low = split(now_ref[0, 0:1, columns])
        im_high, im_low = split(now_ref[1, 0:1, columns])
        return re_high, im_high, re_low, im_low

    for t in range(3):
        place(t)
        placed = acc[:, 0:128] + acc[:, 128:256]
        if t == 0:
            load(7).wait()
        result = left_complex(
            a_plus, jnp.concatenate([placed[b * N : (b + 1) * N] for b in range(PL)], axis=1)
        )
        for r in range(PL):
            for b in range(PL):
                send1[cell_rows(t, r * PL + b), :] = result[
                    r * S : (r + 1) * S, b * 128 : (b + 1) * 128
                ]
        if t == 0:
            pl.semaphore_wait(barrier, S - 1 + G - 1)
        space_send(t, part_chunk(send1, t), part_chunk(recv1, t))
        keep(send1, recv1, t * S * CELL, CELL)

    for at in range(len(later)):
        if at != 7:
            load(at).wait()

    for r in range(PL):
        re = orbit_ref[0, 0, r]
        im = orbit_ref[1, 0, r]
        pieces = []
        for t in range(3):
            pieces += [re[:, t * TILE : (t + 1) * TILE], im[:, t * TILE : (t + 1) * TILE]]
        packed[r * N : (r + 1) * N] = jnp.concatenate(pieces, axis=1)

    every_chunk = pl.ds(0, (S - 1) * CELL)
    for t in range(3):
        wait(t, 1, recv1.at[every_chunk])
        values = jnp.concatenate(
            [
                jnp.concatenate([recv1[cell_rows(t, r * PL + b), :] for r in range(PL)], axis=1)
                for b in range(PL)
            ],
            axis=0,
        )
        result = left_complex(b_plus, values)
        result = jnp.concatenate([result[:, r * 128 : (r + 1) * 128] for r in range(PL)], axis=0)
        result = right(result, lane_plus[t])
        if t == 0:
            fields[...] = result
        else:
            fields[...] += result

    columns_of = right(2.0 * fields[...] * packed[...], cas_in[...])
    columns_of = [left(cas_rows, columns_of[r * N : (r + 1) * N]) for r in range(PL)]

    for g in range(G):
        pieces = []
        for r in range(PL):
            for b in range(PL):
                pieces.append(columns_of[r][b * S : (b + 1) * S, g * QUART : (g + 1) * QUART])
        pieces.append(jnp.zeros((S, HL - PL * PL * QUART), F32))
        w_send[g] = jnp.concatenate(pieces, axis=1)

    band_send(3, lambda peer: w_send.at[peer], lambda mine: w_recv.at[mine])
    w_recv[group] = w_send[group]
    wait(3, 1, w_recv.at[pl.ds(0, G - 1)])
    total = w_recv[0] + w_recv[1] + w_recv[2] + w_recv[3]
    d_all[group] = total
    for t in range(4):
        h_send1[pl.ds(t, S, stride=HROWS), :] = total[:, t * 128 : (t + 1) * 128]
    space_send(4, chunk(h_send1), chunk(h_recv1))
    band_send(5, lambda peer: d_all.at[group], lambda mine: d_all.at[mine])
    keep(h_send1, h_recv1, 0, HROWS)

    lane = lax.broadcasted_iota(jnp.int32, (N, PL * QUART), 1)
    first = signed(lax.broadcasted_iota(jnp.int32, (N, PL * QUART), 0))
    plane = jnp.where(lane >= QUART, 1, 0) + jnp.where(lane >= 2 * QUART, 1, 0)
    second = signed(plane + start)
    third = signed(lane - plane * QUART + group * QUART)
    squared = first * first + second * second + third * third
    coulomb = jnp.where(squared > 0, HARTREE / jnp.maximum(squared, 1).astype(F32), 0.0)

    wait(4, 1, h_recv1.at[pl.ds(0, (S - 1) * HROWS)])
    wide = jnp.concatenate([h_recv1[pl.ds(t, S, stride=HROWS), :] for t in range(4)], axis=1)
    tall = jnp.concatenate(
        [wide[:, r * PL * QUART : (r + 1) * PL * QUART] for r in range(PL)], axis=0
    )
    tall = left(cas_rows, coulomb * left(cas_cols, tall))
    wide = jnp.concatenate(
        [tall[r * S : (r + 1) * S] for r in range(PL)]
        + [jnp.zeros((S, HL - PL * PL * QUART), F32)],
        axis=1,
    )
    for t in range(4):
        h_send2[pl.ds(t, S, stride=HROWS), :] = wide[:, t * 128 : (t + 1) * 128]
    space_send(6, chunk(h_send2), chunk(h_recv2))
    keep(h_send2, h_recv2, 0, HROWS)

    def grid_values(ref):
        planes = []
        for r in range(PL):
            values = jnp.concatenate(
                [
                    jnp.concatenate(
                        [
                            ref[g][:, (r * PL + b) * QUART : (r * PL + b + 1) * QUART]
                            for g in range(G)
                        ],
                        axis=1,
                    )
                    for b in range(PL)
                ],
                axis=0,
            )
            planes.append(left(cas_cols, values))
        return right(jnp.concatenate(planes, axis=0), cas_out[...])

    wait(5, 0, d_all.at[pl.ds(0, G - 1)])
    wait(5, 1, d_all.at[pl.ds(0, G - 1)])
    known = grid_values(d_all) * jnp.concatenate([doubled(xc_ref[r]) for r in range(PL)], axis=0)
    local = jnp.concatenate([doubled(local_ref[r]) for r in range(PL)], axis=0)
    fields[...] = local * fields[...] + known * packed[...]
    xc_part[...] = known

    wait(6, 1, h_recv2.at[pl.ds(0, (S - 1) * HROWS)])
    h_all[group] = jnp.concatenate(
        [h_recv2[pl.ds(t, S, stride=HROWS), :] for t in range(4)], axis=1
    )
    band_send(7, lambda peer: h_all.at[group], lambda mine: h_all.at[mine])
    wait(7, 0, h_all.at[pl.ds(0, G - 1)])
    wait(7, 1, h_all.at[pl.ds(0, G - 1)])

    hartree = grid_values(h_all)
    mixed = right(fields[...] + hartree * packed[...], lane_minus[...])
    result = left_complex(
        b_minus, jnp.concatenate([mixed[r * N : (r + 1) * N] for r in range(PL)], axis=1)
    )
    for b in range(PL):
        for r in range(PL):
            for t in range(3):
                send2[cell_rows(b, r * PL + t), :] = result[
                    b * S : (b + 1) * S, (r * 3 + t) * 128 : (r * 3 + t + 1) * 128
                ]
        space_send(8 + b, part_chunk(send2, b), part_chunk(recv2, b))
        keep(send2, recv2, b * S * CELL, CELL)
    potential = hartree + xc_part[...]
    for r in range(PL):
        pot_ref[r] = jnp.concatenate(
            [potential[r * N : (r + 1) * N, t * 128 : t * 128 + TILE] for t in range(3)], axis=1
        )

    energy = energy_ref[0:1].reshape(1, 1)

    def read_waves(b, columns):
        seen = hot[b * N : (b + 1) * N, columns]
        found = jnp.dot(
            table[...], jnp.concatenate([seen, seen], axis=0), preferred_element_type=F32
        )
        mask = lax.broadcasted_iota(jnp.int32, (N, READ), 0) == miller_ref[2:3, columns]
        sums = []
        for half in range(2):
            total = None
            for t in range(3):
                at = t * 128 + half * TILE
                kept = jnp.where(
                    mask[t * TILE : (t + 1) * TILE], found[at : at + TILE], 0.0
                )
                total = kept if total is None else total + kept
            sums.append(jnp.sum(total, axis=0, keepdims=True))
        if b > 0:
            sums = [sums[half] + lifted[group, half : half + 1, columns] for half in range(2)]
        if b == PL - 1:
            first = signed(miller_ref[0:1, columns])
            second = signed(miller_ref[1:2, columns])
            third = signed(miller_ref[2:3, columns])
            squared = first * first + second * second + third * third
            diagonal = KINETIC * squared.astype(F32) / float(N * N) - energy
            sums = [sums[half] + diagonal * now_ref[half, 0:1, columns] for half in range(2)]
        for half in range(2):
            lifted[group, half : half + 1, columns] = sums[half]

    blocks = WAVES // BLOCK
    per_block = BLOCK // READ

    def block(ref, at, n):
        return ref.at[at, :, pl.ds(n * BLOCK, BLOCK)]

    for b in range(PL):
        wait(8 + b, 1, recv2.at[every_chunk])
        values = jnp.concatenate(
            [
                jnp.concatenate([recv2[cell_rows(b, r * PL + t), :] for t in range(3)], axis=1)
                for r in range(PL)
            ],
            axis=0,
        )
        result = left_complex(a_minus, values)
        high = result.astype(BF16).astype(F32)
        table[...] = jnp.transpose(jnp.concatenate([high, result - high], axis=0)).astype(BF16)

        def one(step, carry):
            read_waves(b, columns_at(step, READ))
            return carry

        for n in range(blocks):
            lax.fori_loop(n * per_block, (n + 1) * per_block, one, 0, unroll=2)
            if b == PL - 1:
                band_send(
                    11 + n,
                    lambda peer: block(lifted, group, n),
                    lambda mine: block(lifted, mine, n),
                )

    def columns_of_tile(step):
        return pl.ds(pl.multiple_of(step * 128, 128), 128)

    def overlap(step, sums):
        columns = columns_of_tile(step)
        occ_re = occ_ref[0, :, columns]
        occ_im = occ_ref[1, :, columns]
        out = []
        for v in range(G):
            re = lifted[v, 0:1, columns]
            im = lifted[v, 1:2, columns]
            out.append(sums[2 * v] + (occ_re * re + occ_im * im))
            out.append(sums[2 * v + 1] + (occ_re * im - occ_im * re))
        return tuple(out)

    def three(ref, n):
        return ref.at[pl.ds(0, G - 1), :, pl.ds(n * BLOCK, BLOCK)]

    tiles = BLOCK // 128
    sums = tuple(jnp.zeros((16, 128), F32) for _ in range(2 * G))
    for n in range(blocks):
        wait(11 + n, 0, three(lifted, n))
        wait(11 + n, 1, three(lifted, n))
        sums = lax.fori_loop(n * tiles, (n + 1) * tiles, overlap, sums, unroll=4)
    lane = lax.broadcasted_iota(jnp.int32, (16, 128), 1)
    band_of = lane // 16
    own_row = (lane % 16) == lax.broadcasted_iota(jnp.int32, (16, 128), 0)
    matrix = jnp.zeros((16, 128), F32)
    for row in range(2 * G):
        column = jnp.sum(sums[row], axis=1, keepdims=True)
        matrix = jnp.where(band_of == row, column, matrix)
    over_send[0] = jnp.sum(jnp.where(own_row, matrix, 0.0), axis=0, keepdims=True)
    space_send(15, lambda peer: over_send.at[0], lambda mine: over_recv.at[mine])
    over_recv[me] = over_send[0]
    wait(15, 1, over_recv.at[pl.ds(0, S - 1)])
    row_sum = jnp.sum(over_recv[...], axis=0)
    spread = jnp.where(own_row, jnp.broadcast_to(row_sum, (16, 128)), 0.0)
    weights = []
    for row in range(2 * G):
        column = jnp.sum(jnp.where(band_of == row, spread, 0.0), axis=1, keepdims=True)
        weights.append(jnp.broadcast_to(column, (16, 128)))

    def correct(step, carry):
        columns = columns_of_tile(step)
        occ_re = occ_ref[0, :, columns]
        occ_im = occ_ref[1, :, columns]
        for v in range(G):
            w_re, w_im = weights[2 * v], weights[2 * v + 1]
            corr[v, 0:1, columns] = jnp.sum(occ_re * w_re - occ_im * w_im, axis=0, keepdims=True)
            corr[v, 1:2, columns] = jnp.sum(occ_re * w_im + occ_im * w_re, axis=0, keepdims=True)
        return carry

    for n in range(blocks):
        lax.fori_loop(n * tiles, (n + 1) * tiles, correct, 0, unroll=4)
        band_send(
            16 + n, lambda peer: block(corr, peer, n), lambda mine: block(corr_recv, mine, n)
        )

    corr_recv[group] = corr[group]
    beta_old = beta_ref[0:1].reshape(1, 1)
    partial = [jnp.zeros((1, 1), F32) for _ in range(4)]
    for n in range(blocks):
        wait(16 + n, 1, three(corr_recv, n))
        columns = pl.ds(n * BLOCK, BLOCK)
        for part in range(2):
            removed = (
                corr_recv[0, part : part + 1, columns]
                + corr_recv[1, part : part + 1, columns]
                + corr_recv[2, part : part + 1, columns]
                + corr_recv[3, part : part + 1, columns]
            )
            q = now_ref[part, 0:1, columns]
            p = prev_ref[part, 0:1, columns]
            u = lifted[group, part : part + 1, columns] - removed - beta_old * p
            rest_ref[part, 0:1, columns] = u
            for slot, product in enumerate((u * u, q * u, q * p, q * q)):
                partial[slot] = partial[slot] + jnp.sum(product, axis=1, keepdims=True)
    lane = lax.broadcasted_iota(jnp.int32, (1, 128), 1)
    row = jnp.zeros((1, 128), F32)
    for slot in range(4):
        row = jnp.where(lane == slot, partial[slot], row)
    sum_send1[0] = row
    band_send(20, lambda peer: sum_send1.at[0], lambda mine: sum_recv1.at[mine])
    sum_recv1[group] = sum_send1[0]
    wait(20, 1, sum_recv1.at[pl.ds(0, G - 1)])
    sum_send2[0] = jnp.sum(sum_recv1[...], axis=0)
    space_send(21, lambda peer: sum_send2.at[0], lambda mine: sum_recv2.at[mine])
    sum_recv2[me] = sum_send2[0]

    for part in range(3):
        wait(part, 0, send1.at[every_chunk])
        wait(8 + part, 0, send2.at[every_chunk])
    wait(3, 0, w_send.at[pl.ds(0, G - 1)])
    wait(4, 0, h_send1.at[pl.ds(0, (S - 1) * HROWS)])
    wait(6, 0, h_send2.at[pl.ds(0, (S - 1) * HROWS)])
    wait(15, 0, over_recv.at[pl.ds(0, S - 1)])
    for n in range(blocks):
        wait(16 + n, 0, three(corr, n))
    wait(20, 0, sum_recv1.at[pl.ds(0, G - 1)])

    wait(21, 0, sum_recv2.at[pl.ds(0, S - 1)])
    wait(21, 1, sum_recv2.at[pl.ds(0, S - 1)])
    row = jnp.sum(sum_recv2[...], axis=0)

    def pick(slot):
        return jnp.sum(jnp.where(lane == slot, row, 0.0), axis=1, keepdims=True)

    norm_u, q_u, q_p, norm_q = [pick(slot) for slot in range(4)]
    alpha = (q_u + beta_old * q_p) / ENTRIES
    square = norm_u - 2.0 * alpha * q_u + alpha * alpha * norm_q
    beta_new = jnp.sqrt(square / ENTRIES)
    scalars_ref[...] = jnp.where(lane == 0, alpha, beta_new)


def finish(rest_ref, now_ref, scalars_ref, pot_in, next_ref, coef_ref, pot_ref, sem):
    through = pltpu.make_async_copy(pot_in, pot_ref, sem)
    through.start()
    alpha = scalars_ref[0:1, 0:1]
    beta_new = scalars_ref[0:1, 1:2]
    inverse = 1.0 / beta_new
    for part in range(2):
        next_ref[part] = (rest_ref[part] - alpha * now_ref[part]) * inverse
    coef_ref[...] = scalars_ref[0:1, 0:2]
    through.wait()


def per_device(
    lanczos_now,
    lanczos_prev,
    beta_prev,
    orbitals,
    band_energy,
    occupied,
    local_pot,
    xc_kernel,
    miller,
):
    later = [lanczos_prev, orbitals, occupied, local_pot, xc_kernel]
    later += [jnp.asarray(table) for table in make_tables()]
    later += [beta_prev, band_energy]
    vmem = pl.BlockSpec(memory_space=pltpu.VMEM)
    in_hbm = pl.BlockSpec(memory_space=pltpu.HBM)
    wide = pltpu.VMEM((3 * S * CELL, 128), F32)
    narrow = pltpu.VMEM((S * HROWS, 128), F32)
    quarter = pltpu.VMEM((G, S, HL), F32)
    band_waves = pltpu.VMEM((G, 2, WAVES), F32)
    real_grid = jax.ShapeDtypeStruct((PL, N, N), F32)
    waves = jax.ShapeDtypeStruct((2, 1, WAVES), F32)
    rest, scalars, potential = pl.pallas_call(
        body,
        out_shape=(waves, jax.ShapeDtypeStruct((1, 128), F32), real_grid),
        in_specs=[vmem, vmem] + [in_hbm] * len(later),
        out_specs=(vmem, vmem, vmem),
        scratch_shapes=[pltpu.VMEM(array.shape, array.dtype) for array in later]
        + [
            pltpu.VMEM((PL * N, WAVES), BF16),
            pltpu.VMEM((PL * N, 256), F32),
            wide,
            wide,
            pltpu.VMEM((PL * N, 384), F32),
            pltpu.VMEM((PL * N, 384), F32),
            pltpu.VMEM((PL * N, 384), F32),
            quarter,
            quarter,
            quarter,
            quarter,
            narrow,
            narrow,
            narrow,
            narrow,
            wide,
            wide,
            pltpu.VMEM((384, 2 * N), BF16),
            band_waves,
            pltpu.VMEM((1, 1, 128), F32),
            pltpu.VMEM((S, 1, 128), F32),
            band_waves,
            band_waves,
            pltpu.VMEM((1, 1, 128), F32),
            pltpu.VMEM((G, 1, 128), F32),
            pltpu.VMEM((1, 1, 128), F32),
            pltpu.VMEM((S, 1, 128), F32),
            pltpu.SemaphoreType.DMA((22, 2)),
            pltpu.SemaphoreType.DMA((len(later),)),
        ],
        compiler_params=pltpu.CompilerParams(
            collective_id=0, has_side_effects=True, vmem_limit_bytes=60 * 1024 * 1024
        ),
    )(lanczos_now, miller, *later)
    return pl.pallas_call(
        finish,
        out_shape=(waves, jax.ShapeDtypeStruct((1, 2), F32), real_grid),
        in_specs=[vmem, vmem, vmem, in_hbm],
        out_specs=(vmem, vmem, in_hbm),
        scratch_shapes=[pltpu.SemaphoreType.DMA],
    )(rest, lanczos_now, scalars, potential)


def solution(mesh):
    return jax.shard_map(
        per_device,
        mesh=mesh,
        in_specs=(
            P(None, "band", "space"),
            P(None, "band", "space"),
            P(),
            P(None, "band", "space", None, None),
            P("band"),
            P(None, "band", "space"),
            P("space", None, None),
            P("space", None, None),
            P(None, "space"),
        ),
        out_specs=(P(None, "band", "space"), P(), P("space", None, None)),
        check_vma=False,
    )
```

```python
import math

import jax
import jax.numpy as jnp
import ml_dtypes
import numpy as np
from jax import lax
from jax.experimental import pallas as pl
from jax.experimental.pallas import tpu as pltpu
from jax.sharding import PartitionSpec as P

MESH = pl.DeviceIdType.MESH
F32 = jnp.float32
BF16 = jnp.bfloat16
KINETIC = 8.0
HARTREE = 4.0
N = 192
S = 64
G = 4
PL = 3
CELL = 9
HROWS = 4
QUART = N // G
HL = 512
TILE = 64
WAVES = 16384
PLACE = 2048
READ = 1024
BLOCK = 4096
STRIDE = 29
ENTRIES = float(2 * G * WAVES * S)


def split_np(table):
    high = table.astype(np.float32).astype(ml_dtypes.bfloat16)
    low = (table - high.astype(np.float64)).astype(np.float32).astype(ml_dtypes.bfloat16)
    return high, low


def left_table(table):
    high, low = split_np(table)
    return np.concatenate([high, low], axis=0)


def right_table(table):
    high, low = split_np(table)
    return np.concatenate([high, high, low], axis=0)


def make_tables():
    index = np.arange(N)
    angle = 2.0 * np.pi * (np.outer(index, index) % N) / N
    cosine = np.cos(angle) / math.sqrt(N)
    sine = np.sin(angle) / math.sqrt(N)
    order = np.concatenate([np.arange(S) * PL + part for part in range(PL)])
    re_lane = index // TILE * 128 + index % TILE
    im_lane = re_lane + TILE

    def lanes(sign):
        table = np.zeros((2 * N, 2 * N))
        table[np.ix_(re_lane, re_lane)] = cosine
        table[np.ix_(im_lane, re_lane)] = -sign * sine
        table[np.ix_(re_lane, im_lane)] = sign * sine
        table[np.ix_(im_lane, im_lane)] = cosine
        return table

    def rows(sign, row_order, column_order):
        both = [
            cosine[row_order][:, column_order],
            sign * sine[row_order][:, column_order],
        ]
        return left_table(np.concatenate(both, axis=0))

    cas = cosine + sine
    cas_in = np.zeros((2 * N, N))
    cas_in[re_lane] = cas
    cas_in[im_lane] = cas
    plus = lanes(1.0)
    return (
        np.stack([right_table(plus[t * 128 : (t + 1) * 128]) for t in range(3)]),
        right_table(lanes(-1.0)),
        rows(1.0, order, index),
        rows(1.0, index, order),
        rows(-1.0, order, index),
        rows(-1.0, index, order),
        right_table(cas_in),
        right_table(cas_in.T),
        left_table(cas[order]),
        left_table(cas[:, order]),
    )


def split(values):
    high = values.astype(BF16)
    low = (values - high.astype(F32)).astype(BF16)
    return high, low


def left(table_ref, values):
    high, low = split(values)
    rows = table_ref.shape[0] // 2
    by_high = jnp.dot(table_ref[...], high, preferred_element_type=F32)
    by_low = jnp.dot(table_ref[0:rows], low, preferred_element_type=F32)
    return by_high[0:rows] + (by_high[rows:] + by_low)


def right(values, table):
    high, low = split(values)
    stacked = jnp.concatenate([high, low, high], axis=1)
    return jnp.dot(stacked, table, preferred_element_type=F32)


def times_i(values):
    lane = lax.broadcasted_iota(jnp.int32, (values.shape[0], 128), 1)
    tiles = []
    for t in range(values.shape[1] // 128):
        turned = pltpu.roll(values[:, t * 128 : (t + 1) * 128], TILE, axis=1)
        tiles.append(jnp.where(lane < TILE, -turned, turned))
    return jnp.concatenate(tiles, axis=1)


def left_complex(table_ref, values):
    both = left(table_ref, values)
    return both[0:N] + times_i(both[N:])


def signed(indices):
    return jnp.where(indices < N // 2, indices, indices - N)


def doubled(values):
    tiles = []
    for t in range(3):
        part = values[:, t * TILE : (t + 1) * TILE]
        tiles += [part, part]
    return jnp.concatenate(tiles, axis=1)


def body(*refs):
    now_ref, miller_ref = refs[:2]
    later = refs[2:19]
    rest_ref, scalars_ref, pot_ref = refs[19:22]
    held = refs[22:39]
    (
        prev_ref,
        orbit_ref,
        occ_ref,
        local_ref,
        xc_ref,
        lane_plus,
        lane_minus,
        a_plus,
        b_plus,
        b_minus,
        a_minus,
        cas_in,
        cas_out,
        cas_rows,
        cas_cols,
        beta_ref,
        energy_ref,
    ) = held
    (
        hot,
        acc,
        send1,
        recv1,
        fields,
        packed,
        xc_part,
        w_send,
        w_recv,
        d_all,
        h_all,
        h_send1,
        h_recv1,
        h_send2,
        h_recv2,
        send2,
        recv2,
        table,
        lifted,
        over_send,
        over_recv,
        corr,
        corr_recv,
        sum_send1,
        sum_recv1,
        sum_send2,
        sum_recv2,
        sems,
        load_sems,
    ) = refs[39:]
    me = lax.axis_index("space")
    group = lax.axis_index("band")
    start = me * PL

    def load(at):
        return pltpu.make_async_copy(later[at], held[at], load_sems.at[at])

    for at in range(len(later)):
        load(at).start()

    barrier = pltpu.get_barrier_semaphore()

    def greet(turn, carry):
        for step in range(7):
            peer = lax.rem(me + (turn * 7 + step + 1) * STRIDE, S)
            pl.semaphore_signal(barrier, inc=1, device_id={"space": peer}, device_id_type=MESH)
        return carry

    lax.fori_loop(0, (S - 1) // 7, greet, 0)
    for step in range(1, G):
        pl.semaphore_signal(
            barrier, inc=1, device_id={"band": lax.rem(group + step, G)}, device_id_type=MESH
        )

    def space_send(phase, source, target):
        def one(turn, carry):
            for step in range(7):
                peer = lax.rem(me + (turn * 7 + step + 1) * STRIDE, S)
                pltpu.make_async_remote_copy(
                    src_ref=source(peer),
                    dst_ref=target(me),
                    send_sem=sems.at[phase, 0],
                    recv_sem=sems.at[phase, 1],
                    device_id={"space": peer},
                    device_id_type=MESH,
                ).start()
            return carry

        lax.fori_loop(0, (S - 1) // 7, one, 0)

    def band_send(phase, source, target):
        for step in (2, 1, 3):
            peer = lax.rem(group + step, G)
            pltpu.make_async_remote_copy(
                src_ref=source(peer),
                dst_ref=target(group),
                send_sem=sems.at[phase, 0],
                recv_sem=sems.at[phase, 1],
                device_id={"band": peer},
                device_id_type=MESH,
            ).start()

    def wait(phase, side, region):
        pltpu.make_async_copy(region, region, sems.at[phase, side]).wait()

    def part_chunk(ref, part):
        return lambda at: ref.at[pl.ds(part * S * CELL + at * CELL, CELL)]

    def chunk(ref):
        return lambda at: ref.at[pl.ds(at * HROWS, HROWS)]

    def keep(source, target, first, rows):
        own = pl.ds(first + me * rows, rows)
        target[own, :] = source[own, :]

    def cell_rows(part, m):
        return pl.ds(part * S * CELL + m, S, stride=CELL)

    def columns_at(step, size):
        return pl.ds(pl.multiple_of(step * size, size), size)

    def place(tile):
        def one(step, carry):
            columns = columns_at(step, PLACE)
            if tile == 0:
                row = (miller_ref[1:2, columns] - start) * N + miller_ref[0:1, columns]
                where = lax.broadcasted_iota(jnp.int16, (PL * N, PLACE), 0)
                hot[:, columns] = jnp.where(
                    where == row.astype(jnp.int16), BF16(1), BF16(0)
                )
            third = (miller_ref[2:3, columns] - tile * TILE).astype(jnp.int16)
            mask = lax.broadcasted_iota(jnp.int16, (TILE, PLACE), 0) == third
            parts = [jnp.where(mask, value, BF16(0)) for value in values_of(columns)]
            product = lax.dot_general(
                hot[:, columns],
                jnp.concatenate(parts, axis=0),
                (((1,), (1,)), ((), ())),
                preferred_element_type=F32,
            )
            acc[...] += product
            return carry

        acc[...] = jnp.zeros_like(acc)
        lax.fori_loop(0, WAVES // PLACE, one, 0, unroll=2)

    def values_of(columns):
        re_high, re_low = split(now_ref[0, 0:1, columns])
        im_high, im_low = split(now_ref[1, 0:1, columns])
        return re_high, im_high, re_low, im_low

    for t in range(3):
        place(t)
        placed = acc[:, 0:128] + acc[:, 128:256]
        if t == 0:
            load(7).wait()
        result = left_complex(
            a_plus, jnp.concatenate([placed[b * N : (b + 1) * N] for b in range(PL)], axis=1)
        )
        for r in range(PL):
            for b in range(PL):
                send1[cell_rows(t, r * PL + b), :] = result[
                    r * S : (r + 1) * S, b * 128 : (b + 1) * 128
                ]
        if t == 0:
            pl.semaphore_wait(barrier, S - 1 + G - 1)
        space_send(t, part_chunk(send1, t), part_chunk(recv1, t))
        keep(send1, recv1, t * S * CELL, CELL)

    for at in range(len(later)):
        if at != 7:
            load(at).wait()

    for r in range(PL):
        re = orbit_ref[0, 0, r]
        im = orbit_ref[1, 0, r]
        pieces = []
        for t in range(3):
            pieces += [re[:, t * TILE : (t + 1) * TILE], im[:, t * TILE : (t + 1) * TILE]]
        packed[r * N : (r + 1) * N] = jnp.concatenate(pieces, axis=1)

    every_chunk = pl.ds(0, (S - 1) * CELL)
    for t in range(3):
        wait(t, 1, recv1.at[every_chunk])
        values = jnp.concatenate(
            [
                jnp.concatenate([recv1[cell_rows(t, r * PL + b), :] for r in range(PL)], axis=1)
                for b in range(PL)
            ],
            axis=0,
        )
        result = left_complex(b_plus, values)
        result = jnp.concatenate([result[:, r * 128 : (r + 1) * 128] for r in range(PL)], axis=0)
        result = right(result, lane_plus[t])
        if t == 0:
            fields[...] = result
        else:
            fields[...] += result

    columns_of = right(2.0 * fields[...] * packed[...], cas_in[...])
    columns_of = [left(cas_rows, columns_of[r * N : (r + 1) * N]) for r in range(PL)]

    for g in range(G):
        pieces = []
        for r in range(PL):
            for b in range(PL):
                pieces.append(columns_of[r][b * S : (b + 1) * S, g * QUART : (g + 1) * QUART])
        pieces.append(jnp.zeros((S, HL - PL * PL * QUART), F32))
        w_send[g] = jnp.concatenate(pieces, axis=1)

    band_send(3, lambda peer: w_send.at[peer], lambda mine: w_recv.at[mine])
    w_recv[group] = w_send[group]
    wait(3, 1, w_recv.at[pl.ds(0, G - 1)])
    total = w_recv[0] + w_recv[1] + w_recv[2] + w_recv[3]
    d_all[group] = total
    for t in range(4):
        h_send1[pl.ds(t, S, stride=HROWS), :] = total[:, t * 128 : (t + 1) * 128]
    space_send(4, chunk(h_send1), chunk(h_recv1))
    band_send(5, lambda peer: d_all.at[group], lambda mine: d_all.at[mine])
    keep(h_send1, h_recv1, 0, HROWS)

    lane = lax.broadcasted_iota(jnp.int32, (N, PL * QUART), 1)
    first = signed(lax.broadcasted_iota(jnp.int32, (N, PL * QUART), 0))
    plane = jnp.where(lane >= QUART, 1, 0) + jnp.where(lane >= 2 * QUART, 1, 0)
    second = signed(plane + start)
    third = signed(lane - plane * QUART + group * QUART)
    squared = first * first + second * second + third * third
    coulomb = jnp.where(squared > 0, HARTREE / jnp.maximum(squared, 1).astype(F32), 0.0)

    wait(4, 1, h_recv1.at[pl.ds(0, (S - 1) * HROWS)])
    wide = jnp.concatenate([h_recv1[pl.ds(t, S, stride=HROWS), :] for t in range(4)], axis=1)
    tall = jnp.concatenate(
        [wide[:, r * PL * QUART : (r + 1) * PL * QUART] for r in range(PL)], axis=0
    )
    tall = left(cas_rows, coulomb * left(cas_cols, tall))
    wide = jnp.concatenate(
        [tall[r * S : (r + 1) * S] for r in range(PL)]
        + [jnp.zeros((S, HL - PL * PL * QUART), F32)],
        axis=1,
    )
    for t in range(4):
        h_send2[pl.ds(t, S, stride=HROWS), :] = wide[:, t * 128 : (t + 1) * 128]
    space_send(6, chunk(h_send2), chunk(h_recv2))
    keep(h_send2, h_recv2, 0, HROWS)

    def grid_values(ref):
        planes = []
        for r in range(PL):
            values = jnp.concatenate(
                [
                    jnp.concatenate(
                        [
                            ref[g][:, (r * PL + b) * QUART : (r * PL + b + 1) * QUART]
                            for g in range(G)
                        ],
                        axis=1,
                    )
                    for b in range(PL)
                ],
                axis=0,
            )
            planes.append(left(cas_cols, values))
        return right(jnp.concatenate(planes, axis=0), cas_out[...])

    wait(5, 0, d_all.at[pl.ds(0, G - 1)])
    wait(5, 1, d_all.at[pl.ds(0, G - 1)])
    known = grid_values(d_all) * jnp.concatenate([doubled(xc_ref[r]) for r in range(PL)], axis=0)
    local = jnp.concatenate([doubled(local_ref[r]) for r in range(PL)], axis=0)
    fields[...] = local * fields[...] + known * packed[...]
    xc_part[...] = known

    wait(6, 1, h_recv2.at[pl.ds(0, (S - 1) * HROWS)])
    h_all[group] = jnp.concatenate(
        [h_recv2[pl.ds(t, S, stride=HROWS), :] for t in range(4)], axis=1
    )
    band_send(7, lambda peer: h_all.at[group], lambda mine: h_all.at[mine])
    wait(7, 0, h_all.at[pl.ds(0, G - 1)])
    wait(7, 1, h_all.at[pl.ds(0, G - 1)])

    hartree = grid_values(h_all)
    mixed = right(fields[...] + hartree * packed[...], lane_minus[...])
    result = left_complex(
        b_minus, jnp.concatenate([mixed[r * N : (r + 1) * N] for r in range(PL)], axis=1)
    )
    for b in range(PL):
        for r in range(PL):
            for t in range(3):
                send2[cell_rows(b, r * PL + t), :] = result[
                    b * S : (b + 1) * S, (r * 3 + t) * 128 : (r * 3 + t + 1) * 128
                ]
        space_send(8 + b, part_chunk(send2, b), part_chunk(recv2, b))
        keep(send2, recv2, b * S * CELL, CELL)
    potential = hartree + xc_part[...]
    for r in range(PL):
        pot_ref[r] = jnp.concatenate(
            [potential[r * N : (r + 1) * N, t * 128 : t * 128 + TILE] for t in range(3)], axis=1
        )

    energy = energy_ref[0:1].reshape(1, 1)

    def read_waves(b, columns):
        seen = hot[b * N : (b + 1) * N, columns]
        found = jnp.dot(table[...], seen, preferred_element_type=F32)
        mask = lax.broadcasted_iota(jnp.int32, (N, READ), 0) == miller_ref[2:3, columns]
        sums = []
        for half in range(2):
            total = None
            for t in range(3):
                at = t * 128 + half * TILE
                kept = jnp.where(
                    mask[t * TILE : (t + 1) * TILE],
                    found[at : at + TILE] + found[384 + at : 384 + at + TILE],
                    0.0,
                )
                total = kept if total is None else total + kept
            sums.append(jnp.sum(total, axis=0, keepdims=True))
        if b > 0:
            sums = [sums[half] + lifted[group, half : half + 1, columns] for half in range(2)]
        if b == PL - 1:
            first = signed(miller_ref[0:1, columns])
            second = signed(miller_ref[1:2, columns])
            third = signed(miller_ref[2:3, columns])
            squared = first * first + second * second + third * third
            diagonal = KINETIC * squared.astype(F32) / float(N * N) - energy
            sums = [sums[half] + diagonal * now_ref[half, 0:1, columns] for half in range(2)]
        for half in range(2):
            lifted[group, half : half + 1, columns] = sums[half]

    blocks = WAVES // BLOCK
    per_block = BLOCK // READ

    def block(ref, at, n):
        return ref.at[at, :, pl.ds(n * BLOCK, BLOCK)]

    for b in range(PL):
        wait(8 + b, 1, recv2.at[every_chunk])
        values = jnp.concatenate(
            [
                jnp.concatenate([recv2[cell_rows(b, r * PL + t), :] for t in range(3)], axis=1)
                for r in range(PL)
            ],
            axis=0,
        )
        result = left_complex(a_minus, values)
        high = result.astype(BF16).astype(F32)
        table[...] = jnp.transpose(jnp.concatenate([high, result - high], axis=1)).astype(BF16)

        def one(step, carry):
            read_waves(b, columns_at(step, READ))
            return carry

        for n in range(blocks):
            lax.fori_loop(n * per_block, (n + 1) * per_block, one, 0, unroll=2)
            if b == PL - 1:
                band_send(
                    11 + n,
                    lambda peer: block(lifted, group, n),
                    lambda mine: block(lifted, mine, n),
                )

    def columns_of_tile(step):
        return pl.ds(pl.multiple_of(step * 128, 128), 128)

    def overlap(step, sums):
        columns = columns_of_tile(step)
        occ_re = occ_ref[0, :, columns]
        occ_im = occ_ref[1, :, columns]
        out = []
        for v in range(G):
            re = lifted[v, 0:1, columns]
            im = lifted[v, 1:2, columns]
            out.append(sums[2 * v] + (occ_re * re + occ_im * im))
            out.append(sums[2 * v + 1] + (occ_re * im - occ_im * re))
        return tuple(out)

    def three(ref, n):
        return ref.at[pl.ds(0, G - 1), :, pl.ds(n * BLOCK, BLOCK)]

    tiles = BLOCK // 128
    sums = tuple(jnp.zeros((16, 128), F32) for _ in range(2 * G))
    for n in range(blocks):
        wait(11 + n, 0, three(lifted, n))
        wait(11 + n, 1, three(lifted, n))
        sums = lax.fori_loop(n * tiles, (n + 1) * tiles, overlap, sums, unroll=4)
    lane = lax.broadcasted_iota(jnp.int32, (16, 128), 1)
    band_of = lane // 16
    own_row = (lane % 16) == lax.broadcasted_iota(jnp.int32, (16, 128), 0)
    matrix = jnp.zeros((16, 128), F32)
    for row in range(2 * G):
        column = jnp.sum(sums[row], axis=1, keepdims=True)
        matrix = jnp.where(band_of == row, column, matrix)
    over_send[0] = jnp.sum(jnp.where(own_row, matrix, 0.0), axis=0, keepdims=True)
    space_send(15, lambda peer: over_send.at[0], lambda mine: over_recv.at[mine])
    over_recv[me] = over_send[0]
    wait(15, 1, over_recv.at[pl.ds(0, S - 1)])
    row_sum = jnp.sum(over_recv[...], axis=0)
    spread = jnp.where(own_row, jnp.broadcast_to(row_sum, (16, 128)), 0.0)
    weights = []
    for row in range(2 * G):
        column = jnp.sum(jnp.where(band_of == row, spread, 0.0), axis=1, keepdims=True)
        weights.append(jnp.broadcast_to(column, (16, 128)))

    def correct(step, carry):
        columns = columns_of_tile(step)
        occ_re = occ_ref[0, :, columns]
        occ_im = occ_ref[1, :, columns]
        for v in range(G):
            w_re, w_im = weights[2 * v], weights[2 * v + 1]
            corr[v, 0:1, columns] = jnp.sum(occ_re * w_re - occ_im * w_im, axis=0, keepdims=True)
            corr[v, 1:2, columns] = jnp.sum(occ_re * w_im + occ_im * w_re, axis=0, keepdims=True)
        return carry

    for n in range(blocks):
        lax.fori_loop(n * tiles, (n + 1) * tiles, correct, 0, unroll=4)
        band_send(
            16 + n, lambda peer: block(corr, peer, n), lambda mine: block(corr_recv, mine, n)
        )

    corr_recv[group] = corr[group]
    beta_old = beta_ref[0:1].reshape(1, 1)
    partial = [jnp.zeros((1, 1), F32) for _ in range(4)]
    for n in range(blocks):
        wait(16 + n, 1, three(corr_recv, n))
        columns = pl.ds(n * BLOCK, BLOCK)
        for part in range(2):
            removed = (
                corr_recv[0, part : part + 1, columns]
                + corr_recv[1, part : part + 1, columns]
                + corr_recv[2, part : part + 1, columns]
                + corr_recv[3, part : part + 1, columns]
            )
            q = now_ref[part, 0:1, columns]
            p = prev_ref[part, 0:1, columns]
            u = lifted[group, part : part + 1, columns] - removed - beta_old * p
            rest_ref[part, 0:1, columns] = u
            for slot, product in enumerate((u * u, q * u, q * p, q * q)):
                partial[slot] = partial[slot] + jnp.sum(product, axis=1, keepdims=True)
    lane = lax.broadcasted_iota(jnp.int32, (1, 128), 1)
    row = jnp.zeros((1, 128), F32)
    for slot in range(4):
        row = jnp.where(lane == slot, partial[slot], row)
    sum_send1[0] = row
    band_send(20, lambda peer: sum_send1.at[0], lambda mine: sum_recv1.at[mine])
    sum_recv1[group] = sum_send1[0]
    wait(20, 1, sum_recv1.at[pl.ds(0, G - 1)])
    sum_send2[0] = jnp.sum(sum_recv1[...], axis=0)
    space_send(21, lambda peer: sum_send2.at[0], lambda mine: sum_recv2.at[mine])
    sum_recv2[me] = sum_send2[0]

    for part in range(3):
        wait(part, 0, send1.at[every_chunk])
        wait(8 + part, 0, send2.at[every_chunk])
    wait(3, 0, w_send.at[pl.ds(0, G - 1)])
    wait(4, 0, h_send1.at[pl.ds(0, (S - 1) * HROWS)])
    wait(6, 0, h_send2.at[pl.ds(0, (S - 1) * HROWS)])
    wait(15, 0, over_recv.at[pl.ds(0, S - 1)])
    for n in range(blocks):
        wait(16 + n, 0, three(corr, n))
    wait(20, 0, sum_recv1.at[pl.ds(0, G - 1)])

    wait(21, 0, sum_recv2.at[pl.ds(0, S - 1)])
    wait(21, 1, sum_recv2.at[pl.ds(0, S - 1)])
    row = jnp.sum(sum_recv2[...], axis=0)

    def pick(slot):
        return jnp.sum(jnp.where(lane == slot, row, 0.0), axis=1, keepdims=True)

    norm_u, q_u, q_p, norm_q = [pick(slot) for slot in range(4)]
    alpha = (q_u + beta_old * q_p) / ENTRIES
    square = norm_u - 2.0 * alpha * q_u + alpha * alpha * norm_q
    beta_new = jnp.sqrt(square / ENTRIES)
    scalars_ref[...] = jnp.where(lane == 0, alpha, beta_new)


def finish(rest_ref, now_ref, scalars_ref, pot_in, next_ref, coef_ref, pot_ref):
    alpha = scalars_ref[0:1, 0:1]
    beta_new = scalars_ref[0:1, 1:2]
    inverse = 1.0 / beta_new
    for part in range(2):
        next_ref[part] = (rest_ref[part] - alpha * now_ref[part]) * inverse
    coef_ref[...] = scalars_ref[0:1, 0:2]
    pot_ref[...] = pot_in[...]


def per_device(
    lanczos_now,
    lanczos_prev,
    beta_prev,
    orbitals,
    band_energy,
    occupied,
    local_pot,
    xc_kernel,
    miller,
):
    later = [lanczos_prev, orbitals, occupied, local_pot, xc_kernel]
    later += [jnp.asarray(table) for table in make_tables()]
    later += [beta_prev, band_energy]
    vmem = pl.BlockSpec(memory_space=pltpu.VMEM)
    in_hbm = pl.BlockSpec(memory_space=pltpu.HBM)
    wide = pltpu.VMEM((3 * S * CELL, 128), F32)
    narrow = pltpu.VMEM((S * HROWS, 128), F32)
    quarter = pltpu.VMEM((G, S, HL), F32)
    band_waves = pltpu.VMEM((G, 2, WAVES), F32)
    real_grid = jax.ShapeDtypeStruct((PL, N, N), F32)
    waves = jax.ShapeDtypeStruct((2, 1, WAVES), F32)
    rest, scalars, potential = pl.pallas_call(
        body,
        out_shape=(waves, jax.ShapeDtypeStruct((1, 128), F32), real_grid),
        in_specs=[vmem, vmem] + [in_hbm] * len(later),
        out_specs=(vmem, vmem, vmem),
        scratch_shapes=[pltpu.VMEM(array.shape, array.dtype) for array in later]
        + [
            pltpu.VMEM((PL * N, WAVES), BF16),
            pltpu.VMEM((PL * N, 256), F32),
            wide,
            wide,
            pltpu.VMEM((PL * N, 384), F32),
            pltpu.VMEM((PL * N, 384), F32),
            pltpu.VMEM((PL * N, 384), F32),
            quarter,
            quarter,
            quarter,
            quarter,
            narrow,
            narrow,
            narrow,
            narrow,
            wide,
            wide,
            pltpu.VMEM((768, N), BF16),
            band_waves,
            pltpu.VMEM((1, 1, 128), F32),
            pltpu.VMEM((S, 1, 128), F32),
            band_waves,
            band_waves,
            pltpu.VMEM((1, 1, 128), F32),
            pltpu.VMEM((G, 1, 128), F32),
            pltpu.VMEM((1, 1, 128), F32),
            pltpu.VMEM((S, 1, 128), F32),
            pltpu.SemaphoreType.DMA((22, 2)),
            pltpu.SemaphoreType.DMA((len(later),)),
        ],
        compiler_params=pltpu.CompilerParams(
            collective_id=0, has_side_effects=True, vmem_limit_bytes=60 * 1024 * 1024
        ),
    )(lanczos_now, miller, *later)
    return pl.pallas_call(
        finish,
        out_shape=(waves, jax.ShapeDtypeStruct((1, 2), F32), real_grid),
        in_specs=[vmem] * 4,
        out_specs=(vmem,) * 3,
    )(rest, lanczos_now, scalars, potential)


def solution(mesh):
    return jax.shard_map(
        per_device,
        mesh=mesh,
        in_specs=(
            P(None, "band", "space"),
            P(None, "band", "space"),
            P(),
            P(None, "band", "space", None, None),
            P("band"),
            P(None, "band", "space"),
            P("space", None, None),
            P("space", None, None),
            P(None, "space"),
        ),
        out_specs=(P(None, "band", "space"), P(), P("space", None, None)),
        check_vma=False,
    )
```

```python
import math

import jax
import jax.numpy as jnp
import ml_dtypes
import numpy as np
from jax import lax
from jax.experimental import pallas as pl
from jax.experimental.pallas import tpu as pltpu
from jax.sharding import PartitionSpec as P

MESH = pl.DeviceIdType.MESH
F32 = jnp.float32
BF16 = jnp.bfloat16
KINETIC = 8.0
HARTREE = 4.0
N = 192
S = 64
Z = 8
C = 8
G = 4
PL = 3
CELL = 9
HROWS = 4
QUART = N // G
HL = 512
TILE = 64
WAVES = 16384
PLACE = 2048
READ = 1024
BLOCK = 4096
STRIDE = 29
ENTRIES = float(2 * G * WAVES * S)


def split_np(table):
    high = table.astype(np.float32).astype(ml_dtypes.bfloat16)
    low = (table - high.astype(np.float64)).astype(np.float32).astype(ml_dtypes.bfloat16)
    return high, low


def left_table(table):
    high, low = split_np(table)
    return np.concatenate([high, low], axis=0)


def right_table(table):
    high, low = split_np(table)
    return np.concatenate([high, high, low], axis=0)


def make_tables():
    index = np.arange(N)
    angle = 2.0 * np.pi * (np.outer(index, index) % N) / N
    cosine = np.cos(angle) / math.sqrt(N)
    sine = np.sin(angle) / math.sqrt(N)
    order = np.concatenate([np.arange(S) * PL + part for part in range(PL)])
    re_lane = index // TILE * 128 + index % TILE
    im_lane = re_lane + TILE

    def lanes(sign):
        table = np.zeros((2 * N, 2 * N))
        table[np.ix_(re_lane, re_lane)] = cosine
        table[np.ix_(im_lane, re_lane)] = -sign * sine
        table[np.ix_(re_lane, im_lane)] = sign * sine
        table[np.ix_(im_lane, im_lane)] = cosine
        return table

    def rows(sign, row_order, column_order):
        both = [
            cosine[row_order][:, column_order],
            sign * sine[row_order][:, column_order],
        ]
        return left_table(np.concatenate(both, axis=0))

    cas = cosine + sine
    cas_in = np.zeros((2 * N, N))
    cas_in[re_lane] = cas
    cas_in[im_lane] = cas
    plus = lanes(1.0)
    return (
        np.stack([right_table(plus[t * 128 : (t + 1) * 128]) for t in range(3)]),
        right_table(lanes(-1.0)),
        rows(1.0, order, index),
        rows(1.0, index, order),
        rows(-1.0, order, index),
        rows(-1.0, index, order),
        right_table(cas_in),
        right_table(cas_in.T),
        left_table(cas[order]),
        left_table(cas[:, order]),
    )


def split(values):
    high = values.astype(BF16)
    low = (values - high.astype(F32)).astype(BF16)
    return high, low


def left(table_ref, values):
    high, low = split(values)
    rows = table_ref.shape[0] // 2
    by_high = jnp.dot(table_ref[...], high, preferred_element_type=F32)
    by_low = jnp.dot(table_ref[0:rows], low, preferred_element_type=F32)
    return by_high[0:rows] + (by_high[rows:] + by_low)


def right(values, table):
    high, low = split(values)
    stacked = jnp.concatenate([high, low, high], axis=1)
    return jnp.dot(stacked, table, preferred_element_type=F32)


def times_i(values):
    lane = lax.broadcasted_iota(jnp.int32, (values.shape[0], 128), 1)
    tiles = []
    for t in range(values.shape[1] // 128):
        turned = pltpu.roll(values[:, t * 128 : (t + 1) * 128], TILE, axis=1)
        tiles.append(jnp.where(lane < TILE, -turned, turned))
    return jnp.concatenate(tiles, axis=1)


def left_complex(table_ref, values):
    both = left(table_ref, values)
    return both[0:N] + times_i(both[N:])


def signed(indices):
    return jnp.where(indices < N // 2, indices, indices - N)


def doubled(values):
    tiles = []
    for t in range(3):
        part = values[:, t * TILE : (t + 1) * TILE]
        tiles += [part, part]
    return jnp.concatenate(tiles, axis=1)


def body(*refs):
    now_ref, miller_ref = refs[:2]
    later = refs[2:19]
    rest_ref, scalars_ref, pot_ref = refs[19:22]
    held = refs[22:39]
    (
        prev_ref,
        orbit_ref,
        occ_ref,
        local_ref,
        xc_ref,
        lane_plus,
        lane_minus,
        a_plus,
        b_plus,
        b_minus,
        a_minus,
        cas_in,
        cas_out,
        cas_rows,
        cas_cols,
        beta_ref,
        energy_ref,
    ) = held
    (
        hot,
        acc,
        send1,
        turn1,
        recv1,
        fields,
        packed,
        xc_part,
        w_send,
        w_recv,
        d_all,
        h_all,
        h_send1,
        h_recv1,
        h_send2,
        h_recv2,
        send2,
        turn2,
        recv2,
        table,
        lifted,
        over_send,
        over_recv,
        corr,
        corr_recv,
        sum_send1,
        sum_recv1,
        sum_send2,
        sum_recv2,
        sems,
        load_sems,
    ) = refs[39:]
    me = lax.axis_index("space")
    group = lax.axis_index("band")
    start = me * PL

    def load(at):
        return pltpu.make_async_copy(later[at], held[at], load_sems.at[at])

    for at in range(len(later)):
        load(at).start()

    barrier = pltpu.get_barrier_semaphore()

    def greet(turn, carry):
        for step in range(7):
            peer = lax.rem(me + (turn * 7 + step + 1) * STRIDE, S)
            pl.semaphore_signal(barrier, inc=1, device_id={"space": peer}, device_id_type=MESH)
        return carry

    lax.fori_loop(0, (S - 1) // 7, greet, 0)
    for step in range(1, G):
        pl.semaphore_signal(
            barrier, inc=1, device_id={"band": lax.rem(group + step, G)}, device_id_type=MESH
        )

    def space_send(phase, source, target):
        def one(turn, carry):
            for step in range(7):
                peer = lax.rem(me + (turn * 7 + step + 1) * STRIDE, S)
                pltpu.make_async_remote_copy(
                    src_ref=source(peer),
                    dst_ref=target(me),
                    send_sem=sems.at[phase, 0],
                    recv_sem=sems.at[phase, 1],
                    device_id={"space": peer},
                    device_id_type=MESH,
                ).start()
            return carry

        lax.fori_loop(0, (S - 1) // 7, one, 0)

    def band_send(phase, source, target):
        for step in (2, 1, 3):
            peer = lax.rem(group + step, G)
            pltpu.make_async_remote_copy(
                src_ref=source(peer),
                dst_ref=target(group),
                send_sem=sems.at[phase, 0],
                recv_sem=sems.at[phase, 1],
                device_id={"band": peer},
                device_id_type=MESH,
            ).start()

    def wait(phase, side, region):
        pltpu.make_async_copy(region, region, sems.at[phase, side]).wait()

    here_z = me // C
    here_c = lax.rem(me, C)
    every_step = pl.ds(0, (Z - 1) * C * CELL)

    def z_send(phase, part, source, target):
        def rows(z):
            return pl.ds(part * S * CELL + z * (C * CELL), C * CELL)

        for step in (4, 3, 5, 2, 6, 1, 7):
            z = lax.rem(here_z + step, Z)
            pltpu.make_async_remote_copy(
                src_ref=source.at[rows(z)],
                dst_ref=target.at[rows(here_z)],
                send_sem=sems.at[phase, 0],
                recv_sem=sems.at[phase, 1],
                device_id={"space": z * C + here_c},
                device_id_type=MESH,
            ).start()
        own = pl.ds(pl.multiple_of(part * S * CELL + here_z * (C * CELL), 8), C * CELL)
        target[own, :] = source[own, :]

    def c_send(z_phase, phase, part, source, target):
        wait(z_phase, 1, source.at[every_step])
        source_view = source.reshape(3 * Z, C * CELL, 128)
        target_view = target.reshape(3 * Z, C * CELL, 128)
        for step in (4, 3, 5, 2, 6, 1, 7):
            c = lax.rem(here_c + step, C)
            pltpu.make_async_remote_copy(
                src_ref=source_view.at[pl.ds(part * Z, Z), pl.ds(c * CELL, CELL)],
                dst_ref=target_view.at[pl.ds(part * Z, Z), pl.ds(here_c * CELL, CELL)],
                send_sem=sems.at[phase, 0],
                recv_sem=sems.at[phase, 1],
                device_id={"space": here_z * C + c},
                device_id_type=MESH,
            ).start()
        for z in range(Z):
            own = pl.ds(part * S * CELL + z * (C * CELL) + here_c * CELL, CELL)
            target[own, :] = source[own, :]

    def chunk(ref):
        return lambda at: ref.at[pl.ds(at * HROWS, HROWS)]

    def keep(source, target, first, rows):
        own = pl.ds(first + me * rows, rows)
        target[own, :] = source[own, :]

    def cell_rows(part, m):
        return pl.ds(part * S * CELL + m, S, stride=CELL)

    def columns_at(step, size):
        return pl.ds(pl.multiple_of(step * size, size), size)

    def place(tile):
        def one(step, carry):
            columns = columns_at(step, PLACE)
            if tile == 0:
                row = (miller_ref[1:2, columns] - start) * N + miller_ref[0:1, columns]
                where = lax.broadcasted_iota(jnp.int16, (PL * N, PLACE), 0)
                hot[:, columns] = jnp.where(
                    where == row.astype(jnp.int16), BF16(1), BF16(0)
                )
            third = (miller_ref[2:3, columns] - tile * TILE).astype(jnp.int16)
            mask = lax.broadcasted_iota(jnp.int16, (TILE, PLACE), 0) == third
            parts = [jnp.where(mask, value, BF16(0)) for value in values_of(columns)]
            product = lax.dot_general(
                hot[:, columns],
                jnp.concatenate(parts, axis=0),
                (((1,), (1,)), ((), ())),
                preferred_element_type=F32,
            )
            acc[...] += product
            return carry

        acc[...] = jnp.zeros_like(acc)
        lax.fori_loop(0, WAVES // PLACE, one, 0, unroll=2)

    def values_of(columns):
        re_high, re_low = split(now_ref[0, 0:1, columns])
        im_high, im_low = split(now_ref[1, 0:1, columns])
        return re_high, im_high, re_low, im_low

    for t in range(3):
        place(t)
        placed = acc[:, 0:128] + acc[:, 128:256]
        if t == 0:
            load(7).wait()
        result = left_complex(
            a_plus, jnp.concatenate([placed[b * N : (b + 1) * N] for b in range(PL)], axis=1)
        )
        for r in range(PL):
            for b in range(PL):
                send1[cell_rows(t, r * PL + b), :] = result[
                    r * S : (r + 1) * S, b * 128 : (b + 1) * 128
                ]
        if t == 0:
            pl.semaphore_wait(barrier, S - 1 + G - 1)
        z_send(22 + t, t, send1, turn1)
        if t > 0:
            c_send(22 + t - 1, t - 1, t - 1, turn1, recv1)
    c_send(24, 2, 2, turn1, recv1)

    for at in range(len(later)):
        if at != 7:
            load(at).wait()

    for r in range(PL):
        re = orbit_ref[0, 0, r]
        im = orbit_ref[1, 0, r]
        pieces = []
        for t in range(3):
            pieces += [re[:, t * TILE : (t + 1) * TILE], im[:, t * TILE : (t + 1) * TILE]]
        packed[r * N : (r + 1) * N] = jnp.concatenate(pieces, axis=1)

    for t in range(3):
        wait(t, 1, recv1.at[every_step])
        values = jnp.concatenate(
            [
                jnp.concatenate([recv1[cell_rows(t, r * PL + b), :] for r in range(PL)], axis=1)
                for b in range(PL)
            ],
            axis=0,
        )
        result = left_complex(b_plus, values)
        result = jnp.concatenate([result[:, r * 128 : (r + 1) * 128] for r in range(PL)], axis=0)
        result = right(result, lane_plus[t])
        if t == 0:
            fields[...] = result
        else:
            fields[...] += result

    columns_of = right(2.0 * fields[...] * packed[...], cas_in[...])
    columns_of = [left(cas_rows, columns_of[r * N : (r + 1) * N]) for r in range(PL)]

    for g in range(G):
        pieces = []
        for r in range(PL):
            for b in range(PL):
                pieces.append(columns_of[r][b * S : (b + 1) * S, g * QUART : (g + 1) * QUART])
        pieces.append(jnp.zeros((S, HL - PL * PL * QUART), F32))
        w_send[g] = jnp.concatenate(pieces, axis=1)

    band_send(3, lambda peer: w_send.at[peer], lambda mine: w_recv.at[mine])
    w_recv[group] = w_send[group]
    wait(3, 1, w_recv.at[pl.ds(0, G - 1)])
    total = w_recv[0] + w_recv[1] + w_recv[2] + w_recv[3]
    d_all[group] = total
    for t in range(4):
        h_send1[pl.ds(t, S, stride=HROWS), :] = total[:, t * 128 : (t + 1) * 128]
    space_send(4, chunk(h_send1), chunk(h_recv1))
    band_send(5, lambda peer: d_all.at[group], lambda mine: d_all.at[mine])
    keep(h_send1, h_recv1, 0, HROWS)

    lane = lax.broadcasted_iota(jnp.int32, (N, PL * QUART), 1)
    first = signed(lax.broadcasted_iota(jnp.int32, (N, PL * QUART), 0))
    plane = jnp.where(lane >= QUART, 1, 0) + jnp.where(lane >= 2 * QUART, 1, 0)
    second = signed(plane + start)
    third = signed(lane - plane * QUART + group * QUART)
    squared = first * first + second * second + third * third
    coulomb = jnp.where(squared > 0, HARTREE / jnp.maximum(squared, 1).astype(F32), 0.0)

    wait(4, 1, h_recv1.at[pl.ds(0, (S - 1) * HROWS)])
    wide = jnp.concatenate([h_recv1[pl.ds(t, S, stride=HROWS), :] for t in range(4)], axis=1)
    tall = jnp.concatenate(
        [wide[:, r * PL * QUART : (r + 1) * PL * QUART] for r in range(PL)], axis=0
    )
    tall = left(cas_rows, coulomb * left(cas_cols, tall))
    wide = jnp.concatenate(
        [tall[r * S : (r + 1) * S] for r in range(PL)]
        + [jnp.zeros((S, HL - PL * PL * QUART), F32)],
        axis=1,
    )
    for t in range(4):
        h_send2[pl.ds(t, S, stride=HROWS), :] = wide[:, t * 128 : (t + 1) * 128]
    space_send(6, chunk(h_send2), chunk(h_recv2))
    keep(h_send2, h_recv2, 0, HROWS)

    def grid_values(ref):
        planes = []
        for r in range(PL):
            values = jnp.concatenate(
                [
                    jnp.concatenate(
                        [
                            ref[g][:, (r * PL + b) * QUART : (r * PL + b + 1) * QUART]
                            for g in range(G)
                        ],
                        axis=1,
                    )
                    for b in range(PL)
                ],
                axis=0,
            )
            planes.append(left(cas_cols, values))
        return right(jnp.concatenate(planes, axis=0), cas_out[...])

    wait(5, 0, d_all.at[pl.ds(0, G - 1)])
    wait(5, 1, d_all.at[pl.ds(0, G - 1)])
    known = grid_values(d_all) * jnp.concatenate([doubled(xc_ref[r]) for r in range(PL)], axis=0)
    local = jnp.concatenate([doubled(local_ref[r]) for r in range(PL)], axis=0)
    fields[...] = local * fields[...] + known * packed[...]
    xc_part[...] = known

    wait(6, 1, h_recv2.at[pl.ds(0, (S - 1) * HROWS)])
    h_all[group] = jnp.concatenate(
        [h_recv2[pl.ds(t, S, stride=HROWS), :] for t in range(4)], axis=1
    )
    band_send(7, lambda peer: h_all.at[group], lambda mine: h_all.at[mine])
    wait(7, 0, h_all.at[pl.ds(0, G - 1)])
    wait(7, 1, h_all.at[pl.ds(0, G - 1)])

    hartree = grid_values(h_all)
    mixed = right(fields[...] + hartree * packed[...], lane_minus[...])
    result = left_complex(
        b_minus, jnp.concatenate([mixed[r * N : (r + 1) * N] for r in range(PL)], axis=1)
    )
    for b in range(PL):
        for r in range(PL):
            for t in range(3):
                send2[cell_rows(b, r * PL + t), :] = result[
                    b * S : (b + 1) * S, (r * 3 + t) * 128 : (r * 3 + t + 1) * 128
                ]
        z_send(25 + b, b, send2, turn2)
    potential = hartree + xc_part[...]
    for r in range(PL):
        pot_ref[r] = jnp.concatenate(
            [potential[r * N : (r + 1) * N, t * 128 : t * 128 + TILE] for t in range(3)], axis=1
        )

    energy = energy_ref[0:1].reshape(1, 1)

    def read_waves(b, columns):
        seen = hot[b * N : (b + 1) * N, columns]
        found = jnp.dot(table[...], seen, preferred_element_type=F32)
        mask = lax.broadcasted_iota(jnp.int32, (N, READ), 0) == miller_ref[2:3, columns]
        sums = []
        for half in range(2):
            total = None
            for t in range(3):
                at = t * 128 + half * TILE
                kept = jnp.where(
                    mask[t * TILE : (t + 1) * TILE],
                    found[at : at + TILE] + found[384 + at : 384 + at + TILE],
                    0.0,
                )
                total = kept if total is None else total + kept
            sums.append(jnp.sum(total, axis=0, keepdims=True))
        if b > 0:
            sums = [sums[half] + lifted[group, half : half + 1, columns] for half in range(2)]
        if b == PL - 1:
            first = signed(miller_ref[0:1, columns])
            second = signed(miller_ref[1:2, columns])
            third = signed(miller_ref[2:3, columns])
            squared = first * first + second * second + third * third
            diagonal = KINETIC * squared.astype(F32) / float(N * N) - energy
            sums = [sums[half] + diagonal * now_ref[half, 0:1, columns] for half in range(2)]
        for half in range(2):
            lifted[group, half : half + 1, columns] = sums[half]

    blocks = WAVES // BLOCK
    per_block = BLOCK // READ

    def block(ref, at, n):
        return ref.at[at, :, pl.ds(n * BLOCK, BLOCK)]

    c_send(25, 8, 0, turn2, recv2)
    for b in range(PL):
        wait(8 + b, 1, recv2.at[every_step])
        values = jnp.concatenate(
            [
                jnp.concatenate([recv2[cell_rows(b, r * PL + t), :] for t in range(3)], axis=1)
                for r in range(PL)
            ],
            axis=0,
        )
        result = left_complex(a_minus, values)
        high = result.astype(BF16).astype(F32)
        table[...] = jnp.transpose(jnp.concatenate([high, result - high], axis=1)).astype(BF16)

        def one(step, carry):
            read_waves(b, columns_at(step, READ))
            return carry

        for n in range(blocks):
            lax.fori_loop(n * per_block, (n + 1) * per_block, one, 0, unroll=2)
            if n == 1 and b < PL - 1:
                c_send(25 + b + 1, 8 + b + 1, b + 1, turn2, recv2)
            if b == PL - 1:
                band_send(
                    11 + n,
                    lambda peer: block(lifted, group, n),
                    lambda mine: block(lifted, mine, n),
                )

    def columns_of_tile(step):
        return pl.ds(pl.multiple_of(step * 128, 128), 128)

    def overlap(step, sums):
        columns = columns_of_tile(step)
        occ_re = occ_ref[0, :, columns]
        occ_im = occ_ref[1, :, columns]
        out = []
        for v in range(G):
            re = lifted[v, 0:1, columns]
            im = lifted[v, 1:2, columns]
            out.append(sums[2 * v] + (occ_re * re + occ_im * im))
            out.append(sums[2 * v + 1] + (occ_re * im - occ_im * re))
        return tuple(out)

    def three(ref, n):
        return ref.at[pl.ds(0, G - 1), :, pl.ds(n * BLOCK, BLOCK)]

    tiles = BLOCK // 128
    sums = tuple(jnp.zeros((16, 128), F32) for _ in range(2 * G))
    for n in range(blocks):
        wait(11 + n, 0, three(lifted, n))
        wait(11 + n, 1, three(lifted, n))
        sums = lax.fori_loop(n * tiles, (n + 1) * tiles, overlap, sums, unroll=4)
    lane = lax.broadcasted_iota(jnp.int32, (16, 128), 1)
    band_of = lane // 16
    own_row = (lane % 16) == lax.broadcasted_iota(jnp.int32, (16, 128), 0)
    matrix = jnp.zeros((16, 128), F32)
    for row in range(2 * G):
        column = jnp.sum(sums[row], axis=1, keepdims=True)
        matrix = jnp.where(band_of == row, column, matrix)
    over_send[0] = jnp.sum(jnp.where(own_row, matrix, 0.0), axis=0, keepdims=True)
    space_send(15, lambda peer: over_send.at[0], lambda mine: over_recv.at[mine])
    over_recv[me] = over_send[0]
    wait(15, 1, over_recv.at[pl.ds(0, S - 1)])
    row_sum = jnp.sum(over_recv[...], axis=0)
    spread = jnp.where(own_row, jnp.broadcast_to(row_sum, (16, 128)), 0.0)
    weights = []
    for row in range(2 * G):
        column = jnp.sum(jnp.where(band_of == row, spread, 0.0), axis=1, keepdims=True)
        weights.append(jnp.broadcast_to(column, (16, 128)))

    def correct(step, carry):
        columns = columns_of_tile(step)
        occ_re = occ_ref[0, :, columns]
        occ_im = occ_ref[1, :, columns]
        for v in range(G):
            w_re, w_im = weights[2 * v], weights[2 * v + 1]
            corr[v, 0:1, columns] = jnp.sum(occ_re * w_re - occ_im * w_im, axis=0, keepdims=True)
            corr[v, 1:2, columns] = jnp.sum(occ_re * w_im + occ_im * w_re, axis=0, keepdims=True)
        return carry

    for n in range(blocks):
        lax.fori_loop(n * tiles, (n + 1) * tiles, correct, 0, unroll=4)
        band_send(
            16 + n, lambda peer: block(corr, peer, n), lambda mine: block(corr_recv, mine, n)
        )

    corr_recv[group] = corr[group]
    beta_old = beta_ref[0:1].reshape(1, 1)
    partial = [jnp.zeros((1, 1), F32) for _ in range(4)]
    for n in range(blocks):
        wait(16 + n, 1, three(corr_recv, n))
        columns = pl.ds(n * BLOCK, BLOCK)
        for part in range(2):
            removed = (
                corr_recv[0, part : part + 1, columns]
                + corr_recv[1, part : part + 1, columns]
                + corr_recv[2, part : part + 1, columns]
                + corr_recv[3, part : part + 1, columns]
            )
            q = now_ref[part, 0:1, columns]
            p = prev_ref[part, 0:1, columns]
            u = lifted[group, part : part + 1, columns] - removed - beta_old * p
            rest_ref[part, 0:1, columns] = u
            for slot, product in enumerate((u * u, q * u, q * p, q * q)):
                partial[slot] = partial[slot] + jnp.sum(product, axis=1, keepdims=True)
    lane = lax.broadcasted_iota(jnp.int32, (1, 128), 1)
    row = jnp.zeros((1, 128), F32)
    for slot in range(4):
        row = jnp.where(lane == slot, partial[slot], row)
    sum_send1[0] = row
    band_send(20, lambda peer: sum_send1.at[0], lambda mine: sum_recv1.at[mine])
    sum_recv1[group] = sum_send1[0]
    wait(20, 1, sum_recv1.at[pl.ds(0, G - 1)])
    sum_send2[0] = jnp.sum(sum_recv1[...], axis=0)
    space_send(21, lambda peer: sum_send2.at[0], lambda mine: sum_recv2.at[mine])
    sum_recv2[me] = sum_send2[0]

    for part in range(3):
        for phase in (part, 8 + part, 22 + part, 25 + part):
            wait(phase, 0, send1.at[every_step])
    wait(3, 0, w_send.at[pl.ds(0, G - 1)])
    wait(4, 0, h_send1.at[pl.ds(0, (S - 1) * HROWS)])
    wait(6, 0, h_send2.at[pl.ds(0, (S - 1) * HROWS)])
    wait(15, 0, over_recv.at[pl.ds(0, S - 1)])
    for n in range(blocks):
        wait(16 + n, 0, three(corr, n))
    wait(20, 0, sum_recv1.at[pl.ds(0, G - 1)])

    wait(21, 0, sum_recv2.at[pl.ds(0, S - 1)])
    wait(21, 1, sum_recv2.at[pl.ds(0, S - 1)])
    row = jnp.sum(sum_recv2[...], axis=0)

    def pick(slot):
        return jnp.sum(jnp.where(lane == slot, row, 0.0), axis=1, keepdims=True)

    norm_u, q_u, q_p, norm_q = [pick(slot) for slot in range(4)]
    alpha = (q_u + beta_old * q_p) / ENTRIES
    square = norm_u - 2.0 * alpha * q_u + alpha * alpha * norm_q
    beta_new = jnp.sqrt(square / ENTRIES)
    scalars_ref[...] = jnp.where(lane == 0, alpha, beta_new)


def finish(rest_ref, now_ref, scalars_ref, pot_in, next_ref, coef_ref, pot_ref):
    alpha = scalars_ref[0:1, 0:1]
    beta_new = scalars_ref[0:1, 1:2]
    inverse = 1.0 / beta_new
    for part in range(2):
        next_ref[part] = (rest_ref[part] - alpha * now_ref[part]) * inverse
    coef_ref[...] = scalars_ref[0:1, 0:2]
    pot_ref[...] = pot_in[...]


def per_device(
    lanczos_now,
    lanczos_prev,
    beta_prev,
    orbitals,
    band_energy,
    occupied,
    local_pot,
    xc_kernel,
    miller,
):
    later = [lanczos_prev, orbitals, occupied, local_pot, xc_kernel]
    later += [jnp.asarray(table) for table in make_tables()]
    later += [beta_prev, band_energy]
    vmem = pl.BlockSpec(memory_space=pltpu.VMEM)
    in_hbm = pl.BlockSpec(memory_space=pltpu.HBM)
    wide = pltpu.VMEM((3 * S * CELL, 128), F32)
    narrow = pltpu.VMEM((S * HROWS, 128), F32)
    quarter = pltpu.VMEM((G, S, HL), F32)
    band_waves = pltpu.VMEM((G, 2, WAVES), F32)
    real_grid = jax.ShapeDtypeStruct((PL, N, N), F32)
    waves = jax.ShapeDtypeStruct((2, 1, WAVES), F32)
    rest, scalars, potential = pl.pallas_call(
        body,
        out_shape=(waves, jax.ShapeDtypeStruct((1, 128), F32), real_grid),
        in_specs=[vmem, vmem] + [in_hbm] * len(later),
        out_specs=(vmem, vmem, vmem),
        scratch_shapes=[pltpu.VMEM(array.shape, array.dtype) for array in later]
        + [
            pltpu.VMEM((PL * N, WAVES), BF16),
            pltpu.VMEM((PL * N, 256), F32),
            wide,
            wide,
            wide,
            pltpu.VMEM((PL * N, 384), F32),
            pltpu.VMEM((PL * N, 384), F32),
            pltpu.VMEM((PL * N, 384), F32),
            quarter,
            quarter,
            quarter,
            quarter,
            narrow,
            narrow,
            narrow,
            narrow,
            wide,
            wide,
            wide,
            pltpu.VMEM((768, N), BF16),
            band_waves,
            pltpu.VMEM((1, 1, 128), F32),
            pltpu.VMEM((S, 1, 128), F32),
            band_waves,
            band_waves,
            pltpu.VMEM((1, 1, 128), F32),
            pltpu.VMEM((G, 1, 128), F32),
            pltpu.VMEM((1, 1, 128), F32),
            pltpu.VMEM((S, 1, 128), F32),
            pltpu.SemaphoreType.DMA((28, 2)),
            pltpu.SemaphoreType.DMA((len(later),)),
        ],
        compiler_params=pltpu.CompilerParams(
            collective_id=0, has_side_effects=True, vmem_limit_bytes=60 * 1024 * 1024
        ),
    )(lanczos_now, miller, *later)
    return pl.pallas_call(
        finish,
        out_shape=(waves, jax.ShapeDtypeStruct((1, 2), F32), real_grid),
        in_specs=[vmem] * 4,
        out_specs=(vmem,) * 3,
    )(rest, lanczos_now, scalars, potential)


def solution(mesh):
    return jax.shard_map(
        per_device,
        mesh=mesh,
        in_specs=(
            P(None, "band", "space"),
            P(None, "band", "space"),
            P(),
            P(None, "band", "space", None, None),
            P("band"),
            P(None, "band", "space"),
            P("space", None, None),
            P("space", None, None),
            P(None, "space"),
        ),
        out_specs=(P(None, "band", "space"), P(), P("space", None, None)),
        check_vma=False,
    )
```

```python
import math

import jax
import jax.numpy as jnp
import ml_dtypes
import numpy as np
from jax import lax
from jax.experimental import pallas as pl
from jax.experimental.pallas import tpu as pltpu
from jax.sharding import PartitionSpec as P

MESH = pl.DeviceIdType.MESH
F32 = jnp.float32
BF16 = jnp.bfloat16
KINETIC = 8.0
HARTREE = 4.0
N = 192
S = 64
G = 4
PL = 3
CELL = 9
HROWS = 4
QUART = N // G
THIRD = PL * QUART
HL = 512
LOW = 4
HIGH = S // LOW
TILE = 64
WAVES = 16384
PLACE = 2048
READ = 256
BLOCK = 4096
W_PHASE = (3, 22, 23, 24)
H_PHASE = (7, 25, 26, 27)
STRIDE = 29
ENTRIES = float(2 * G * WAVES * S)


def split_np(table):
    high = table.astype(np.float32).astype(ml_dtypes.bfloat16)
    low = (table - high.astype(np.float64)).astype(np.float32).astype(ml_dtypes.bfloat16)
    return high, low


def left_table(table):
    high, low = split_np(table)
    return np.concatenate([high, low], axis=0)


def right_table(table):
    high, low = split_np(table)
    return np.concatenate([high, high, low], axis=0)


def make_tables():
    index = np.arange(N)
    angle = 2.0 * np.pi * (np.outer(index, index) % N) / N
    cosine = np.cos(angle) / math.sqrt(N)
    sine = np.sin(angle) / math.sqrt(N)
    order = np.concatenate([np.arange(S) * PL + part for part in range(PL)])
    re_lane = index // TILE * 128 + index % TILE
    im_lane = re_lane + TILE

    def lanes(sign):
        table = np.zeros((2 * N, 2 * N))
        table[np.ix_(re_lane, re_lane)] = cosine
        table[np.ix_(im_lane, re_lane)] = -sign * sine
        table[np.ix_(re_lane, im_lane)] = sign * sine
        table[np.ix_(im_lane, im_lane)] = cosine
        return table

    def rows(sign, row_order, column_order):
        both = [
            cosine[row_order][:, column_order],
            sign * sine[row_order][:, column_order],
        ]
        return left_table(np.concatenate(both, axis=0))

    cas = cosine + sine
    cas_in = np.zeros((2 * N, N))
    cas_in[re_lane] = cas
    cas_in[im_lane] = cas
    plus = lanes(1.0)
    return (
        np.stack([right_table(plus[t * 128 : (t + 1) * 128]) for t in range(3)]),
        right_table(lanes(-1.0)),
        rows(1.0, order, index),
        rows(1.0, index, order),
        rows(-1.0, order, index),
        rows(-1.0, index, order),
        right_table(cas_in),
        right_table(cas_in.T),
        left_table(cas[order]),
        left_table(cas[:, order]),
    )


def split(values):
    high = values.astype(BF16)
    low = (values - high.astype(F32)).astype(BF16)
    return high, low


def left(table_ref, values):
    high, low = split(values)
    rows = table_ref.shape[0] // 2
    by_high = jnp.dot(table_ref[...], high, preferred_element_type=F32)
    by_low = jnp.dot(table_ref[0:rows], low, preferred_element_type=F32)
    return by_high[0:rows] + (by_high[rows:] + by_low)


def right(values, table):
    high, low = split(values)
    stacked = jnp.concatenate([high, low, high], axis=1)
    return jnp.dot(stacked, table, preferred_element_type=F32)


def times_i(values):
    lane = lax.broadcasted_iota(jnp.int32, (values.shape[0], 128), 1)
    tiles = []
    for t in range(values.shape[1] // 128):
        turned = pltpu.roll(values[:, t * 128 : (t + 1) * 128], TILE, axis=1)
        tiles.append(jnp.where(lane < TILE, -turned, turned))
    return jnp.concatenate(tiles, axis=1)


def left_complex(table_ref, values):
    both = left(table_ref, values)
    return both[0:N] + times_i(both[N:])


def signed(indices):
    return jnp.where(indices < N // 2, indices, indices - N)


def doubled(values):
    tiles = []
    for t in range(3):
        part = values[:, t * TILE : (t + 1) * TILE]
        tiles += [part, part]
    return jnp.concatenate(tiles, axis=1)


def body(*refs):
    now_ref, miller_ref = refs[:2]
    later = refs[2:19]
    rest_ref, scalars_ref, pot_ref = refs[19:22]
    held = refs[22:39]
    (
        prev_ref,
        orbit_ref,
        occ_ref,
        local_ref,
        xc_ref,
        lane_plus,
        lane_minus,
        a_plus,
        b_plus,
        b_minus,
        a_minus,
        cas_in,
        cas_out,
        cas_rows,
        cas_cols,
        beta_ref,
        energy_ref,
    ) = held
    (
        hot,
        acc,
        send1,
        recv1,
        fields,
        packed,
        xc_part,
        w_send,
        w_recv,
        d_all,
        h_all,
        h_send1,
        h_recv1,
        h_send2,
        h_recv2,
        send2,
        recv2,
        table,
        lifted,
        over_send,
        over_recv,
        corr,
        corr_recv,
        sum_send1,
        sum_recv1,
        sum_send2,
        sum_recv2,
        sems,
        load_sems,
    ) = refs[39:]
    me = lax.axis_index("space")
    group = lax.axis_index("band")
    start = me * PL

    def load(at):
        return pltpu.make_async_copy(later[at], held[at], load_sems.at[at])

    for at in range(len(later)):
        load(at).start()

    barrier = pltpu.get_barrier_semaphore()

    def greet(turn, carry):
        for step in range(7):
            peer = lax.rem(me + (turn * 7 + step + 1) * STRIDE, S)
            pl.semaphore_signal(barrier, inc=1, device_id={"space": peer}, device_id_type=MESH)
        return carry

    lax.fori_loop(0, (S - 1) // 7, greet, 0)
    for step in range(1, G):
        for low in range(LOW):
            peer = me // LOW * LOW + lax.rem(me + low, LOW)
            pl.semaphore_signal(
                barrier,
                inc=1,
                device_id={"band": lax.rem(group + step, G), "space": peer},
                device_id_type=MESH,
            )

    def space_send(phase, source, target):
        def one(turn, carry):
            for step in range(7):
                peer = lax.rem(me + (turn * 7 + step + 1) * STRIDE, S)
                pltpu.make_async_remote_copy(
                    src_ref=source(peer),
                    dst_ref=target(me),
                    send_sem=sems.at[phase, 0],
                    recv_sem=sems.at[phase, 1],
                    device_id={"space": peer},
                    device_id_type=MESH,
                ).start()
            return carry

        lax.fori_loop(0, (S - 1) // 7, one, 0)

    def band_send(phase, source, target):
        for step in (2, 1, 3):
            peer = lax.rem(group + step, G)
            pltpu.make_async_remote_copy(
                src_ref=source(peer),
                dst_ref=target(group),
                send_sem=sems.at[phase, 0],
                recv_sem=sems.at[phase, 1],
                device_id={"band": peer},
                device_id_type=MESH,
            ).start()

    def wait(phase, side, region):
        pltpu.make_async_copy(region, region, sems.at[phase, side]).wait()

    def part_chunk(ref, part):
        return lambda at: ref.at[pl.ds(part * S * CELL + at * CELL, CELL)]

    def chunk(ref):
        return lambda at: ref.at[pl.ds(at * HROWS, HROWS)]

    def keep(source, target, first, rows):
        own = pl.ds(first + me * rows, rows)
        target[own, :] = source[own, :]

    def cell_rows(part, m):
        return pl.ds(part * S * CELL + m, S, stride=CELL)

    def columns_at(step, size):
        return pl.ds(pl.multiple_of(step * size, size), size)

    def place(tile):
        def one(step, carry):
            columns = columns_at(step, PLACE)
            if tile == 0:
                row = (miller_ref[1:2, columns] - start) * N + miller_ref[0:1, columns]
                where = lax.broadcasted_iota(jnp.int16, (PL * N, PLACE), 0)
                hot[:, columns] = jnp.where(
                    where == row.astype(jnp.int16), BF16(1), BF16(0)
                )
            third = (miller_ref[2:3, columns] - tile * TILE).astype(jnp.int16)
            mask = lax.broadcasted_iota(jnp.int16, (TILE, PLACE), 0) == third
            parts = [jnp.where(mask, value, BF16(0)) for value in values_of(columns)]
            product = lax.dot_general(
                hot[:, columns],
                jnp.concatenate(parts, axis=0),
                (((1,), (1,)), ((), ())),
                preferred_element_type=F32,
            )
            acc[...] += product
            return carry

        acc[...] = jnp.zeros_like(acc)
        lax.fori_loop(0, WAVES // PLACE, one, 0, unroll=2)

    def values_of(columns):
        re_high, re_low = split(now_ref[0, 0:1, columns])
        im_high, im_low = split(now_ref[1, 0:1, columns])
        return re_high, im_high, re_low, im_low

    for t in range(3):
        place(t)
        placed = acc[:, 0:128] + acc[:, 128:256]
        if t == 0:
            load(7).wait()
        result = left_complex(
            a_plus, jnp.concatenate([placed[b * N : (b + 1) * N] for b in range(PL)], axis=1)
        )
        for r in range(PL):
            for b in range(PL):
                send1[cell_rows(t, r * PL + b), :] = result[
                    r * S : (r + 1) * S, b * 128 : (b + 1) * 128
                ]
        if t == 0:
            pl.semaphore_wait(barrier, S - 1 + (G - 1) * LOW)
        space_send(t, part_chunk(send1, t), part_chunk(recv1, t))
        keep(send1, recv1, t * S * CELL, CELL)

    for at in range(len(later)):
        if at != 7:
            load(at).wait()

    for r in range(PL):
        re = orbit_ref[0, 0, r]
        im = orbit_ref[1, 0, r]
        pieces = []
        for t in range(3):
            pieces += [re[:, t * TILE : (t + 1) * TILE], im[:, t * TILE : (t + 1) * TILE]]
        packed[r * N : (r + 1) * N] = jnp.concatenate(pieces, axis=1)

    every_chunk = pl.ds(0, (S - 1) * CELL)
    for t in range(3):
        wait(t, 1, recv1.at[every_chunk])
        values = jnp.concatenate(
            [
                jnp.concatenate([recv1[cell_rows(t, r * PL + b), :] for r in range(PL)], axis=1)
                for b in range(PL)
            ],
            axis=0,
        )
        result = left_complex(b_plus, values)
        result = jnp.concatenate([result[:, r * 128 : (r + 1) * 128] for r in range(PL)], axis=0)
        result = right(result, lane_plus[t])
        if t == 0:
            fields[...] = result
        else:
            fields[...] += result

    def tile_at(t):
        return pl.ds(t * 128, 128)

    tails = [[] for _ in range(G)]
    for r in range(PL):
        plane = pl.ds(r * N, N)
        values = left(cas_rows, right(2.0 * fields[plane, :] * packed[plane, :], cas_in[...]))
        for g in range(G):
            row = jnp.concatenate(
                [
                    values[b * S : (b + 1) * S, g * QUART : (g + 1) * QUART]
                    for b in range(PL)
                ],
                axis=1,
            )
            w_send[g, :, tile_at(r)] = row[:, :128]
            tails[g].append(row[:, 128:])
        if r == PL - 1:
            for g in range(G):
                w_send[g, :, tile_at(PL)] = jnp.concatenate(
                    tails[g] + [jnp.zeros((S, HL - PL * THIRD), F32)], axis=1
                )
        for t in (r,) if r < PL - 1 else (r, PL):
            band_send(
                W_PHASE[t],
                lambda peer: w_send.at[peer, :, tile_at(t)],
                lambda mine: w_recv.at[mine, :, tile_at(t)],
            )

    w_recv[group] = w_send[group]
    totals = []
    for t in range(4):
        wait(W_PHASE[t], 1, w_recv.at[pl.ds(0, G - 1), :, tile_at(t)])
        parts = [w_recv[g, :, tile_at(t)] for g in range(G)]
        totals.append(parts[0] + parts[1] + parts[2] + parts[3])
        h_send1[pl.ds(t, S, stride=HROWS), :] = totals[t]
    total = jnp.concatenate(totals, axis=1)
    space_send(4, chunk(h_send1), chunk(h_recv1))
    d_all[group] = total
    band_send(5, lambda peer: d_all.at[group], lambda mine: d_all.at[mine])
    keep(h_send1, h_recv1, 0, HROWS)

    lane = lax.broadcasted_iota(jnp.int32, (N, PL * QUART), 1)
    first = signed(lax.broadcasted_iota(jnp.int32, (N, PL * QUART), 0))
    plane = jnp.where(lane >= QUART, 1, 0) + jnp.where(lane >= 2 * QUART, 1, 0)
    second = signed(plane + start)
    third = signed(lane - plane * QUART + group * QUART)
    squared = first * first + second * second + third * third
    coulomb = jnp.where(squared > 0, HARTREE / jnp.maximum(squared, 1).astype(F32), 0.0)

    wait(4, 1, h_recv1.at[pl.ds(0, (S - 1) * HROWS)])
    pieces = [h_recv1[pl.ds(t, S, stride=HROWS), :] for t in range(4)]
    tall = jnp.concatenate(
        [
            jnp.concatenate([pieces[r], pieces[PL][:, r * 16 : (r + 1) * 16]], axis=1)
            for r in range(PL)
        ],
        axis=0,
    )
    tall = left(cas_rows, coulomb * left(cas_cols, tall))
    for r in range(PL):
        h_send2[pl.ds(r, S, stride=HROWS), :] = tall[r * S : (r + 1) * S, :128]
    h_send2[pl.ds(PL, S, stride=HROWS), :] = jnp.concatenate(
        [tall[r * S : (r + 1) * S, 128:] for r in range(PL)]
        + [jnp.zeros((S, HL - PL * THIRD), F32)],
        axis=1,
    )
    space_send(6, chunk(h_send2), chunk(h_recv2))
    keep(h_send2, h_recv2, 0, HROWS)

    def grid_values(ref, r):
        rows = [
            jnp.concatenate(
                [ref[g, :, tile_at(r)], ref[g, :, tile_at(PL)][:, r * 16 : (r + 1) * 16]], axis=1
            )
            for g in range(G)
        ]
        values = jnp.concatenate(
            [
                jnp.concatenate([row[:, b * QUART : (b + 1) * QUART] for row in rows], axis=1)
                for b in range(PL)
            ],
            axis=0,
        )
        return right(left(cas_cols, values), cas_out[...])

    wait(5, 0, d_all.at[pl.ds(0, G - 1)])
    wait(5, 1, d_all.at[pl.ds(0, G - 1)])
    for r in range(PL):
        plane = pl.ds(r * N, N)
        known = grid_values(d_all, r) * doubled(xc_ref[r])
        fields[plane, :] = doubled(local_ref[r]) * fields[plane, :] + known * packed[plane, :]
        xc_part[plane, :] = known

    wait(6, 1, h_recv2.at[pl.ds(0, (S - 1) * HROWS)])
    for t in (PL, 0, 1, 2):
        h_all[group, :, tile_at(t)] = h_recv2[pl.ds(t, S, stride=HROWS), :]
        band_send(
            H_PHASE[t],
            lambda peer: h_all.at[group, :, tile_at(t)],
            lambda mine: h_all.at[mine, :, tile_at(t)],
        )
    mixed = []
    for r in range(PL):
        plane = pl.ds(r * N, N)
        for t in (PL, 0) if r == 0 else (r,):
            wait(H_PHASE[t], 0, h_all.at[pl.ds(0, G - 1), :, tile_at(t)])
            wait(H_PHASE[t], 1, h_all.at[pl.ds(0, G - 1), :, tile_at(t)])
        hartree = grid_values(h_all, r)
        mixed.append(right(fields[plane, :] + hartree * packed[plane, :], lane_minus[...]))
        xc_part[plane, :] += hartree
    result = left_complex(b_minus, jnp.concatenate(mixed, axis=1))
    for b in range(PL):
        for r in range(PL):
            for t in range(3):
                send2[cell_rows(b, r * PL + t), :] = result[
                    b * S : (b + 1) * S, (r * 3 + t) * 128 : (r * 3 + t + 1) * 128
                ]
        space_send(8 + b, part_chunk(send2, b), part_chunk(recv2, b))
        keep(send2, recv2, b * S * CELL, CELL)
    potential = xc_part[...]
    for r in range(PL):
        pot_ref[r] = jnp.concatenate(
            [potential[r * N : (r + 1) * N, t * 128 : t * 128 + TILE] for t in range(3)], axis=1
        )

    energy = energy_ref[0:1].reshape(1, 1)

    def read_waves(b, columns):
        seen = hot[b * N : (b + 1) * N, columns]
        found = jnp.dot(table[...], seen, preferred_element_type=F32)
        mask = lax.broadcasted_iota(jnp.int32, (N, READ), 0) == miller_ref[2:3, columns]
        sums = []
        for half in range(2):
            total = None
            for t in range(3):
                at = t * 128 + half * TILE
                kept = jnp.where(
                    mask[t * TILE : (t + 1) * TILE],
                    found[at : at + TILE] + found[384 + at : 384 + at + TILE],
                    0.0,
                )
                total = kept if total is None else total + kept
            sums.append(jnp.sum(total, axis=0, keepdims=True))
        if b > 0:
            sums = [sums[half] + lifted[group, half : half + 1, columns] for half in range(2)]
        if b == PL - 1:
            first = signed(miller_ref[0:1, columns])
            second = signed(miller_ref[1:2, columns])
            third = signed(miller_ref[2:3, columns])
            squared = first * first + second * second + third * third
            diagonal = KINETIC * squared.astype(F32) / float(N * N) - energy
            sums = [sums[half] + diagonal * now_ref[half, 0:1, columns] for half in range(2)]
        for half in range(2):
            lifted[group, half : half + 1, columns] = sums[half]

    blocks = WAVES // BLOCK
    per_block = BLOCK // READ

    def block(ref, at, n):
        return ref.at[at, :, pl.ds(n * BLOCK, BLOCK)]

    for b in range(PL):
        wait(8 + b, 1, recv2.at[every_chunk])
        values = jnp.concatenate(
            [
                jnp.concatenate([recv2[cell_rows(b, r * PL + t), :] for t in range(3)], axis=1)
                for r in range(PL)
            ],
            axis=0,
        )
        result = left_complex(a_minus, values)
        high = result.astype(BF16).astype(F32)
        table[...] = jnp.transpose(jnp.concatenate([high, result - high], axis=1)).astype(BF16)

        def one(step, carry):
            read_waves(b, columns_at(step, READ))
            return carry

        for n in range(blocks):
            lax.fori_loop(n * per_block, (n + 1) * per_block, one, 0, unroll=4)
            if b == PL - 1:
                band_send(
                    11 + n,
                    lambda peer: block(lifted, group, n),
                    lambda mine: block(lifted, mine, n),
                )

    def columns_of_tile(step):
        return pl.ds(pl.multiple_of(step * 128, 128), 128)

    def overlap(step, sums):
        columns = columns_of_tile(step)
        occ_re = occ_ref[0, :, columns]
        occ_im = occ_ref[1, :, columns]
        out = []
        for v in range(G):
            re = lifted[v, 0:1, columns]
            im = lifted[v, 1:2, columns]
            out.append(sums[2 * v] + (occ_re * re + occ_im * im))
            out.append(sums[2 * v + 1] + (occ_re * im - occ_im * re))
        return tuple(out)

    def three(ref, n):
        return ref.at[pl.ds(0, G - 1), :, pl.ds(n * BLOCK, BLOCK)]

    tiles = BLOCK // 128
    sums = tuple(jnp.zeros((16, 128), F32) for _ in range(2 * G))
    for n in range(blocks):
        wait(11 + n, 0, three(lifted, n))
        wait(11 + n, 1, three(lifted, n))
        sums = lax.fori_loop(n * tiles, (n + 1) * tiles, overlap, sums, unroll=4)
    lane = lax.broadcasted_iota(jnp.int32, (16, 128), 1)
    band_of = lane // 16
    own_row = (lane % 16) == lax.broadcasted_iota(jnp.int32, (16, 128), 0)
    matrix = jnp.zeros((16, 128), F32)
    for row in range(2 * G):
        column = jnp.sum(sums[row], axis=1, keepdims=True)
        matrix = jnp.where(band_of == row, column, matrix)
    over_send[0] = jnp.sum(jnp.where(own_row, matrix, 0.0), axis=0, keepdims=True)
    space_send(15, lambda peer: over_send.at[0], lambda mine: over_recv.at[mine])
    over_recv[me] = over_send[0]
    wait(15, 1, over_recv.at[pl.ds(0, S - 1)])
    row_sum = jnp.sum(over_recv[...], axis=0)
    spread = jnp.where(own_row, jnp.broadcast_to(row_sum, (16, 128)), 0.0)
    weights = []
    for row in range(2 * G):
        column = jnp.sum(jnp.where(band_of == row, spread, 0.0), axis=1, keepdims=True)
        weights.append(jnp.broadcast_to(column, (16, 128)))

    def correct(step, carry):
        columns = columns_of_tile(step)
        occ_re = occ_ref[0, :, columns]
        occ_im = occ_ref[1, :, columns]
        for v in range(G):
            w_re, w_im = weights[2 * v], weights[2 * v + 1]
            corr[v, 0:1, columns] = jnp.sum(occ_re * w_re - occ_im * w_im, axis=0, keepdims=True)
            corr[v, 1:2, columns] = jnp.sum(occ_re * w_im + occ_im * w_re, axis=0, keepdims=True)
        return carry

    for n in range(blocks):
        lax.fori_loop(n * tiles, (n + 1) * tiles, correct, 0, unroll=4)
        band_send(
            16 + n, lambda peer: block(corr, peer, n), lambda mine: block(corr_recv, mine, n)
        )

    corr_recv[group] = corr[group]
    beta_old = beta_ref[0:1].reshape(1, 1)
    partial = [jnp.zeros((1, 1), F32) for _ in range(4)]
    for n in range(blocks):
        wait(16 + n, 1, three(corr_recv, n))
        columns = pl.ds(n * BLOCK, BLOCK)
        for part in range(2):
            removed = (
                corr_recv[0, part : part + 1, columns]
                + corr_recv[1, part : part + 1, columns]
                + corr_recv[2, part : part + 1, columns]
                + corr_recv[3, part : part + 1, columns]
            )
            q = now_ref[part, 0:1, columns]
            p = prev_ref[part, 0:1, columns]
            u = lifted[group, part : part + 1, columns] - removed - beta_old * p
            rest_ref[part, 0:1, columns] = u
            for slot, product in enumerate((u * u, q * u, q * p, q * q)):
                partial[slot] = partial[slot] + jnp.sum(product, axis=1, keepdims=True)
    lane = lax.broadcasted_iota(jnp.int32, (1, 128), 1)
    row = jnp.zeros((1, 128), F32)
    for slot in range(4):
        row = jnp.where(lane == slot, partial[slot], row)
    sum_send1[0] = row
    here_low = lax.rem(me, LOW)
    here_high = me // LOW
    for step in range(1, G * LOW):
        peer_band = lax.rem(group + step // LOW, G)
        peer_low = lax.rem(here_low + step % LOW, LOW)
        pltpu.make_async_remote_copy(
            src_ref=sum_send1.at[0],
            dst_ref=sum_recv1.at[group * LOW + here_low],
            send_sem=sems.at[20, 0],
            recv_sem=sems.at[20, 1],
            device_id={"band": peer_band, "space": here_high * LOW + peer_low},
            device_id_type=MESH,
        ).start()
    sum_recv1[group * LOW + here_low] = sum_send1[0]
    wait(20, 1, sum_recv1.at[pl.ds(0, G * LOW - 1)])
    sum_send2[0] = jnp.sum(sum_recv1[...], axis=0)
    for step in range(1, HIGH):
        peer_high = lax.rem(here_high + step, HIGH)
        pltpu.make_async_remote_copy(
            src_ref=sum_send2.at[0],
            dst_ref=sum_recv2.at[here_high],
            send_sem=sems.at[21, 0],
            recv_sem=sems.at[21, 1],
            device_id={"space": peer_high * LOW + here_low},
            device_id_type=MESH,
        ).start()
    sum_recv2[here_high] = sum_send2[0]

    for part in range(3):
        wait(part, 0, send1.at[every_chunk])
        wait(8 + part, 0, send2.at[every_chunk])
    for t in range(4):
        wait(W_PHASE[t], 0, w_send.at[pl.ds(0, G - 1), :, tile_at(t)])
    wait(4, 0, h_send1.at[pl.ds(0, (S - 1) * HROWS)])
    wait(6, 0, h_send2.at[pl.ds(0, (S - 1) * HROWS)])
    wait(15, 0, over_recv.at[pl.ds(0, S - 1)])
    for n in range(blocks):
        wait(16 + n, 0, three(corr, n))
    wait(20, 0, sum_recv1.at[pl.ds(0, G * LOW - 1)])

    wait(21, 0, sum_recv2.at[pl.ds(0, HIGH - 1)])
    wait(21, 1, sum_recv2.at[pl.ds(0, HIGH - 1)])
    row = jnp.sum(sum_recv2[...], axis=0)

    def pick(slot):
        return jnp.sum(jnp.where(lane == slot, row, 0.0), axis=1, keepdims=True)

    norm_u, q_u, q_p, norm_q = [pick(slot) for slot in range(4)]
    alpha = (q_u + beta_old * q_p) / ENTRIES
    square = norm_u - 2.0 * alpha * q_u + alpha * alpha * norm_q
    beta_new = jnp.sqrt(square / ENTRIES)
    scalars_ref[...] = jnp.where(lane == 0, alpha, beta_new)


def finish(rest_ref, now_ref, scalars_ref, pot_in, next_ref, coef_ref, pot_ref):
    alpha = scalars_ref[0:1, 0:1]
    beta_new = scalars_ref[0:1, 1:2]
    inverse = 1.0 / beta_new
    for part in range(2):
        next_ref[part] = (rest_ref[part] - alpha * now_ref[part]) * inverse
    coef_ref[...] = scalars_ref[0:1, 0:2]
    pot_ref[...] = pot_in[...]


def per_device(
    lanczos_now,
    lanczos_prev,
    beta_prev,
    orbitals,
    band_energy,
    occupied,
    local_pot,
    xc_kernel,
    miller,
):
    later = [lanczos_prev, orbitals, occupied, local_pot, xc_kernel]
    later += [jnp.asarray(table) for table in make_tables()]
    later += [beta_prev, band_energy]
    vmem = pl.BlockSpec(memory_space=pltpu.VMEM)
    in_hbm = pl.BlockSpec(memory_space=pltpu.HBM)
    wide = pltpu.VMEM((3 * S * CELL, 128), F32)
    narrow = pltpu.VMEM((S * HROWS, 128), F32)
    quarter = pltpu.VMEM((G, S, HL), F32)
    band_waves = pltpu.VMEM((G, 2, WAVES), F32)
    real_grid = jax.ShapeDtypeStruct((PL, N, N), F32)
    waves = jax.ShapeDtypeStruct((2, 1, WAVES), F32)
    rest, scalars, potential = pl.pallas_call(
        body,
        out_shape=(waves, jax.ShapeDtypeStruct((1, 128), F32), real_grid),
        in_specs=[vmem, vmem] + [in_hbm] * len(later),
        out_specs=(vmem, vmem, vmem),
        scratch_shapes=[pltpu.VMEM(array.shape, array.dtype) for array in later]
        + [
            pltpu.VMEM((PL * N, WAVES), BF16),
            pltpu.VMEM((PL * N, 256), F32),
            wide,
            wide,
            pltpu.VMEM((PL * N, 384), F32),
            pltpu.VMEM((PL * N, 384), F32),
            pltpu.VMEM((PL * N, 384), F32),
            quarter,
            quarter,
            quarter,
            quarter,
            narrow,
            narrow,
            narrow,
            narrow,
            wide,
            wide,
            pltpu.VMEM((768, N), BF16),
            band_waves,
            pltpu.VMEM((1, 1, 128), F32),
            pltpu.VMEM((S, 1, 128), F32),
            band_waves,
            band_waves,
            pltpu.VMEM((1, 1, 128), F32),
            pltpu.VMEM((G * LOW, 1, 128), F32),
            pltpu.VMEM((1, 1, 128), F32),
            pltpu.VMEM((HIGH, 1, 128), F32),
            pltpu.SemaphoreType.DMA((28, 2)),
            pltpu.SemaphoreType.DMA((len(later),)),
        ],
        compiler_params=pltpu.CompilerParams(
            collective_id=0, has_side_effects=True, vmem_limit_bytes=60 * 1024 * 1024
        ),
    )(lanczos_now, miller, *later)
    return pl.pallas_call(
        finish,
        out_shape=(waves, jax.ShapeDtypeStruct((1, 2), F32), real_grid),
        in_specs=[vmem] * 4,
        out_specs=(vmem,) * 3,
    )(rest, lanczos_now, scalars, potential)


def solution(mesh):
    return jax.shard_map(
        per_device,
        mesh=mesh,
        in_specs=(
            P(None, "band", "space"),
            P(None, "band", "space"),
            P(),
            P(None, "band", "space", None, None),
            P("band"),
            P(None, "band", "space"),
            P("space", None, None),
            P("space", None, None),
            P(None, "space"),
        ),
        out_specs=(P(None, "band", "space"), P(), P("space", None, None)),
        check_vma=False,
    )
```

```python
import math

import jax
import jax.numpy as jnp
import ml_dtypes
import numpy as np
from jax import lax
from jax.experimental import pallas as pl
from jax.experimental.pallas import tpu as pltpu
from jax.sharding import PartitionSpec as P

MESH = pl.DeviceIdType.MESH
F32 = jnp.float32
BF16 = jnp.bfloat16
KINETIC = 8.0
HARTREE = 4.0
N = 192
S = 64
G = 4
PL = 3
CELL = 9
HROWS = 4
QUART = N // G
THIRD = PL * QUART
HL = 512
LOW = 4
HIGH = S // LOW
TILE = 64
WAVES = 16384
PLACE = 2048
READ = 1024
PASSES = ((0, 1), (1, 3))
BLOCK = 4096
W_PHASE = (3, 22, 23, 24)
H_PHASE = (7, 25, 26, 27)
STRIDE = 29
ENTRIES = float(2 * G * WAVES * S)


def split_np(table):
    high = table.astype(np.float32).astype(ml_dtypes.bfloat16)
    low = (table - high.astype(np.float64)).astype(np.float32).astype(ml_dtypes.bfloat16)
    return high, low


def left_table(table):
    high, low = split_np(table)
    return np.concatenate([high, low], axis=0)


def right_table(table):
    high, low = split_np(table)
    return np.concatenate([high, high, low], axis=0)


def make_tables():
    index = np.arange(N)
    angle = 2.0 * np.pi * (np.outer(index, index) % N) / N
    cosine = np.cos(angle) / math.sqrt(N)
    sine = np.sin(angle) / math.sqrt(N)
    order = np.concatenate([np.arange(S) * PL + part for part in range(PL)])
    re_lane = index // TILE * 128 + index % TILE
    im_lane = re_lane + TILE

    def lanes(sign):
        table = np.zeros((2 * N, 2 * N))
        table[np.ix_(re_lane, re_lane)] = cosine
        table[np.ix_(im_lane, re_lane)] = -sign * sine
        table[np.ix_(re_lane, im_lane)] = sign * sine
        table[np.ix_(im_lane, im_lane)] = cosine
        return table

    def rows(sign, row_order, column_order):
        both = [
            cosine[row_order][:, column_order],
            sign * sine[row_order][:, column_order],
        ]
        return left_table(np.concatenate(both, axis=0))

    cas = cosine + sine
    cas_in = np.zeros((2 * N, N))
    cas_in[re_lane] = cas
    cas_in[im_lane] = cas
    plus = lanes(1.0)
    return (
        np.stack([right_table(plus[t * 128 : (t + 1) * 128]) for t in range(3)]),
        right_table(lanes(-1.0)),
        rows(1.0, order, index),
        rows(1.0, index, order),
        rows(-1.0, order, index),
        rows(-1.0, index, order),
        right_table(cas_in),
        right_table(cas_in.T),
        left_table(cas[order]),
        left_table(cas[:, order]),
    )


def split(values):
    high = values.astype(BF16)
    low = (values - high.astype(F32)).astype(BF16)
    return high, low


def left(table_ref, values):
    high, low = split(values)
    rows = table_ref.shape[0] // 2
    by_high = jnp.dot(table_ref[...], high, preferred_element_type=F32)
    by_low = jnp.dot(table_ref[0:rows], low, preferred_element_type=F32)
    return by_high[0:rows] + (by_high[rows:] + by_low)


def right(values, table):
    high, low = split(values)
    stacked = jnp.concatenate([high, low, high], axis=1)
    return jnp.dot(stacked, table, preferred_element_type=F32)


def times_i(values):
    lane = lax.broadcasted_iota(jnp.int32, (values.shape[0], 128), 1)
    tiles = []
    for t in range(values.shape[1] // 128):
        turned = pltpu.roll(values[:, t * 128 : (t + 1) * 128], TILE, axis=1)
        tiles.append(jnp.where(lane < TILE, -turned, turned))
    return jnp.concatenate(tiles, axis=1)


def left_complex(table_ref, values):
    both = left(table_ref, values)
    return both[0:N] + times_i(both[N:])


def signed(indices):
    return jnp.where(indices < N // 2, indices, indices - N)


def doubled(values):
    tiles = []
    for t in range(3):
        part = values[:, t * TILE : (t + 1) * TILE]
        tiles += [part, part]
    return jnp.concatenate(tiles, axis=1)


def body(*refs):
    now_ref, miller_ref = refs[:2]
    later = refs[2:19]
    rest_ref, scalars_ref, pot_ref = refs[19:22]
    held = refs[22:39]
    (
        prev_ref,
        orbit_ref,
        occ_ref,
        local_ref,
        xc_ref,
        lane_plus,
        lane_minus,
        a_plus,
        b_plus,
        b_minus,
        a_minus,
        cas_in,
        cas_out,
        cas_rows,
        cas_cols,
        beta_ref,
        energy_ref,
    ) = held
    (
        hot,
        acc,
        send1,
        recv1,
        fields,
        packed,
        xc_part,
        w_send,
        w_recv,
        d_all,
        h_all,
        h_send1,
        h_recv1,
        h_send2,
        h_recv2,
        send2,
        recv2,
        table,
        lifted,
        over_send,
        over_recv,
        corr,
        corr_recv,
        sum_send1,
        sum_recv1,
        sum_send2,
        sum_recv2,
        sems,
        load_sems,
    ) = refs[39:]
    me = lax.axis_index("space")
    group = lax.axis_index("band")
    start = me * PL

    def load(at):
        return pltpu.make_async_copy(later[at], held[at], load_sems.at[at])

    for at in range(len(later)):
        load(at).start()

    barrier = pltpu.get_barrier_semaphore()

    def greet(turn, carry):
        for step in range(7):
            peer = lax.rem(me + (turn * 7 + step + 1) * STRIDE, S)
            pl.semaphore_signal(barrier, inc=1, device_id={"space": peer}, device_id_type=MESH)
        return carry

    lax.fori_loop(0, (S - 1) // 7, greet, 0)
    for step in range(1, G):
        for low in range(LOW):
            peer = me // LOW * LOW + lax.rem(me + low, LOW)
            pl.semaphore_signal(
                barrier,
                inc=1,
                device_id={"band": lax.rem(group + step, G), "space": peer},
                device_id_type=MESH,
            )

    def space_send(phase, source, target):
        def one(turn, carry):
            for step in range(7):
                peer = lax.rem(me + (turn * 7 + step + 1) * STRIDE, S)
                pltpu.make_async_remote_copy(
                    src_ref=source(peer),
                    dst_ref=target(me),
                    send_sem=sems.at[phase, 0],
                    recv_sem=sems.at[phase, 1],
                    device_id={"space": peer},
                    device_id_type=MESH,
                ).start()
            return carry

        lax.fori_loop(0, (S - 1) // 7, one, 0)

    def band_send(phase, source, target):
        for step in (2, 1, 3):
            peer = lax.rem(group + step, G)
            pltpu.make_async_remote_copy(
                src_ref=source(peer),
                dst_ref=target(group),
                send_sem=sems.at[phase, 0],
                recv_sem=sems.at[phase, 1],
                device_id={"band": peer},
                device_id_type=MESH,
            ).start()

    def wait(phase, side, region):
        pltpu.make_async_copy(region, region, sems.at[phase, side]).wait()

    def part_chunk(ref, part):
        return lambda at: ref.at[pl.ds(part * S * CELL + at * CELL, CELL)]

    def chunk(ref):
        return lambda at: ref.at[pl.ds(at * HROWS, HROWS)]

    def keep(source, target, first, rows):
        own = pl.ds(first + me * rows, rows)
        target[own, :] = source[own, :]

    def cell_rows(part, m):
        return pl.ds(part * S * CELL + m, S, stride=CELL)

    def columns_at(step, size):
        return pl.ds(pl.multiple_of(step * size, size), size)

    def place(tile):
        def one(step, carry):
            columns = columns_at(step, PLACE)
            if tile == 0:
                row = (miller_ref[1:2, columns] - start) * N + miller_ref[0:1, columns]
                where = lax.broadcasted_iota(jnp.int16, (PL * N, PLACE), 0)
                hot[:, columns] = jnp.where(
                    where == row.astype(jnp.int16), BF16(1), BF16(0)
                )
            third = (miller_ref[2:3, columns] - tile * TILE).astype(jnp.int16)
            mask = lax.broadcasted_iota(jnp.int16, (TILE, PLACE), 0) == third
            parts = [jnp.where(mask, value, BF16(0)) for value in values_of(columns)]
            product = lax.dot_general(
                hot[:, columns],
                jnp.concatenate(parts, axis=0),
                (((1,), (1,)), ((), ())),
                preferred_element_type=F32,
            )
            acc[...] += product
            return carry

        acc[...] = jnp.zeros_like(acc)
        lax.fori_loop(0, WAVES // PLACE, one, 0, unroll=2)

    def values_of(columns):
        re_high, re_low = split(now_ref[0, 0:1, columns])
        im_high, im_low = split(now_ref[1, 0:1, columns])
        return re_high, im_high, re_low, im_low

    for t in range(3):
        place(t)
        placed = acc[:, 0:128] + acc[:, 128:256]
        if t == 0:
            load(7).wait()
        result = left_complex(
            a_plus, jnp.concatenate([placed[b * N : (b + 1) * N] for b in range(PL)], axis=1)
        )
        for r in range(PL):
            for b in range(PL):
                send1[cell_rows(t, r * PL + b), :] = result[
                    r * S : (r + 1) * S, b * 128 : (b + 1) * 128
                ]
        if t == 0:
            pl.semaphore_wait(barrier, S - 1 + (G - 1) * LOW)
        space_send(t, part_chunk(send1, t), part_chunk(recv1, t))
        keep(send1, recv1, t * S * CELL, CELL)

    for at in range(len(later)):
        if at != 7:
            load(at).wait()

    for r in range(PL):
        re = orbit_ref[0, 0, r]
        im = orbit_ref[1, 0, r]
        pieces = []
        for t in range(3):
            pieces += [re[:, t * TILE : (t + 1) * TILE], im[:, t * TILE : (t + 1) * TILE]]
        packed[r * N : (r + 1) * N] = jnp.concatenate(pieces, axis=1)

    every_chunk = pl.ds(0, (S - 1) * CELL)
    for t in range(3):
        wait(t, 1, recv1.at[every_chunk])
        values = jnp.concatenate(
            [
                jnp.concatenate([recv1[cell_rows(t, r * PL + b), :] for r in range(PL)], axis=1)
                for b in range(PL)
            ],
            axis=0,
        )
        result = left_complex(b_plus, values)
        result = jnp.concatenate([result[:, r * 128 : (r + 1) * 128] for r in range(PL)], axis=0)
        result = right(result, lane_plus[t])
        if t == 0:
            fields[...] = result
        else:
            fields[...] += result

    def tile_at(t):
        return pl.ds(t * 128, 128)

    tails = [[] for _ in range(G)]
    for r in range(PL):
        plane = pl.ds(r * N, N)
        values = left(cas_rows, right(2.0 * fields[plane, :] * packed[plane, :], cas_in[...]))
        for g in range(G):
            row = jnp.concatenate(
                [
                    values[b * S : (b + 1) * S, g * QUART : (g + 1) * QUART]
                    for b in range(PL)
                ],
                axis=1,
            )
            w_send[g, :, tile_at(r)] = row[:, :128]
            tails[g].append(row[:, 128:])
        if r == PL - 1:
            for g in range(G):
                w_send[g, :, tile_at(PL)] = jnp.concatenate(
                    tails[g] + [jnp.zeros((S, HL - PL * THIRD), F32)], axis=1
                )
        for t in (r,) if r < PL - 1 else (r, PL):
            band_send(
                W_PHASE[t],
                lambda peer: w_send.at[peer, :, tile_at(t)],
                lambda mine: w_recv.at[mine, :, tile_at(t)],
            )

    w_recv[group] = w_send[group]
    totals = []
    for t in range(4):
        wait(W_PHASE[t], 1, w_recv.at[pl.ds(0, G - 1), :, tile_at(t)])
        parts = [w_recv[g, :, tile_at(t)] for g in range(G)]
        totals.append(parts[0] + parts[1] + parts[2] + parts[3])
        h_send1[pl.ds(t, S, stride=HROWS), :] = totals[t]
    total = jnp.concatenate(totals, axis=1)
    space_send(4, chunk(h_send1), chunk(h_recv1))
    d_all[group] = total
    band_send(5, lambda peer: d_all.at[group], lambda mine: d_all.at[mine])
    keep(h_send1, h_recv1, 0, HROWS)

    lane = lax.broadcasted_iota(jnp.int32, (N, PL * QUART), 1)
    first = signed(lax.broadcasted_iota(jnp.int32, (N, PL * QUART), 0))
    plane = jnp.where(lane >= QUART, 1, 0) + jnp.where(lane >= 2 * QUART, 1, 0)
    second = signed(plane + start)
    third = signed(lane - plane * QUART + group * QUART)
    squared = first * first + second * second + third * third
    coulomb = jnp.where(squared > 0, HARTREE / jnp.maximum(squared, 1).astype(F32), 0.0)

    wait(4, 1, h_recv1.at[pl.ds(0, (S - 1) * HROWS)])
    pieces = [h_recv1[pl.ds(t, S, stride=HROWS), :] for t in range(4)]
    tall = jnp.concatenate(
        [
            jnp.concatenate([pieces[r], pieces[PL][:, r * 16 : (r + 1) * 16]], axis=1)
            for r in range(PL)
        ],
        axis=0,
    )
    tall = left(cas_rows, coulomb * left(cas_cols, tall))
    for r in range(PL):
        h_send2[pl.ds(r, S, stride=HROWS), :] = tall[r * S : (r + 1) * S, :128]
    h_send2[pl.ds(PL, S, stride=HROWS), :] = jnp.concatenate(
        [tall[r * S : (r + 1) * S, 128:] for r in range(PL)]
        + [jnp.zeros((S, HL - PL * THIRD), F32)],
        axis=1,
    )
    space_send(6, chunk(h_send2), chunk(h_recv2))
    keep(h_send2, h_recv2, 0, HROWS)

    def grid_values(ref, r):
        rows = [
            jnp.concatenate(
                [ref[g, :, tile_at(r)], ref[g, :, tile_at(PL)][:, r * 16 : (r + 1) * 16]], axis=1
            )
            for g in range(G)
        ]
        values = jnp.concatenate(
            [
                jnp.concatenate([row[:, b * QUART : (b + 1) * QUART] for row in rows], axis=1)
                for b in range(PL)
            ],
            axis=0,
        )
        return right(left(cas_cols, values), cas_out[...])

    wait(5, 0, d_all.at[pl.ds(0, G - 1)])
    wait(5, 1, d_all.at[pl.ds(0, G - 1)])
    for r in range(PL):
        plane = pl.ds(r * N, N)
        known = grid_values(d_all, r) * doubled(xc_ref[r])
        fields[plane, :] = doubled(local_ref[r]) * fields[plane, :] + known * packed[plane, :]
        xc_part[plane, :] = known

    wait(6, 1, h_recv2.at[pl.ds(0, (S - 1) * HROWS)])
    for t in (PL, 0, 1, 2):
        h_all[group, :, tile_at(t)] = h_recv2[pl.ds(t, S, stride=HROWS), :]
        band_send(
            H_PHASE[t],
            lambda peer: h_all.at[group, :, tile_at(t)],
            lambda mine: h_all.at[mine, :, tile_at(t)],
        )
    mixed = []
    for r in range(PL):
        plane = pl.ds(r * N, N)
        for t in (PL, 0) if r == 0 else (r,):
            wait(H_PHASE[t], 0, h_all.at[pl.ds(0, G - 1), :, tile_at(t)])
            wait(H_PHASE[t], 1, h_all.at[pl.ds(0, G - 1), :, tile_at(t)])
        hartree = grid_values(h_all, r)
        mixed.append(right(fields[plane, :] + hartree * packed[plane, :], lane_minus[...]))
        xc_part[plane, :] += hartree
    result = left_complex(b_minus, jnp.concatenate(mixed, axis=1))
    for b in range(PL):
        for r in range(PL):
            for t in range(3):
                send2[cell_rows(b, r * PL + t), :] = result[
                    b * S : (b + 1) * S, (r * 3 + t) * 128 : (r * 3 + t + 1) * 128
                ]
        space_send(8 + b, part_chunk(send2, b), part_chunk(recv2, b))
        keep(send2, recv2, b * S * CELL, CELL)
    potential = xc_part[...]
    for r in range(PL):
        pot_ref[r] = jnp.concatenate(
            [potential[r * N : (r + 1) * N, t * 128 : t * 128 + TILE] for t in range(3)], axis=1
        )

    energy = energy_ref[0:1].reshape(1, 1)

    def read_waves(first, last, columns):
        seen = hot[first * N : last * N, columns]
        found = jnp.dot(
            table[:, 0 : 2 * (last - first) * N],
            jnp.concatenate([seen, seen], axis=0),
            preferred_element_type=F32,
        )
        mask = lax.broadcasted_iota(jnp.int32, (N, READ), 0) == miller_ref[2:3, columns]
        sums = []
        for half in range(2):
            total = None
            for t in range(3):
                at = t * 128 + half * TILE
                kept = jnp.where(
                    mask[t * TILE : (t + 1) * TILE],
                    found[at : at + TILE],
                    0.0,
                )
                total = kept if total is None else total + kept
            sums.append(jnp.sum(total, axis=0, keepdims=True))
        if first > 0:
            sums = [sums[half] + lifted[group, half : half + 1, columns] for half in range(2)]
        if last == PL:
            index = [signed(miller_ref[d : d + 1, columns]) for d in range(3)]
            squared = index[0] * index[0] + index[1] * index[1] + index[2] * index[2]
            diagonal = KINETIC * squared.astype(F32) / float(N * N) - energy
            sums = [sums[half] + diagonal * now_ref[half, 0:1, columns] for half in range(2)]
        for half in range(2):
            lifted[group, half : half + 1, columns] = sums[half]

    blocks = WAVES // BLOCK
    per_block = BLOCK // READ

    def block(ref, at, n):
        return ref.at[at, :, pl.ds(n * BLOCK, BLOCK)]

    for first, last in PASSES:
        highs, lows = [], []
        for b in range(first, last):
            wait(8 + b, 1, recv2.at[every_chunk])
            values = jnp.concatenate(
                [
                    jnp.concatenate([recv2[cell_rows(b, r * PL + t), :] for t in range(3)], axis=1)
                    for r in range(PL)
                ],
                axis=0,
            )
            result = left_complex(a_minus, values)
            high = result.astype(BF16).astype(F32)
            highs.append(high)
            lows.append(result - high)
        table[:, 0 : 2 * (last - first) * N] = jnp.transpose(
            jnp.concatenate(highs + lows, axis=0)
        ).astype(BF16)

        def one(step, carry):
            read_waves(first, last, columns_at(step, READ))
            return carry

        for n in range(blocks):
            lax.fori_loop(n * per_block, (n + 1) * per_block, one, 0, unroll=2)
            if last == PL:
                band_send(
                    11 + n,
                    lambda peer: block(lifted, group, n),
                    lambda mine: block(lifted, mine, n),
                )

    def columns_of_tile(step):
        return pl.ds(pl.multiple_of(step * 128, 128), 128)

    def overlap(step, sums):
        columns = columns_of_tile(step)
        occ_re = occ_ref[0, :, columns]
        occ_im = occ_ref[1, :, columns]
        out = []
        for v in range(G):
            re = lifted[v, 0:1, columns]
            im = lifted[v, 1:2, columns]
            out.append(sums[2 * v] + (occ_re * re + occ_im * im))
            out.append(sums[2 * v + 1] + (occ_re * im - occ_im * re))
        return tuple(out)

    def three(ref, n):
        return ref.at[pl.ds(0, G - 1), :, pl.ds(n * BLOCK, BLOCK)]

    tiles = BLOCK // 128
    sums = tuple(jnp.zeros((16, 128), F32) for _ in range(2 * G))
    for n in range(blocks):
        wait(11 + n, 0, three(lifted, n))
        wait(11 + n, 1, three(lifted, n))
        sums = lax.fori_loop(n * tiles, (n + 1) * tiles, overlap, sums, unroll=4)
    lane = lax.broadcasted_iota(jnp.int32, (16, 128), 1)
    band_of = lane // 16
    own_row = (lane % 16) == lax.broadcasted_iota(jnp.int32, (16, 128), 0)
    matrix = jnp.zeros((16, 128), F32)
    for row in range(2 * G):
        column = jnp.sum(sums[row], axis=1, keepdims=True)
        matrix = jnp.where(band_of == row, column, matrix)
    over_send[0] = jnp.sum(jnp.where(own_row, matrix, 0.0), axis=0, keepdims=True)
    space_send(15, lambda peer: over_send.at[0], lambda mine: over_recv.at[mine])
    over_recv[me] = over_send[0]
    wait(15, 1, over_recv.at[pl.ds(0, S - 1)])
    row_sum = jnp.sum(over_recv[...], axis=0)
    spread = jnp.where(own_row, jnp.broadcast_to(row_sum, (16, 128)), 0.0)
    weights = []
    for row in range(2 * G):
        column = jnp.sum(jnp.where(band_of == row, spread, 0.0), axis=1, keepdims=True)
        weights.append(jnp.broadcast_to(column, (16, 128)))

    def correct(step, carry):
        columns = columns_of_tile(step)
        occ_re = occ_ref[0, :, columns]
        occ_im = occ_ref[1, :, columns]
        for v in range(G):
            w_re, w_im = weights[2 * v], weights[2 * v + 1]
            corr[v, 0:1, columns] = jnp.sum(occ_re * w_re - occ_im * w_im, axis=0, keepdims=True)
            corr[v, 1:2, columns] = jnp.sum(occ_re * w_im + occ_im * w_re, axis=0, keepdims=True)
        return carry

    for n in range(blocks):
        lax.fori_loop(n * tiles, (n + 1) * tiles, correct, 0, unroll=4)
        band_send(
            16 + n, lambda peer: block(corr, peer, n), lambda mine: block(corr_recv, mine, n)
        )

    corr_recv[group] = corr[group]
    beta_old = beta_ref[0:1].reshape(1, 1)
    partial = [jnp.zeros((1, 1), F32) for _ in range(4)]
    for n in range(blocks):
        wait(16 + n, 1, three(corr_recv, n))
        columns = pl.ds(n * BLOCK, BLOCK)
        for part in range(2):
            removed = (
                corr_recv[0, part : part + 1, columns]
                + corr_recv[1, part : part + 1, columns]
                + corr_recv[2, part : part + 1, columns]
                + corr_recv[3, part : part + 1, columns]
            )
            q = now_ref[part, 0:1, columns]
            p = prev_ref[part, 0:1, columns]
            u = lifted[group, part : part + 1, columns] - removed - beta_old * p
            rest_ref[part, 0:1, columns] = u
            for slot, product in enumerate((u * u, q * u, q * p, q * q)):
                partial[slot] = partial[slot] + jnp.sum(product, axis=1, keepdims=True)
    lane = lax.broadcasted_iota(jnp.int32, (1, 128), 1)
    row = jnp.zeros((1, 128), F32)
    for slot in range(4):
        row = jnp.where(lane == slot, partial[slot], row)
    sum_send1[0] = row
    here_low = lax.rem(me, LOW)
    here_high = me // LOW
    for step in range(1, G * LOW):
        peer_band = lax.rem(group + step // LOW, G)
        peer_low = lax.rem(here_low + step % LOW, LOW)
        pltpu.make_async_remote_copy(
            src_ref=sum_send1.at[0],
            dst_ref=sum_recv1.at[group * LOW + here_low],
            send_sem=sems.at[20, 0],
            recv_sem=sems.at[20, 1],
            device_id={"band": peer_band, "space": here_high * LOW + peer_low},
            device_id_type=MESH,
        ).start()
    sum_recv1[group * LOW + here_low] = sum_send1[0]
    wait(20, 1, sum_recv1.at[pl.ds(0, G * LOW - 1)])
    sum_send2[0] = jnp.sum(sum_recv1[...], axis=0)
    for step in range(1, HIGH):
        peer_high = lax.rem(here_high + step, HIGH)
        pltpu.make_async_remote_copy(
            src_ref=sum_send2.at[0],
            dst_ref=sum_recv2.at[here_high],
            send_sem=sems.at[21, 0],
            recv_sem=sems.at[21, 1],
            device_id={"space": peer_high * LOW + here_low},
            device_id_type=MESH,
        ).start()
    sum_recv2[here_high] = sum_send2[0]

    for part in range(3):
        wait(part, 0, send1.at[every_chunk])
        wait(8 + part, 0, send2.at[every_chunk])
    for t in range(4):
        wait(W_PHASE[t], 0, w_send.at[pl.ds(0, G - 1), :, tile_at(t)])
    wait(4, 0, h_send1.at[pl.ds(0, (S - 1) * HROWS)])
    wait(6, 0, h_send2.at[pl.ds(0, (S - 1) * HROWS)])
    wait(15, 0, over_recv.at[pl.ds(0, S - 1)])
    for n in range(blocks):
        wait(16 + n, 0, three(corr, n))
    wait(20, 0, sum_recv1.at[pl.ds(0, G * LOW - 1)])

    wait(21, 0, sum_recv2.at[pl.ds(0, HIGH - 1)])
    wait(21, 1, sum_recv2.at[pl.ds(0, HIGH - 1)])
    row = jnp.sum(sum_recv2[...], axis=0)

    def pick(slot):
        return jnp.sum(jnp.where(lane == slot, row, 0.0), axis=1, keepdims=True)

    norm_u, q_u, q_p, norm_q = [pick(slot) for slot in range(4)]
    alpha = (q_u + beta_old * q_p) / ENTRIES
    square = norm_u - 2.0 * alpha * q_u + alpha * alpha * norm_q
    beta_new = jnp.sqrt(square / ENTRIES)
    scalars_ref[...] = jnp.where(lane == 0, alpha, beta_new)


def finish(rest_ref, now_ref, scalars_ref, pot_in, next_ref, coef_ref, pot_ref):
    alpha = scalars_ref[0:1, 0:1]
    beta_new = scalars_ref[0:1, 1:2]
    inverse = 1.0 / beta_new
    for part in range(2):
        next_ref[part] = (rest_ref[part] - alpha * now_ref[part]) * inverse
    coef_ref[...] = scalars_ref[0:1, 0:2]
    pot_ref[...] = pot_in[...]


def per_device(
    lanczos_now,
    lanczos_prev,
    beta_prev,
    orbitals,
    band_energy,
    occupied,
    local_pot,
    xc_kernel,
    miller,
):
    later = [lanczos_prev, orbitals, occupied, local_pot, xc_kernel]
    later += [jnp.asarray(table) for table in make_tables()]
    later += [beta_prev, band_energy]
    vmem = pl.BlockSpec(memory_space=pltpu.VMEM)
    in_hbm = pl.BlockSpec(memory_space=pltpu.HBM)
    wide = pltpu.VMEM((3 * S * CELL, 128), F32)
    narrow = pltpu.VMEM((S * HROWS, 128), F32)
    quarter = pltpu.VMEM((G, S, HL), F32)
    band_waves = pltpu.VMEM((G, 2, WAVES), F32)
    real_grid = jax.ShapeDtypeStruct((PL, N, N), F32)
    waves = jax.ShapeDtypeStruct((2, 1, WAVES), F32)
    rest, scalars, potential = pl.pallas_call(
        body,
        out_shape=(waves, jax.ShapeDtypeStruct((1, 128), F32), real_grid),
        in_specs=[vmem, vmem] + [in_hbm] * len(later),
        out_specs=(vmem, vmem, vmem),
        scratch_shapes=[pltpu.VMEM(array.shape, array.dtype) for array in later]
        + [
            pltpu.VMEM((PL * N, WAVES), BF16),
            pltpu.VMEM((PL * N, 256), F32),
            wide,
            wide,
            pltpu.VMEM((PL * N, 384), F32),
            pltpu.VMEM((PL * N, 384), F32),
            pltpu.VMEM((PL * N, 384), F32),
            quarter,
            quarter,
            quarter,
            quarter,
            narrow,
            narrow,
            narrow,
            narrow,
            wide,
            wide,
            pltpu.VMEM((384, 4 * N), BF16),
            band_waves,
            pltpu.VMEM((1, 1, 128), F32),
            pltpu.VMEM((S, 1, 128), F32),
            band_waves,
            band_waves,
            pltpu.VMEM((1, 1, 128), F32),
            pltpu.VMEM((G * LOW, 1, 128), F32),
            pltpu.VMEM((1, 1, 128), F32),
            pltpu.VMEM((HIGH, 1, 128), F32),
            pltpu.SemaphoreType.DMA((28, 2)),
            pltpu.SemaphoreType.DMA((len(later),)),
        ],
        compiler_params=pltpu.CompilerParams(
            collective_id=0, has_side_effects=True, vmem_limit_bytes=60 * 1024 * 1024
        ),
    )(lanczos_now, miller, *later)
    return pl.pallas_call(
        finish,
        out_shape=(waves, jax.ShapeDtypeStruct((1, 2), F32), real_grid),
        in_specs=[vmem] * 4,
        out_specs=(vmem,) * 3,
    )(rest, lanczos_now, scalars, potential)


def solution(mesh):
    return jax.shard_map(
        per_device,
        mesh=mesh,
        in_specs=(
            P(None, "band", "space"),
            P(None, "band", "space"),
            P(),
            P(None, "band", "space", None, None),
            P("band"),
            P(None, "band", "space"),
            P("space", None, None),
            P("space", None, None),
            P(None, "space"),
        ),
        out_specs=(P(None, "band", "space"), P(), P("space", None, None)),
        check_vma=False,
    )
```

```python
import math

import jax
import jax.numpy as jnp
import ml_dtypes
import numpy as np
from jax import lax
from jax.experimental import pallas as pl
from jax.experimental.pallas import tpu as pltpu
from jax.sharding import PartitionSpec as P

MESH = pl.DeviceIdType.MESH
F32 = jnp.float32
BF16 = jnp.bfloat16
KINETIC = 8.0
HARTREE = 4.0
N = 192
S = 64
G = 4
PL = 3
CELL = 9
HROWS = 4
QUART = N // G
THIRD = PL * QUART
HL = 512
LOW = 4
HIGH = S // LOW
TILE = 64
WAVES = 16384
PLACE = 2048
READ = 1024
HALF = N // 2
BLOCK = 4096
W_PHASE = (3, 22, 23, 24)
H_PHASE = (7, 25, 26, 27)
STRIDE = 29
ENTRIES = float(2 * G * WAVES * S)


def split_np(table):
    high = table.astype(np.float32).astype(ml_dtypes.bfloat16)
    low = (table - high.astype(np.float64)).astype(np.float32).astype(ml_dtypes.bfloat16)
    return high, low


def left_table(table):
    high, low = split_np(table)
    return np.concatenate([high, low], axis=0)


def right_table(table):
    high, low = split_np(table)
    return np.concatenate([high, high, low], axis=0)


def make_tables():
    index = np.arange(N)
    angle = 2.0 * np.pi * (np.outer(index, index) % N) / N
    cosine = np.cos(angle) / math.sqrt(N)
    sine = np.sin(angle) / math.sqrt(N)
    order = np.concatenate([np.arange(S) * PL + part for part in range(PL)])
    re_lane = index // TILE * 128 + index % TILE
    im_lane = re_lane + TILE

    def lanes(sign):
        table = np.zeros((2 * N, 2 * N))
        table[np.ix_(re_lane, re_lane)] = cosine
        table[np.ix_(im_lane, re_lane)] = -sign * sine
        table[np.ix_(re_lane, im_lane)] = sign * sine
        table[np.ix_(im_lane, im_lane)] = cosine
        return table

    def rows(sign, row_order, column_order):
        both = [
            cosine[row_order][:, column_order],
            sign * sine[row_order][:, column_order],
        ]
        return left_table(np.concatenate(both, axis=0))

    cas = cosine + sine
    cas_in = np.zeros((2 * N, N))
    cas_in[re_lane] = cas
    cas_in[im_lane] = cas
    plus = lanes(1.0)
    return (
        np.stack([right_table(plus[t * 128 : (t + 1) * 128]) for t in range(3)]),
        right_table(lanes(-1.0)),
        rows(1.0, order, index),
        rows(1.0, index, order),
        rows(-1.0, order, index),
        rows(-1.0, index, order),
        right_table(cas_in),
        right_table(cas_in.T),
        left_table(cas[order]),
        left_table(cas[:, order]),
    )


def split(values):
    high = values.astype(BF16)
    low = (values - high.astype(F32)).astype(BF16)
    return high, low


def left(table_ref, values):
    high, low = split(values)
    rows = table_ref.shape[0] // 2
    by_high = jnp.dot(table_ref[...], high, preferred_element_type=F32)
    by_low = jnp.dot(table_ref[0:rows], low, preferred_element_type=F32)
    return by_high[0:rows] + (by_high[rows:] + by_low)


def right(values, table):
    high, low = split(values)
    stacked = jnp.concatenate([high, low, high], axis=1)
    return jnp.dot(stacked, table, preferred_element_type=F32)


def times_i(values):
    lane = lax.broadcasted_iota(jnp.int32, (values.shape[0], 128), 1)
    tiles = []
    for t in range(values.shape[1] // 128):
        turned = pltpu.roll(values[:, t * 128 : (t + 1) * 128], TILE, axis=1)
        tiles.append(jnp.where(lane < TILE, -turned, turned))
    return jnp.concatenate(tiles, axis=1)


def left_complex(table_ref, values):
    both = left(table_ref, values)
    return both[0:N] + times_i(both[N:])


def signed(indices):
    return jnp.where(indices < N // 2, indices, indices - N)


def doubled(values):
    tiles = []
    for t in range(3):
        part = values[:, t * TILE : (t + 1) * TILE]
        tiles += [part, part]
    return jnp.concatenate(tiles, axis=1)


def body(*refs):
    now_ref, miller_ref = refs[:2]
    later = refs[2:19]
    rest_ref, scalars_ref, pot_ref = refs[19:22]
    held = refs[22:39]
    (
        prev_ref,
        orbit_ref,
        occ_ref,
        local_ref,
        xc_ref,
        lane_plus,
        lane_minus,
        a_plus,
        b_plus,
        b_minus,
        a_minus,
        cas_in,
        cas_out,
        cas_rows,
        cas_cols,
        beta_ref,
        energy_ref,
    ) = held
    (
        hot,
        acc,
        send1,
        recv1,
        fields,
        packed,
        xc_part,
        w_send,
        w_recv,
        d_all,
        h_all,
        h_send1,
        h_recv1,
        h_send2,
        h_recv2,
        send2,
        recv2,
        table,
        lifted,
        over_send,
        over_recv,
        corr,
        corr_recv,
        sum_send1,
        sum_recv1,
        sum_send2,
        sum_recv2,
        sems,
        load_sems,
    ) = refs[39:]
    me = lax.axis_index("space")
    group = lax.axis_index("band")
    start = me * PL

    def load(at):
        return pltpu.make_async_copy(later[at], held[at], load_sems.at[at])

    for at in range(len(later)):
        load(at).start()

    barrier = pltpu.get_barrier_semaphore()

    def greet(turn, carry):
        for step in range(7):
            peer = lax.rem(me + (turn * 7 + step + 1) * STRIDE, S)
            pl.semaphore_signal(barrier, inc=1, device_id={"space": peer}, device_id_type=MESH)
        return carry

    lax.fori_loop(0, (S - 1) // 7, greet, 0)
    for step in range(1, G):
        for low in range(LOW):
            peer = me // LOW * LOW + lax.rem(me + low, LOW)
            pl.semaphore_signal(
                barrier,
                inc=1,
                device_id={"band": lax.rem(group + step, G), "space": peer},
                device_id_type=MESH,
            )

    def space_send(phase, source, target):
        def one(turn, carry):
            for step in range(7):
                peer = lax.rem(me + (turn * 7 + step + 1) * STRIDE, S)
                pltpu.make_async_remote_copy(
                    src_ref=source(peer),
                    dst_ref=target(me),
                    send_sem=sems.at[phase, 0],
                    recv_sem=sems.at[phase, 1],
                    device_id={"space": peer},
                    device_id_type=MESH,
                ).start()
            return carry

        lax.fori_loop(0, (S - 1) // 7, one, 0)

    def band_send(phase, source, target):
        for step in (2, 1, 3):
            peer = lax.rem(group + step, G)
            pltpu.make_async_remote_copy(
                src_ref=source(peer),
                dst_ref=target(group),
                send_sem=sems.at[phase, 0],
                recv_sem=sems.at[phase, 1],
                device_id={"band": peer},
                device_id_type=MESH,
            ).start()

    def wait(phase, side, region):
        pltpu.make_async_copy(region, region, sems.at[phase, side]).wait()

    def part_chunk(ref, part):
        return lambda at: ref.at[pl.ds(part * S * CELL + at * CELL, CELL)]

    def chunk(ref):
        return lambda at: ref.at[pl.ds(at * HROWS, HROWS)]

    def keep(source, target, first, rows):
        own = pl.ds(first + me * rows, rows)
        target[own, :] = source[own, :]

    def cell_rows(part, m):
        return pl.ds(part * S * CELL + m, S, stride=CELL)

    def columns_at(step, size):
        return pl.ds(pl.multiple_of(step * size, size), size)

    def place(tile):
        def one(step, carry):
            columns = columns_at(step, PLACE)
            if tile == 0:
                row = (miller_ref[1:2, columns] - start) * N + miller_ref[0:1, columns]
                where = lax.broadcasted_iota(jnp.int16, (PL * N, PLACE), 0)
                hot[:, columns] = jnp.where(
                    where == row.astype(jnp.int16), BF16(1), BF16(0)
                )
            third = (miller_ref[2:3, columns] - tile * TILE).astype(jnp.int16)
            mask = lax.broadcasted_iota(jnp.int16, (TILE, PLACE), 0) == third
            parts = [jnp.where(mask, value, BF16(0)) for value in values_of(columns)]
            product = lax.dot_general(
                hot[:, columns],
                jnp.concatenate(parts, axis=0),
                (((1,), (1,)), ((), ())),
                preferred_element_type=F32,
            )
            acc[...] += product
            return carry

        acc[...] = jnp.zeros_like(acc)
        lax.fori_loop(0, WAVES // PLACE, one, 0, unroll=2)

    def values_of(columns):
        re_high, re_low = split(now_ref[0, 0:1, columns])
        im_high, im_low = split(now_ref[1, 0:1, columns])
        return re_high, im_high, re_low, im_low

    for t in range(3):
        place(t)
        placed = acc[:, 0:128] + acc[:, 128:256]
        if t == 0:
            load(7).wait()
        result = left_complex(
            a_plus, jnp.concatenate([placed[b * N : (b + 1) * N] for b in range(PL)], axis=1)
        )
        for r in range(PL):
            for b in range(PL):
                send1[cell_rows(t, r * PL + b), :] = result[
                    r * S : (r + 1) * S, b * 128 : (b + 1) * 128
                ]
        if t == 0:
            pl.semaphore_wait(barrier, S - 1 + (G - 1) * LOW)
        space_send(t, part_chunk(send1, t), part_chunk(recv1, t))
        keep(send1, recv1, t * S * CELL, CELL)

    for at in range(len(later)):
        if at != 7:
            load(at).wait()

    for r in range(PL):
        re = orbit_ref[0, 0, r]
        im = orbit_ref[1, 0, r]
        pieces = []
        for t in range(3):
            pieces += [re[:, t * TILE : (t + 1) * TILE], im[:, t * TILE : (t + 1) * TILE]]
        packed[r * N : (r + 1) * N] = jnp.concatenate(pieces, axis=1)

    every_chunk = pl.ds(0, (S - 1) * CELL)
    for t in range(3):
        wait(t, 1, recv1.at[every_chunk])
        values = jnp.concatenate(
            [
                jnp.concatenate([recv1[cell_rows(t, r * PL + b), :] for r in range(PL)], axis=1)
                for b in range(PL)
            ],
            axis=0,
        )
        result = left_complex(b_plus, values)
        result = jnp.concatenate([result[:, r * 128 : (r + 1) * 128] for r in range(PL)], axis=0)
        result = right(result, lane_plus[t])
        if t == 0:
            fields[...] = result
        else:
            fields[...] += result

    def tile_at(t):
        return pl.ds(t * 128, 128)

    tails = [[] for _ in range(G)]
    for r in range(PL):
        plane = pl.ds(r * N, N)
        values = left(cas_rows, right(2.0 * fields[plane, :] * packed[plane, :], cas_in[...]))
        for g in range(G):
            row = jnp.concatenate(
                [
                    values[b * S : (b + 1) * S, g * QUART : (g + 1) * QUART]
                    for b in range(PL)
                ],
                axis=1,
            )
            w_send[g, :, tile_at(r)] = row[:, :128]
            tails[g].append(row[:, 128:])
        if r == PL - 1:
            for g in range(G):
                w_send[g, :, tile_at(PL)] = jnp.concatenate(
                    tails[g] + [jnp.zeros((S, HL - PL * THIRD), F32)], axis=1
                )
        for t in (r,) if r < PL - 1 else (r, PL):
            band_send(
                W_PHASE[t],
                lambda peer: w_send.at[peer, :, tile_at(t)],
                lambda mine: w_recv.at[mine, :, tile_at(t)],
            )

    w_recv[group] = w_send[group]
    totals = []
    for t in range(4):
        wait(W_PHASE[t], 1, w_recv.at[pl.ds(0, G - 1), :, tile_at(t)])
        parts = [w_recv[g, :, tile_at(t)] for g in range(G)]
        totals.append(parts[0] + parts[1] + parts[2] + parts[3])
        h_send1[pl.ds(t, S, stride=HROWS), :] = totals[t]
    total = jnp.concatenate(totals, axis=1)
    space_send(4, chunk(h_send1), chunk(h_recv1))
    d_all[group] = total
    band_send(5, lambda peer: d_all.at[group], lambda mine: d_all.at[mine])
    keep(h_send1, h_recv1, 0, HROWS)

    lane = lax.broadcasted_iota(jnp.int32, (N, PL * QUART), 1)
    first = signed(lax.broadcasted_iota(jnp.int32, (N, PL * QUART), 0))
    plane = jnp.where(lane >= QUART, 1, 0) + jnp.where(lane >= 2 * QUART, 1, 0)
    second = signed(plane + start)
    third = signed(lane - plane * QUART + group * QUART)
    squared = first * first + second * second + third * third
    coulomb = jnp.where(squared > 0, HARTREE / jnp.maximum(squared, 1).astype(F32), 0.0)

    wait(4, 1, h_recv1.at[pl.ds(0, (S - 1) * HROWS)])
    pieces = [h_recv1[pl.ds(t, S, stride=HROWS), :] for t in range(4)]
    tall = jnp.concatenate(
        [
            jnp.concatenate([pieces[r], pieces[PL][:, r * 16 : (r + 1) * 16]], axis=1)
            for r in range(PL)
        ],
        axis=0,
    )
    tall = left(cas_rows, coulomb * left(cas_cols, tall))
    for r in range(PL):
        h_send2[pl.ds(r, S, stride=HROWS), :] = tall[r * S : (r + 1) * S, :128]
    h_send2[pl.ds(PL, S, stride=HROWS), :] = jnp.concatenate(
        [tall[r * S : (r + 1) * S, 128:] for r in range(PL)]
        + [jnp.zeros((S, HL - PL * THIRD), F32)],
        axis=1,
    )
    space_send(6, chunk(h_send2), chunk(h_recv2))
    keep(h_send2, h_recv2, 0, HROWS)

    def grid_values(ref, r):
        rows = [
            jnp.concatenate(
                [ref[g, :, tile_at(r)], ref[g, :, tile_at(PL)][:, r * 16 : (r + 1) * 16]], axis=1
            )
            for g in range(G)
        ]
        values = jnp.concatenate(
            [
                jnp.concatenate([row[:, b * QUART : (b + 1) * QUART] for row in rows], axis=1)
                for b in range(PL)
            ],
            axis=0,
        )
        return right(left(cas_cols, values), cas_out[...])

    wait(5, 0, d_all.at[pl.ds(0, G - 1)])
    wait(5, 1, d_all.at[pl.ds(0, G - 1)])
    for r in range(PL):
        plane = pl.ds(r * N, N)
        known = grid_values(d_all, r) * doubled(xc_ref[r])
        fields[plane, :] = doubled(local_ref[r]) * fields[plane, :] + known * packed[plane, :]
        xc_part[plane, :] = known

    wait(6, 1, h_recv2.at[pl.ds(0, (S - 1) * HROWS)])
    for t in (PL, 0, 1, 2):
        h_all[group, :, tile_at(t)] = h_recv2[pl.ds(t, S, stride=HROWS), :]
        band_send(
            H_PHASE[t],
            lambda peer: h_all.at[group, :, tile_at(t)],
            lambda mine: h_all.at[mine, :, tile_at(t)],
        )
    mixed = []
    for r in range(PL):
        plane = pl.ds(r * N, N)
        for t in (PL, 0) if r == 0 else (r,):
            wait(H_PHASE[t], 0, h_all.at[pl.ds(0, G - 1), :, tile_at(t)])
            wait(H_PHASE[t], 1, h_all.at[pl.ds(0, G - 1), :, tile_at(t)])
        hartree = grid_values(h_all, r)
        mixed.append(right(fields[plane, :] + hartree * packed[plane, :], lane_minus[...]))
        xc_part[plane, :] += hartree
    result = left_complex(b_minus, jnp.concatenate(mixed, axis=1))
    for b in range(PL):
        for r in range(PL):
            for t in range(3):
                send2[cell_rows(b, r * PL + t), :] = result[
                    b * S : (b + 1) * S, (r * 3 + t) * 128 : (r * 3 + t + 1) * 128
                ]
        space_send(8 + b, part_chunk(send2, b), part_chunk(recv2, b))
        keep(send2, recv2, b * S * CELL, CELL)
    potential = xc_part[...]
    for r in range(PL):
        pot_ref[r] = jnp.concatenate(
            [potential[r * N : (r + 1) * N, t * 128 : t * 128 + TILE] for t in range(3)], axis=1
        )

    energy = energy_ref[0:1].reshape(1, 1)

    def read_waves(b, columns):
        seen = hot[b * N : (b + 1) * N, columns]
        third = miller_ref[2:3, columns]
        upper = third >= HALF
        upper_bit = jnp.where(upper, 1.0, 0.0).astype(BF16)
        high_part = seen * upper_bit
        low_part = seen - high_part
        found = jnp.dot(
            table[...],
            jnp.concatenate([low_part, low_part, high_part, high_part], axis=0),
            preferred_element_type=F32,
        )
        mask = lax.broadcasted_iota(jnp.int32, (HALF, READ), 0) == jnp.where(
            upper, third - HALF, third
        )
        sums = [
            jnp.sum(
                jnp.where(mask, found[half * HALF : (half + 1) * HALF], 0.0),
                axis=0,
                keepdims=True,
            )
            for half in range(2)
        ]
        if b > 0:
            sums = [sums[half] + lifted[group, half : half + 1, columns] for half in range(2)]
        if b == PL - 1:
            index = [signed(miller_ref[d : d + 1, columns]) for d in range(3)]
            squared = index[0] * index[0] + index[1] * index[1] + index[2] * index[2]
            diagonal = KINETIC * squared.astype(F32) / float(N * N) - energy
            sums = [sums[half] + diagonal * now_ref[half, 0:1, columns] for half in range(2)]
        for half in range(2):
            lifted[group, half : half + 1, columns] = sums[half]

    blocks = WAVES // BLOCK
    per_block = BLOCK // READ

    def block(ref, at, n):
        return ref.at[at, :, pl.ds(n * BLOCK, BLOCK)]

    for b in range(PL):
        wait(8 + b, 1, recv2.at[every_chunk])
        values = jnp.concatenate(
            [
                jnp.concatenate([recv2[cell_rows(b, r * PL + t), :] for t in range(3)], axis=1)
                for r in range(PL)
            ],
            axis=0,
        )
        turned = jnp.transpose(left_complex(a_minus, values))
        pieces = []
        for side in range(2):
            rows = []
            for half in range(2):
                whole = jnp.concatenate(
                    [
                        turned[t * 128 + half * TILE : t * 128 + (half + 1) * TILE]
                        for t in range(3)
                    ],
                    axis=0,
                )
                rows.append(whole[side * HALF : (side + 1) * HALF])
            rows = jnp.concatenate(rows, axis=0)
            high = rows.astype(BF16).astype(F32)
            pieces += [high, rows - high]
        table[...] = jnp.concatenate(pieces, axis=1).astype(BF16)

        def one(step, carry):
            read_waves(b, columns_at(step, READ))
            return carry

        for n in range(blocks):
            lax.fori_loop(n * per_block, (n + 1) * per_block, one, 0, unroll=2)
            if b == PL - 1:
                band_send(
                    11 + n,
                    lambda peer: block(lifted, group, n),
                    lambda mine: block(lifted, mine, n),
                )

    def columns_of_tile(step):
        return pl.ds(pl.multiple_of(step * 128, 128), 128)

    def overlap(step, sums):
        columns = columns_of_tile(step)
        occ_re = occ_ref[0, :, columns]
        occ_im = occ_ref[1, :, columns]
        out = []
        for v in range(G):
            re = lifted[v, 0:1, columns]
            im = lifted[v, 1:2, columns]
            out.append(sums[2 * v] + (occ_re * re + occ_im * im))
            out.append(sums[2 * v + 1] + (occ_re * im - occ_im * re))
        return tuple(out)

    def three(ref, n):
        return ref.at[pl.ds(0, G - 1), :, pl.ds(n * BLOCK, BLOCK)]

    tiles = BLOCK // 128
    sums = tuple(jnp.zeros((16, 128), F32) for _ in range(2 * G))
    for n in range(blocks):
        wait(11 + n, 0, three(lifted, n))
        wait(11 + n, 1, three(lifted, n))
        sums = lax.fori_loop(n * tiles, (n + 1) * tiles, overlap, sums, unroll=4)
    lane = lax.broadcasted_iota(jnp.int32, (16, 128), 1)
    band_of = lane // 16
    own_row = (lane % 16) == lax.broadcasted_iota(jnp.int32, (16, 128), 0)
    matrix = jnp.zeros((16, 128), F32)
    for row in range(2 * G):
        column = jnp.sum(sums[row], axis=1, keepdims=True)
        matrix = jnp.where(band_of == row, column, matrix)
    over_send[0] = jnp.sum(jnp.where(own_row, matrix, 0.0), axis=0, keepdims=True)
    space_send(15, lambda peer: over_send.at[0], lambda mine: over_recv.at[mine])
    over_recv[me] = over_send[0]
    wait(15, 1, over_recv.at[pl.ds(0, S - 1)])
    row_sum = jnp.sum(over_recv[...], axis=0)
    spread = jnp.where(own_row, jnp.broadcast_to(row_sum, (16, 128)), 0.0)
    weights = []
    for row in range(2 * G):
        column = jnp.sum(jnp.where(band_of == row, spread, 0.0), axis=1, keepdims=True)
        weights.append(jnp.broadcast_to(column, (16, 128)))

    def correct(step, carry):
        columns = columns_of_tile(step)
        occ_re = occ_ref[0, :, columns]
        occ_im = occ_ref[1, :, columns]
        for v in range(G):
            w_re, w_im = weights[2 * v], weights[2 * v + 1]
            corr[v, 0:1, columns] = jnp.sum(occ_re * w_re - occ_im * w_im, axis=0, keepdims=True)
            corr[v, 1:2, columns] = jnp.sum(occ_re * w_im + occ_im * w_re, axis=0, keepdims=True)
        return carry

    for n in range(blocks):
        lax.fori_loop(n * tiles, (n + 1) * tiles, correct, 0, unroll=4)
        band_send(
            16 + n, lambda peer: block(corr, peer, n), lambda mine: block(corr_recv, mine, n)
        )

    corr_recv[group] = corr[group]
    beta_old = beta_ref[0:1].reshape(1, 1)
    partial = [jnp.zeros((1, 1), F32) for _ in range(4)]
    for n in range(blocks):
        wait(16 + n, 1, three(corr_recv, n))
        columns = pl.ds(n * BLOCK, BLOCK)
        for part in range(2):
            removed = (
                corr_recv[0, part : part + 1, columns]
                + corr_recv[1, part : part + 1, columns]
                + corr_recv[2, part : part + 1, columns]
                + corr_recv[3, part : part + 1, columns]
            )
            q = now_ref[part, 0:1, columns]
            p = prev_ref[part, 0:1, columns]
            u = lifted[group, part : part + 1, columns] - removed - beta_old * p
            rest_ref[part, 0:1, columns] = u
            for slot, product in enumerate((u * u, q * u, q * p, q * q)):
                partial[slot] = partial[slot] + jnp.sum(product, axis=1, keepdims=True)
    lane = lax.broadcasted_iota(jnp.int32, (1, 128), 1)
    row = jnp.zeros((1, 128), F32)
    for slot in range(4):
        row = jnp.where(lane == slot, partial[slot], row)
    sum_send1[0] = row
    here_low = lax.rem(me, LOW)
    here_high = me // LOW
    for step in range(1, G * LOW):
        peer_band = lax.rem(group + step // LOW, G)
        peer_low = lax.rem(here_low + step % LOW, LOW)
        pltpu.make_async_remote_copy(
            src_ref=sum_send1.at[0],
            dst_ref=sum_recv1.at[group * LOW + here_low],
            send_sem=sems.at[20, 0],
            recv_sem=sems.at[20, 1],
            device_id={"band": peer_band, "space": here_high * LOW + peer_low},
            device_id_type=MESH,
        ).start()
    sum_recv1[group * LOW + here_low] = sum_send1[0]
    wait(20, 1, sum_recv1.at[pl.ds(0, G * LOW - 1)])
    sum_send2[0] = jnp.sum(sum_recv1[...], axis=0)
    for step in range(1, HIGH):
        peer_high = lax.rem(here_high + step, HIGH)
        pltpu.make_async_remote_copy(
            src_ref=sum_send2.at[0],
            dst_ref=sum_recv2.at[here_high],
            send_sem=sems.at[21, 0],
            recv_sem=sems.at[21, 1],
            device_id={"space": peer_high * LOW + here_low},
            device_id_type=MESH,
        ).start()
    sum_recv2[here_high] = sum_send2[0]

    for part in range(3):
        wait(part, 0, send1.at[every_chunk])
        wait(8 + part, 0, send2.at[every_chunk])
    for t in range(4):
        wait(W_PHASE[t], 0, w_send.at[pl.ds(0, G - 1), :, tile_at(t)])
    wait(4, 0, h_send1.at[pl.ds(0, (S - 1) * HROWS)])
    wait(6, 0, h_send2.at[pl.ds(0, (S - 1) * HROWS)])
    wait(15, 0, over_recv.at[pl.ds(0, S - 1)])
    for n in range(blocks):
        wait(16 + n, 0, three(corr, n))
    wait(20, 0, sum_recv1.at[pl.ds(0, G * LOW - 1)])

    wait(21, 0, sum_recv2.at[pl.ds(0, HIGH - 1)])
    wait(21, 1, sum_recv2.at[pl.ds(0, HIGH - 1)])
    row = jnp.sum(sum_recv2[...], axis=0)

    def pick(slot):
        return jnp.sum(jnp.where(lane == slot, row, 0.0), axis=1, keepdims=True)

    norm_u, q_u, q_p, norm_q = [pick(slot) for slot in range(4)]
    alpha = (q_u + beta_old * q_p) / ENTRIES
    square = norm_u - 2.0 * alpha * q_u + alpha * alpha * norm_q
    beta_new = jnp.sqrt(square / ENTRIES)
    scalars_ref[...] = jnp.where(lane == 0, alpha, beta_new)


def finish(rest_ref, now_ref, scalars_ref, pot_in, next_ref, coef_ref, pot_ref):
    alpha = scalars_ref[0:1, 0:1]
    beta_new = scalars_ref[0:1, 1:2]
    inverse = 1.0 / beta_new
    for part in range(2):
        next_ref[part] = (rest_ref[part] - alpha * now_ref[part]) * inverse
    coef_ref[...] = scalars_ref[0:1, 0:2]
    pot_ref[...] = pot_in[...]


def per_device(
    lanczos_now,
    lanczos_prev,
    beta_prev,
    orbitals,
    band_energy,
    occupied,
    local_pot,
    xc_kernel,
    miller,
):
    later = [lanczos_prev, orbitals, occupied, local_pot, xc_kernel]
    later += [jnp.asarray(table) for table in make_tables()]
    later += [beta_prev, band_energy]
    vmem = pl.BlockSpec(memory_space=pltpu.VMEM)
    in_hbm = pl.BlockSpec(memory_space=pltpu.HBM)
    wide = pltpu.VMEM((3 * S * CELL, 128), F32)
    narrow = pltpu.VMEM((S * HROWS, 128), F32)
    quarter = pltpu.VMEM((G, S, HL), F32)
    band_waves = pltpu.VMEM((G, 2, WAVES), F32)
    real_grid = jax.ShapeDtypeStruct((PL, N, N), F32)
    waves = jax.ShapeDtypeStruct((2, 1, WAVES), F32)
    rest, scalars, potential = pl.pallas_call(
        body,
        out_shape=(waves, jax.ShapeDtypeStruct((1, 128), F32), real_grid),
        in_specs=[vmem, vmem] + [in_hbm] * len(later),
        out_specs=(vmem, vmem, vmem),
        scratch_shapes=[pltpu.VMEM(array.shape, array.dtype) for array in later]
        + [
            pltpu.VMEM((PL * N, WAVES), BF16),
            pltpu.VMEM((PL * N, 256), F32),
            wide,
            wide,
            pltpu.VMEM((PL * N, 384), F32),
            pltpu.VMEM((PL * N, 384), F32),
            pltpu.VMEM((PL * N, 384), F32),
            quarter,
            quarter,
            quarter,
            quarter,
            narrow,
            narrow,
            narrow,
            narrow,
            wide,
            wide,
            pltpu.VMEM((N, 4 * N), BF16),
            band_waves,
            pltpu.VMEM((1, 1, 128), F32),
            pltpu.VMEM((S, 1, 128), F32),
            band_waves,
            band_waves,
            pltpu.VMEM((1, 1, 128), F32),
            pltpu.VMEM((G * LOW, 1, 128), F32),
            pltpu.VMEM((1, 1, 128), F32),
            pltpu.VMEM((HIGH, 1, 128), F32),
            pltpu.SemaphoreType.DMA((28, 2)),
            pltpu.SemaphoreType.DMA((len(later),)),
        ],
        compiler_params=pltpu.CompilerParams(
            collective_id=0, has_side_effects=True, vmem_limit_bytes=60 * 1024 * 1024
        ),
    )(lanczos_now, miller, *later)
    return pl.pallas_call(
        finish,
        out_shape=(waves, jax.ShapeDtypeStruct((1, 2), F32), real_grid),
        in_specs=[vmem] * 4,
        out_specs=(vmem,) * 3,
    )(rest, lanczos_now, scalars, potential)


def solution(mesh):
    return jax.shard_map(
        per_device,
        mesh=mesh,
        in_specs=(
            P(None, "band", "space"),
            P(None, "band", "space"),
            P(),
            P(None, "band", "space", None, None),
            P("band"),
            P(None, "band", "space"),
            P("space", None, None),
            P("space", None, None),
            P(None, "space"),
        ),
        out_specs=(P(None, "band", "space"), P(), P("space", None, None)),
        check_vma=False,
    )
```

```python
import math

import jax
import jax.numpy as jnp
import ml_dtypes
import numpy as np
from jax import lax
from jax.experimental import pallas as pl
from jax.experimental.pallas import tpu as pltpu
from jax.sharding import PartitionSpec as P

MESH = pl.DeviceIdType.MESH
F32 = jnp.float32
BF16 = jnp.bfloat16
KINETIC = 8.0
HARTREE = 4.0
N = 192
S = 64
G = 4
PL = 3
CELL = 9
HROWS = 4
QUART = N // G
THIRD = PL * QUART
HL = 512
LOW = 4
HIGH = S // LOW
TILE = 64
WAVES = 16384
PLACE = 2048
READ = 1024
HALF = N // 2
BLOCK = 4096
W_PHASE = (3, 22, 23, 24)
H_PHASE = (7, 25, 26, 27)
STRIDE = 29
ENTRIES = float(2 * G * WAVES * S)


def split_np(table):
    high = table.astype(np.float32).astype(ml_dtypes.bfloat16)
    low = (table - high.astype(np.float64)).astype(np.float32).astype(ml_dtypes.bfloat16)
    return high, low


def left_table(table):
    high, low = split_np(table)
    return np.concatenate([high, low], axis=0)


def right_table(table):
    high, low = split_np(table)
    return np.concatenate([high, high, low], axis=0)


def make_tables():
    index = np.arange(N)
    angle = 2.0 * np.pi * (np.outer(index, index) % N) / N
    cosine = np.cos(angle) / math.sqrt(N)
    sine = np.sin(angle) / math.sqrt(N)
    order = np.concatenate([np.arange(S) * PL + part for part in range(PL)])
    re_lane = index // TILE * 128 + index % TILE
    im_lane = re_lane + TILE

    def lanes(sign):
        table = np.zeros((2 * N, 2 * N))
        table[np.ix_(re_lane, re_lane)] = cosine
        table[np.ix_(im_lane, re_lane)] = -sign * sine
        table[np.ix_(re_lane, im_lane)] = sign * sine
        table[np.ix_(im_lane, im_lane)] = cosine
        return table

    def rows(sign, row_order, column_order):
        both = [
            cosine[row_order][:, column_order],
            sign * sine[row_order][:, column_order],
        ]
        return left_table(np.concatenate(both, axis=0))

    cas = cosine + sine
    cas_in = np.zeros((2 * N, N))
    cas_in[re_lane] = cas
    cas_in[im_lane] = cas
    plus = lanes(1.0)
    return (
        np.stack([right_table(plus[t * 128 : (t + 1) * 128]) for t in range(3)]),
        right_table(lanes(-1.0)),
        rows(1.0, order, index),
        rows(1.0, index, order),
        np.stack([rows(-1.0, order[b * S : (b + 1) * S], index) for b in range(PL)]),
        rows(-1.0, index, order),
        right_table(cas_in),
        right_table(cas_in.T),
        left_table(cas[order]),
        left_table(cas[:, order]),
    )


def split(values):
    high = values.astype(BF16)
    low = (values - high.astype(F32)).astype(BF16)
    return high, low


def left(table_ref, values, parts=None):
    high, low = parts or split(values)
    rows = table_ref.shape[0] // 2
    by_high = jnp.dot(table_ref[...], high, preferred_element_type=F32)
    by_low = jnp.dot(table_ref[0:rows], low, preferred_element_type=F32)
    return by_high[0:rows] + (by_high[rows:] + by_low)


def right(values, table):
    high, low = split(values)
    stacked = jnp.concatenate([high, low, high], axis=1)
    return jnp.dot(stacked, table, preferred_element_type=F32)


def times_i(values):
    lane = lax.broadcasted_iota(jnp.int32, (values.shape[0], 128), 1)
    tiles = []
    for t in range(values.shape[1] // 128):
        turned = pltpu.roll(values[:, t * 128 : (t + 1) * 128], TILE, axis=1)
        tiles.append(jnp.where(lane < TILE, -turned, turned))
    return jnp.concatenate(tiles, axis=1)


def left_complex(table_ref, values, parts=None):
    both = left(table_ref, values, parts)
    rows = table_ref.shape[0] // 4
    return both[0:rows] + times_i(both[rows:])


def signed(indices):
    return jnp.where(indices < N // 2, indices, indices - N)


def doubled(values):
    tiles = []
    for t in range(3):
        part = values[:, t * TILE : (t + 1) * TILE]
        tiles += [part, part]
    return jnp.concatenate(tiles, axis=1)


def body(*refs):
    now_ref, miller_ref = refs[:2]
    later = refs[2:19]
    rest_ref, scalars_ref, pot_ref = refs[19:22]
    held = refs[22:39]
    (
        prev_ref,
        orbit_ref,
        occ_ref,
        local_ref,
        xc_ref,
        lane_plus,
        lane_minus,
        a_plus,
        b_plus,
        b_minus,
        a_minus,
        cas_in,
        cas_out,
        cas_rows,
        cas_cols,
        beta_ref,
        energy_ref,
    ) = held
    (
        hot,
        acc,
        send1,
        recv1,
        fields,
        packed,
        xc_part,
        w_send,
        w_recv,
        d_all,
        h_all,
        h_send1,
        h_recv1,
        h_send2,
        h_recv2,
        send2,
        recv2,
        table,
        occ_split,
        lifted,
        over_send,
        over_recv,
        corr,
        corr_recv,
        sum_send1,
        sum_recv1,
        sum_send2,
        sum_recv2,
        sems,
        load_sems,
    ) = refs[39:]
    me = lax.axis_index("space")
    group = lax.axis_index("band")
    start = me * PL

    def load(at):
        return pltpu.make_async_copy(later[at], held[at], load_sems.at[at])

    for at in range(len(later)):
        load(at).start()

    barrier = pltpu.get_barrier_semaphore()

    def greet(turn, carry):
        for step in range(7):
            peer = lax.rem(me + (turn * 7 + step + 1) * STRIDE, S)
            pl.semaphore_signal(barrier, inc=1, device_id={"space": peer}, device_id_type=MESH)
        return carry

    lax.fori_loop(0, (S - 1) // 7, greet, 0)
    for step in range(1, G):
        for low in range(LOW):
            peer = me // LOW * LOW + lax.rem(me + low, LOW)
            pl.semaphore_signal(
                barrier,
                inc=1,
                device_id={"band": lax.rem(group + step, G), "space": peer},
                device_id_type=MESH,
            )

    def space_send(phase, source, target):
        def one(turn, carry):
            for step in range(7):
                peer = lax.rem(me + (turn * 7 + step + 1) * STRIDE, S)
                pltpu.make_async_remote_copy(
                    src_ref=source(peer),
                    dst_ref=target(me),
                    send_sem=sems.at[phase, 0],
                    recv_sem=sems.at[phase, 1],
                    device_id={"space": peer},
                    device_id_type=MESH,
                ).start()
            return carry

        lax.fori_loop(0, (S - 1) // 7, one, 0)

    def band_send(phase, source, target):
        for step in (2, 1, 3):
            peer = lax.rem(group + step, G)
            pltpu.make_async_remote_copy(
                src_ref=source(peer),
                dst_ref=target(group),
                send_sem=sems.at[phase, 0],
                recv_sem=sems.at[phase, 1],
                device_id={"band": peer},
                device_id_type=MESH,
            ).start()

    def wait(phase, side, region):
        pltpu.make_async_copy(region, region, sems.at[phase, side]).wait()

    def part_chunk(ref, part):
        return lambda at: ref.at[pl.ds(part * S * CELL + at * CELL, CELL)]

    def chunk(ref):
        return lambda at: ref.at[pl.ds(at * HROWS, HROWS)]

    def keep(source, target, first, rows):
        own = pl.ds(first + me * rows, rows)
        target[own, :] = source[own, :]

    def cell_rows(part, m):
        return pl.ds(part * S * CELL + m, S, stride=CELL)

    def columns_at(step, size):
        return pl.ds(pl.multiple_of(step * size, size), size)

    def place(tile):
        def one(step, carry):
            columns = columns_at(step, PLACE)
            if tile == 0:
                row = (miller_ref[1:2, columns] - start) * N + miller_ref[0:1, columns]
                where = lax.broadcasted_iota(jnp.int16, (PL * N, PLACE), 0)
                hot[:, columns] = jnp.where(
                    where == row.astype(jnp.int16), BF16(1), BF16(0)
                )
            third = (miller_ref[2:3, columns] - tile * TILE).astype(jnp.int16)
            mask = lax.broadcasted_iota(jnp.int16, (TILE, PLACE), 0) == third
            parts = [jnp.where(mask, value, BF16(0)) for value in values_of(columns)]
            product = lax.dot_general(
                hot[:, columns],
                jnp.concatenate(parts, axis=0),
                (((1,), (1,)), ((), ())),
                preferred_element_type=F32,
            )
            acc[...] += product
            return carry

        acc[...] = jnp.zeros_like(acc)
        lax.fori_loop(0, WAVES // PLACE, one, 0, unroll=2)

    def values_of(columns):
        re_high, re_low = split(now_ref[0, 0:1, columns])
        im_high, im_low = split(now_ref[1, 0:1, columns])
        return re_high, im_high, re_low, im_low

    for t in range(3):
        place(t)
        placed = acc[:, 0:128] + acc[:, 128:256]
        if t == 0:
            load(7).wait()
        result = left_complex(
            a_plus, jnp.concatenate([placed[b * N : (b + 1) * N] for b in range(PL)], axis=1)
        )
        for r in range(PL):
            for b in range(PL):
                send1[cell_rows(t, r * PL + b), :] = result[
                    r * S : (r + 1) * S, b * 128 : (b + 1) * 128
                ]
        if t == 0:
            pl.semaphore_wait(barrier, S - 1 + (G - 1) * LOW)
        space_send(t, part_chunk(send1, t), part_chunk(recv1, t))
        keep(send1, recv1, t * S * CELL, CELL)

    for at in range(len(later)):
        if at != 7:
            load(at).wait()

    for r in range(PL):
        re = orbit_ref[0, 0, r]
        im = orbit_ref[1, 0, r]
        pieces = []
        for t in range(3):
            pieces += [re[:, t * TILE : (t + 1) * TILE], im[:, t * TILE : (t + 1) * TILE]]
        packed[r * N : (r + 1) * N] = jnp.concatenate(pieces, axis=1)

    every_chunk = pl.ds(0, (S - 1) * CELL)
    for t in range(3):
        wait(t, 1, recv1.at[every_chunk])
        values = jnp.concatenate(
            [
                jnp.concatenate([recv1[cell_rows(t, r * PL + b), :] for r in range(PL)], axis=1)
                for b in range(PL)
            ],
            axis=0,
        )
        result = left_complex(b_plus, values)
        result = jnp.concatenate([result[:, r * 128 : (r + 1) * 128] for r in range(PL)], axis=0)
        result = right(result, lane_plus[t])
        if t == 0:
            fields[...] = result
        else:
            fields[...] += result

    def tile_at(t):
        return pl.ds(t * 128, 128)

    tails = [[] for _ in range(G)]
    for r in range(PL):
        plane = pl.ds(r * N, N)
        values = left(cas_rows, right(2.0 * fields[plane, :] * packed[plane, :], cas_in[...]))
        for g in range(G):
            row = jnp.concatenate(
                [
                    values[b * S : (b + 1) * S, g * QUART : (g + 1) * QUART]
                    for b in range(PL)
                ],
                axis=1,
            )
            w_send[g, :, tile_at(r)] = row[:, :128]
            tails[g].append(row[:, 128:])
        if r == PL - 1:
            for g in range(G):
                w_send[g, :, tile_at(PL)] = jnp.concatenate(
                    tails[g] + [jnp.zeros((S, HL - PL * THIRD), F32)], axis=1
                )
        for t in (r,) if r < PL - 1 else (r, PL):
            band_send(
                W_PHASE[t],
                lambda peer: w_send.at[peer, :, tile_at(t)],
                lambda mine: w_recv.at[mine, :, tile_at(t)],
            )

    w_recv[group] = w_send[group]
    totals = []
    for t in range(4):
        wait(W_PHASE[t], 1, w_recv.at[pl.ds(0, G - 1), :, tile_at(t)])
        parts = [w_recv[g, :, tile_at(t)] for g in range(G)]
        totals.append(parts[0] + parts[1] + parts[2] + parts[3])
        h_send1[pl.ds(t, S, stride=HROWS), :] = totals[t]
    total = jnp.concatenate(totals, axis=1)
    space_send(4, chunk(h_send1), chunk(h_recv1))
    d_all[group] = total
    band_send(5, lambda peer: d_all.at[group], lambda mine: d_all.at[mine])
    keep(h_send1, h_recv1, 0, HROWS)

    lane = lax.broadcasted_iota(jnp.int32, (N, PL * QUART), 1)
    first = signed(lax.broadcasted_iota(jnp.int32, (N, PL * QUART), 0))
    plane = jnp.where(lane >= QUART, 1, 0) + jnp.where(lane >= 2 * QUART, 1, 0)
    second = signed(plane + start)
    third = signed(lane - plane * QUART + group * QUART)
    squared = first * first + second * second + third * third
    coulomb = jnp.where(squared > 0, HARTREE / jnp.maximum(squared, 1).astype(F32), 0.0)

    wait(4, 1, h_recv1.at[pl.ds(0, (S - 1) * HROWS)])
    pieces = [h_recv1[pl.ds(t, S, stride=HROWS), :] for t in range(4)]
    tall = jnp.concatenate(
        [
            jnp.concatenate([pieces[r], pieces[PL][:, r * 16 : (r + 1) * 16]], axis=1)
            for r in range(PL)
        ],
        axis=0,
    )
    tall = left(cas_rows, coulomb * left(cas_cols, tall))
    for r in range(PL):
        h_send2[pl.ds(r, S, stride=HROWS), :] = tall[r * S : (r + 1) * S, :128]
    h_send2[pl.ds(PL, S, stride=HROWS), :] = jnp.concatenate(
        [tall[r * S : (r + 1) * S, 128:] for r in range(PL)]
        + [jnp.zeros((S, HL - PL * THIRD), F32)],
        axis=1,
    )
    space_send(6, chunk(h_send2), chunk(h_recv2))
    keep(h_send2, h_recv2, 0, HROWS)

    def grid_values(ref, r):
        rows = [
            jnp.concatenate(
                [ref[g, :, tile_at(r)], ref[g, :, tile_at(PL)][:, r * 16 : (r + 1) * 16]], axis=1
            )
            for g in range(G)
        ]
        values = jnp.concatenate(
            [
                jnp.concatenate([row[:, b * QUART : (b + 1) * QUART] for row in rows], axis=1)
                for b in range(PL)
            ],
            axis=0,
        )
        return right(left(cas_cols, values), cas_out[...])

    wait(5, 0, d_all.at[pl.ds(0, G - 1)])
    wait(5, 1, d_all.at[pl.ds(0, G - 1)])
    for r in range(PL):
        plane = pl.ds(r * N, N)
        known = grid_values(d_all, r) * doubled(xc_ref[r])
        fields[plane, :] = doubled(local_ref[r]) * fields[plane, :] + known * packed[plane, :]
        xc_part[plane, :] = known

    wait(6, 1, h_recv2.at[pl.ds(0, (S - 1) * HROWS)])
    for t in (PL, 0, 1, 2):
        h_all[group, :, tile_at(t)] = h_recv2[pl.ds(t, S, stride=HROWS), :]
        band_send(
            H_PHASE[t],
            lambda peer: h_all.at[group, :, tile_at(t)],
            lambda mine: h_all.at[mine, :, tile_at(t)],
        )
    mixed = []
    for r in range(PL):
        plane = pl.ds(r * N, N)
        for t in (PL, 0) if r == 0 else (r,):
            wait(H_PHASE[t], 0, h_all.at[pl.ds(0, G - 1), :, tile_at(t)])
            wait(H_PHASE[t], 1, h_all.at[pl.ds(0, G - 1), :, tile_at(t)])
        hartree = grid_values(h_all, r)
        mixed.append(right(fields[plane, :] + hartree * packed[plane, :], lane_minus[...]))
        xc_part[plane, :] += hartree
    parts = split(jnp.concatenate(mixed, axis=1))
    for b in range(PL):
        result = left_complex(b_minus.at[b], None, parts)
        for r in range(PL):
            for t in range(3):
                send2[cell_rows(b, r * PL + t), :] = result[
                    :, (r * 3 + t) * 128 : (r * 3 + t + 1) * 128
                ]
        space_send(8 + b, part_chunk(send2, b), part_chunk(recv2, b))
        keep(send2, recv2, b * S * CELL, CELL)
    potential = xc_part[...]
    for r in range(PL):
        pot_ref[r] = jnp.concatenate(
            [potential[r * N : (r + 1) * N, t * 128 : t * 128 + TILE] for t in range(3)], axis=1
        )

    energy = energy_ref[0:1].reshape(1, 1)

    def read_waves(b, columns):
        seen = hot[b * N : (b + 1) * N, columns]
        third = miller_ref[2:3, columns]
        upper = third >= HALF
        upper_bit = jnp.where(upper, 1.0, 0.0).astype(BF16)
        high_part = seen * upper_bit
        low_part = seen - high_part
        found = jnp.dot(
            table[...],
            jnp.concatenate([low_part, low_part, high_part, high_part], axis=0),
            preferred_element_type=F32,
        )
        mask = lax.broadcasted_iota(jnp.int32, (HALF, READ), 0) == jnp.where(
            upper, third - HALF, third
        )
        sums = [
            jnp.sum(
                jnp.where(mask, found[half * HALF : (half + 1) * HALF], 0.0),
                axis=0,
                keepdims=True,
            )
            for half in range(2)
        ]
        for half in range(2):
            lifted[group, half : half + 1, columns] += sums[half]

    blocks = WAVES // BLOCK
    per_block = BLOCK // READ

    for n in range(blocks):
        columns = pl.ds(n * BLOCK, BLOCK)
        index = [signed(miller_ref[d : d + 1, columns]) for d in range(3)]
        squared = index[0] * index[0] + index[1] * index[1] + index[2] * index[2]
        diagonal = KINETIC * squared.astype(F32) / float(N * N) - energy
        for half in range(2):
            lifted[group, half : half + 1, columns] = diagonal * now_ref[half, 0:1, columns]
        high, low = split(
            jnp.concatenate([occ_ref[0, :, columns], occ_ref[1, :, columns]], axis=0)
        )
        occ_split[0:32, columns] = high
        occ_split[32:64, columns] = low
        occ_split[64:96, columns] = high

    def block(ref, at, n):
        return ref.at[at, :, pl.ds(n * BLOCK, BLOCK)]

    for b in range(PL):
        wait(8 + b, 1, recv2.at[every_chunk])
        values = jnp.concatenate(
            [
                jnp.concatenate([recv2[cell_rows(b, r * PL + t), :] for t in range(3)], axis=1)
                for r in range(PL)
            ],
            axis=0,
        )
        turned = jnp.transpose(left_complex(a_minus, values))
        pieces = []
        for side in range(2):
            rows = []
            for half in range(2):
                whole = jnp.concatenate(
                    [
                        turned[t * 128 + half * TILE : t * 128 + (half + 1) * TILE]
                        for t in range(3)
                    ],
                    axis=0,
                )
                rows.append(whole[side * HALF : (side + 1) * HALF])
            rows = jnp.concatenate(rows, axis=0)
            high = rows.astype(BF16).astype(F32)
            pieces += [high, rows - high]
        table[...] = jnp.concatenate(pieces, axis=1).astype(BF16)

        def one(step, carry):
            read_waves(b, columns_at(step, READ))
            return carry

        for n in range(blocks):
            lax.fori_loop(n * per_block, (n + 1) * per_block, one, 0, unroll=2)
            if b == PL - 1:
                band_send(
                    11 + n,
                    lambda peer: block(lifted, group, n),
                    lambda mine: block(lifted, mine, n),
                )

    def columns_of_tile(step):
        return pl.ds(pl.multiple_of(step * 128, 128), 128)

    def overlap(step, sums):
        columns = columns_of_tile(step)
        occ_re = occ_ref[0, :, columns]
        occ_im = occ_ref[1, :, columns]
        out = []
        for v in range(G):
            re = lifted[v, 0:1, columns]
            im = lifted[v, 1:2, columns]
            out.append(sums[2 * v] + (occ_re * re + occ_im * im))
            out.append(sums[2 * v + 1] + (occ_re * im - occ_im * re))
        return tuple(out)

    def three(ref, n):
        return ref.at[pl.ds(0, G - 1), :, pl.ds(n * BLOCK, BLOCK)]

    tiles = BLOCK // 128
    sums = tuple(jnp.zeros((16, 128), F32) for _ in range(2 * G))
    for n in range(blocks):
        wait(11 + n, 0, three(lifted, n))
        wait(11 + n, 1, three(lifted, n))
        sums = lax.fori_loop(n * tiles, (n + 1) * tiles, overlap, sums, unroll=4)
    lane = lax.broadcasted_iota(jnp.int32, (16, 128), 1)
    band_of = lane // 16
    own_row = (lane % 16) == lax.broadcasted_iota(jnp.int32, (16, 128), 0)
    matrix = jnp.zeros((16, 128), F32)
    for row in range(2 * G):
        column = jnp.sum(sums[row], axis=1, keepdims=True)
        matrix = jnp.where(band_of == row, column, matrix)
    over_send[0] = jnp.sum(jnp.where(own_row, matrix, 0.0), axis=0, keepdims=True)
    space_send(15, lambda peer: over_send.at[0], lambda mine: over_recv.at[mine])
    over_recv[me] = over_send[0]
    wait(15, 1, over_recv.at[pl.ds(0, S - 1)])
    row_sum = jnp.sum(over_recv[...], axis=0)
    lane = lax.broadcasted_iota(jnp.int32, (8, 128), 1)
    line = lax.broadcasted_iota(jnp.int32, (8, 128), 0)
    spread = jnp.where(lane // 16 == line, jnp.broadcast_to(row_sum, (8, 128)), 0.0)
    for shift in (64, 32, 16):
        spread = spread + pltpu.roll(spread, shift, axis=1)
    crossed = jnp.where(
        line % 2 == 0, -pltpu.roll(spread, 7, axis=0), pltpu.roll(spread, 1, axis=0)
    )
    weights = jnp.where(lane // 16 % 2 == 0, spread, crossed)
    weights_high = weights.astype(BF16).astype(F32)
    weights = jnp.where(lane < 64, weights_high, weights - weights_high).astype(BF16)[:, :96]

    def correct(step, carry):
        columns = columns_at(step, READ)
        result = jnp.dot(weights, occ_split[:, columns], preferred_element_type=F32)
        for v in range(G):
            for part in range(2):
                corr[v, part : part + 1, columns] = result[2 * v + part : 2 * v + part + 1]
        return carry

    for n in range(blocks):
        lax.fori_loop(n * per_block, (n + 1) * per_block, correct, 0, unroll=2)
        band_send(
            16 + n, lambda peer: block(corr, peer, n), lambda mine: block(corr_recv, mine, n)
        )

    corr_recv[group] = corr[group]
    beta_old = beta_ref[0:1].reshape(1, 1)
    partial = [jnp.zeros((1, 1), F32) for _ in range(4)]
    for n in range(blocks):
        wait(16 + n, 1, three(corr_recv, n))
        columns = pl.ds(n * BLOCK, BLOCK)
        for part in range(2):
            removed = (
                corr_recv[0, part : part + 1, columns]
                + corr_recv[1, part : part + 1, columns]
                + corr_recv[2, part : part + 1, columns]
                + corr_recv[3, part : part + 1, columns]
            )
            q = now_ref[part, 0:1, columns]
            p = prev_ref[part, 0:1, columns]
            u = lifted[group, part : part + 1, columns] - removed - beta_old * p
            rest_ref[part, 0:1, columns] = u
            for slot, product in enumerate((u * u, q * u, q * p, q * q)):
                partial[slot] = partial[slot] + jnp.sum(product, axis=1, keepdims=True)
    lane = lax.broadcasted_iota(jnp.int32, (1, 128), 1)
    row = jnp.zeros((1, 128), F32)
    for slot in range(4):
        row = jnp.where(lane == slot, partial[slot], row)
    sum_send1[0] = row
    here_low = lax.rem(me, LOW)
    here_high = me // LOW
    for step in range(1, G * LOW):
        peer_band = lax.rem(group + step // LOW, G)
        peer_low = lax.rem(here_low + step % LOW, LOW)
        pltpu.make_async_remote_copy(
            src_ref=sum_send1.at[0],
            dst_ref=sum_recv1.at[group * LOW + here_low],
            send_sem=sems.at[20, 0],
            recv_sem=sems.at[20, 1],
            device_id={"band": peer_band, "space": here_high * LOW + peer_low},
            device_id_type=MESH,
        ).start()
    sum_recv1[group * LOW + here_low] = sum_send1[0]
    wait(20, 1, sum_recv1.at[pl.ds(0, G * LOW - 1)])
    sum_send2[0] = jnp.sum(sum_recv1[...], axis=0)
    for step in range(1, HIGH):
        peer_high = lax.rem(here_high + step, HIGH)
        pltpu.make_async_remote_copy(
            src_ref=sum_send2.at[0],
            dst_ref=sum_recv2.at[here_high],
            send_sem=sems.at[21, 0],
            recv_sem=sems.at[21, 1],
            device_id={"space": peer_high * LOW + here_low},
            device_id_type=MESH,
        ).start()
    sum_recv2[here_high] = sum_send2[0]

    for part in range(3):
        wait(part, 0, send1.at[every_chunk])
        wait(8 + part, 0, send2.at[every_chunk])
    for t in range(4):
        wait(W_PHASE[t], 0, w_send.at[pl.ds(0, G - 1), :, tile_at(t)])
    wait(4, 0, h_send1.at[pl.ds(0, (S - 1) * HROWS)])
    wait(6, 0, h_send2.at[pl.ds(0, (S - 1) * HROWS)])
    wait(15, 0, over_recv.at[pl.ds(0, S - 1)])
    for n in range(blocks):
        wait(16 + n, 0, three(corr, n))
    wait(20, 0, sum_recv1.at[pl.ds(0, G * LOW - 1)])

    wait(21, 0, sum_recv2.at[pl.ds(0, HIGH - 1)])
    wait(21, 1, sum_recv2.at[pl.ds(0, HIGH - 1)])
    row = jnp.sum(sum_recv2[...], axis=0)

    def pick(slot):
        return jnp.sum(jnp.where(lane == slot, row, 0.0), axis=1, keepdims=True)

    norm_u, q_u, q_p, norm_q = [pick(slot) for slot in range(4)]
    alpha = (q_u + beta_old * q_p) / ENTRIES
    square = norm_u - 2.0 * alpha * q_u + alpha * alpha * norm_q
    beta_new = jnp.sqrt(square / ENTRIES)
    scalars_ref[...] = jnp.where(lane == 0, alpha, beta_new)


def finish(rest_ref, now_ref, scalars_ref, pot_in, next_ref, coef_ref, pot_ref):
    alpha = scalars_ref[0:1, 0:1]
    beta_new = scalars_ref[0:1, 1:2]
    inverse = 1.0 / beta_new
    for part in range(2):
        next_ref[part] = (rest_ref[part] - alpha * now_ref[part]) * inverse
    coef_ref[...] = scalars_ref[0:1, 0:2]
    pot_ref[...] = pot_in[...]


def per_device(
    lanczos_now,
    lanczos_prev,
    beta_prev,
    orbitals,
    band_energy,
    occupied,
    local_pot,
    xc_kernel,
    miller,
):
    later = [lanczos_prev, orbitals, occupied, local_pot, xc_kernel]
    later += [jnp.asarray(table) for table in make_tables()]
    later += [beta_prev, band_energy]
    vmem = pl.BlockSpec(memory_space=pltpu.VMEM)
    in_hbm = pl.BlockSpec(memory_space=pltpu.HBM)
    wide = pltpu.VMEM((3 * S * CELL, 128), F32)
    narrow = pltpu.VMEM((S * HROWS, 128), F32)
    quarter = pltpu.VMEM((G, S, HL), F32)
    band_waves = pltpu.VMEM((G, 2, WAVES), F32)
    real_grid = jax.ShapeDtypeStruct((PL, N, N), F32)
    waves = jax.ShapeDtypeStruct((2, 1, WAVES), F32)
    rest, scalars, potential = pl.pallas_call(
        body,
        out_shape=(waves, jax.ShapeDtypeStruct((1, 128), F32), real_grid),
        in_specs=[vmem, vmem] + [in_hbm] * len(later),
        out_specs=(vmem, vmem, vmem),
        scratch_shapes=[pltpu.VMEM(array.shape, array.dtype) for array in later]
        + [
            pltpu.VMEM((PL * N, WAVES), BF16),
            pltpu.VMEM((PL * N, 256), F32),
            wide,
            wide,
            pltpu.VMEM((PL * N, 384), F32),
            pltpu.VMEM((PL * N, 384), F32),
            pltpu.VMEM((PL * N, 384), F32),
            quarter,
            quarter,
            quarter,
            quarter,
            narrow,
            narrow,
            narrow,
            narrow,
            wide,
            wide,
            pltpu.VMEM((N, 4 * N), BF16),
            pltpu.VMEM((96, WAVES), BF16),
            band_waves,
            pltpu.VMEM((1, 1, 128), F32),
            pltpu.VMEM((S, 1, 128), F32),
            band_waves,
            band_waves,
            pltpu.VMEM((1, 1, 128), F32),
            pltpu.VMEM((G * LOW, 1, 128), F32),
            pltpu.VMEM((1, 1, 128), F32),
            pltpu.VMEM((HIGH, 1, 128), F32),
            pltpu.SemaphoreType.DMA((28, 2)),
            pltpu.SemaphoreType.DMA((len(later),)),
        ],
        compiler_params=pltpu.CompilerParams(
            collective_id=0, has_side_effects=True, vmem_limit_bytes=60 * 1024 * 1024
        ),
    )(lanczos_now, miller, *later)
    return pl.pallas_call(
        finish,
        out_shape=(waves, jax.ShapeDtypeStruct((1, 2), F32), real_grid),
        in_specs=[vmem] * 4,
        out_specs=(vmem,) * 3,
    )(rest, lanczos_now, scalars, potential)


def solution(mesh):
    return jax.shard_map(
        per_device,
        mesh=mesh,
        in_specs=(
            P(None, "band", "space"),
            P(None, "band", "space"),
            P(),
            P(None, "band", "space", None, None),
            P("band"),
            P(None, "band", "space"),
            P("space", None, None),
            P("space", None, None),
            P(None, "space"),
        ),
        out_specs=(P(None, "band", "space"), P(), P("space", None, None)),
        check_vma=False,
    )
```

```python
import math

import jax
import jax.numpy as jnp
import ml_dtypes
import numpy as np
from jax import lax
from jax.experimental import pallas as pl
from jax.experimental.pallas import tpu as pltpu
from jax.sharding import PartitionSpec as P

MESH = pl.DeviceIdType.MESH
F32 = jnp.float32
BF16 = jnp.bfloat16
KINETIC = 8.0
HARTREE = 4.0
N = 192
S = 64
G = 4
PL = 3
CELL = 9
HROWS = 4
QUART = N // G
THIRD = PL * QUART
HL = 512
LOW = 4
HIGH = S // LOW
TILE = 64
WAVES = 16384
PLACE = 4096
READ = 2048
HALF = N // 2
BLOCK = 4096
W_PHASE = (3, 22, 23, 24)
H_PHASE = (7, 25, 26, 27)
STRIDE = 29
ENTRIES = float(2 * G * WAVES * S)


def split_np(table):
    high = table.astype(np.float32).astype(ml_dtypes.bfloat16)
    low = (table - high.astype(np.float64)).astype(np.float32).astype(ml_dtypes.bfloat16)
    return high, low


def left_table(table):
    high, low = split_np(table)
    return np.concatenate([high, low], axis=0)


def right_table(table):
    high, low = split_np(table)
    return np.concatenate([high, high, low], axis=0)


def make_tables():
    index = np.arange(N)
    angle = 2.0 * np.pi * (np.outer(index, index) % N) / N
    cosine = np.cos(angle) / math.sqrt(N)
    sine = np.sin(angle) / math.sqrt(N)
    order = np.concatenate([np.arange(S) * PL + part for part in range(PL)])
    re_lane = index // TILE * 128 + index % TILE
    im_lane = re_lane + TILE

    def lanes(sign):
        table = np.zeros((2 * N, 2 * N))
        table[np.ix_(re_lane, re_lane)] = cosine
        table[np.ix_(im_lane, re_lane)] = -sign * sine
        table[np.ix_(re_lane, im_lane)] = sign * sine
        table[np.ix_(im_lane, im_lane)] = cosine
        return table

    def rows(sign, row_order, column_order):
        both = [
            cosine[row_order][:, column_order],
            sign * sine[row_order][:, column_order],
        ]
        return left_table(np.concatenate(both, axis=0))

    cas = cosine + sine
    cas_in = np.zeros((2 * N, N))
    cas_in[re_lane] = cas
    cas_in[im_lane] = cas
    plus = lanes(1.0)
    return (
        np.stack([right_table(plus[t * 128 : (t + 1) * 128]) for t in range(3)]),
        right_table(lanes(-1.0)),
        rows(1.0, order, index),
        rows(1.0, index, order),
        np.stack([rows(-1.0, order[b * S : (b + 1) * S], index) for b in range(PL)]),
        rows(-1.0, index, order),
        right_table(cas_in),
        right_table(cas_in.T),
        left_table(cas[order]),
        left_table(cas[:, order]),
    )


def split(values):
    high = values.astype(BF16)
    low = (values - high.astype(F32)).astype(BF16)
    return high, low


def left(table_ref, values, parts=None):
    high, low = parts or split(values)
    rows = table_ref.shape[0] // 2
    by_high = jnp.dot(table_ref[...], high, preferred_element_type=F32)
    by_low = jnp.dot(table_ref[0:rows], low, preferred_element_type=F32)
    return by_high[0:rows] + (by_high[rows:] + by_low)


def right(values, table):
    high, low = split(values)
    stacked = jnp.concatenate([high, low, high], axis=1)
    return jnp.dot(stacked, table, preferred_element_type=F32)


def times_i(values):
    lane = lax.broadcasted_iota(jnp.int32, (values.shape[0], 128), 1)
    tiles = []
    for t in range(values.shape[1] // 128):
        turned = pltpu.roll(values[:, t * 128 : (t + 1) * 128], TILE, axis=1)
        tiles.append(jnp.where(lane < TILE, -turned, turned))
    return jnp.concatenate(tiles, axis=1)


def left_complex(table_ref, values, parts=None):
    both = left(table_ref, values, parts)
    rows = table_ref.shape[0] // 4
    return both[0:rows] + times_i(both[rows:])


def signed(indices):
    return jnp.where(indices < N // 2, indices, indices - N)


def doubled(values):
    tiles = []
    for t in range(3):
        part = values[:, t * TILE : (t + 1) * TILE]
        tiles += [part, part]
    return jnp.concatenate(tiles, axis=1)


def body(*refs):
    now_ref, miller_ref = refs[:2]
    later = refs[2:19]
    rest_ref, scalars_ref, pot_ref = refs[19:22]
    held = refs[22:39]
    (
        prev_ref,
        orbit_ref,
        occ_ref,
        local_ref,
        xc_ref,
        lane_plus,
        lane_minus,
        a_plus,
        b_plus,
        b_minus,
        a_minus,
        cas_in,
        cas_out,
        cas_rows,
        cas_cols,
        beta_ref,
        energy_ref,
    ) = held
    (
        hot,
        acc,
        send1,
        recv1,
        fields,
        packed,
        xc_part,
        w_send,
        w_recv,
        d_all,
        h_all,
        h_send1,
        h_recv1,
        h_send2,
        h_recv2,
        send2,
        recv2,
        table,
        occ_split,
        lifted,
        over_send,
        over_recv,
        corr,
        corr_recv,
        sum_send1,
        sum_recv1,
        sum_send2,
        sum_recv2,
        sems,
        load_sems,
    ) = refs[39:]
    me = lax.axis_index("space")
    group = lax.axis_index("band")
    start = me * PL

    def load(at):
        return pltpu.make_async_copy(later[at], held[at], load_sems.at[at])

    for at in range(len(later)):
        load(at).start()

    barrier = pltpu.get_barrier_semaphore()

    def greet(turn, carry):
        for step in range(7):
            peer = lax.rem(me + (turn * 7 + step + 1) * STRIDE, S)
            pl.semaphore_signal(barrier, inc=1, device_id={"space": peer}, device_id_type=MESH)
        return carry

    lax.fori_loop(0, (S - 1) // 7, greet, 0)
    for step in range(1, G):
        for low in range(LOW):
            peer = me // LOW * LOW + lax.rem(me + low, LOW)
            pl.semaphore_signal(
                barrier,
                inc=1,
                device_id={"band": lax.rem(group + step, G), "space": peer},
                device_id_type=MESH,
            )

    def space_send(phase, source, target):
        def one(turn, carry):
            for step in range(7):
                peer = lax.rem(me + (turn * 7 + step + 1) * STRIDE, S)
                pltpu.make_async_remote_copy(
                    src_ref=source(peer),
                    dst_ref=target(me),
                    send_sem=sems.at[phase, 0],
                    recv_sem=sems.at[phase, 1],
                    device_id={"space": peer},
                    device_id_type=MESH,
                ).start()
            return carry

        lax.fori_loop(0, (S - 1) // 7, one, 0)

    def band_send(phase, source, target):
        for step in (2, 1, 3):
            peer = lax.rem(group + step, G)
            pltpu.make_async_remote_copy(
                src_ref=source(peer),
                dst_ref=target(group),
                send_sem=sems.at[phase, 0],
                recv_sem=sems.at[phase, 1],
                device_id={"band": peer},
                device_id_type=MESH,
            ).start()

    def wait(phase, side, region):
        pltpu.make_async_copy(region, region, sems.at[phase, side]).wait()

    def part_chunk(ref, part):
        return lambda at: ref.at[pl.ds(part * S * CELL + at * CELL, CELL)]

    def chunk(ref):
        return lambda at: ref.at[pl.ds(at * HROWS, HROWS)]

    def keep(source, target, first, rows):
        own = pl.ds(first + me * rows, rows)
        target[own, :] = source[own, :]

    def cell_rows(part, m):
        return pl.ds(part * S * CELL + m, S, stride=CELL)

    def columns_at(step, size):
        return pl.ds(pl.multiple_of(step * size, size), size)

    def place(tile):
        def one(step, carry):
            columns = columns_at(step, PLACE)
            if tile == 0:
                row = (miller_ref[1:2, columns] - start) * N + miller_ref[0:1, columns]
                where = lax.broadcasted_iota(jnp.int16, (PL * N, PLACE), 0)
                seen = jnp.where(where == row.astype(jnp.int16), BF16(1), BF16(0))
                hot[:, columns] = seen
            else:
                seen = hot[:, columns]
            third = (miller_ref[2:3, columns] - tile * TILE).astype(jnp.int16)
            mask = lax.broadcasted_iota(jnp.int16, (TILE, PLACE), 0) == third
            parts = [jnp.where(mask, value, BF16(0)) for value in values_of(columns)]
            product = lax.dot_general(
                seen,
                jnp.concatenate(parts, axis=0),
                (((1,), (1,)), ((), ())),
                preferred_element_type=F32,
            )
            acc[...] += product
            return carry

        acc[...] = jnp.zeros_like(acc)
        lax.fori_loop(0, WAVES // PLACE, one, 0, unroll=2)

    def values_of(columns):
        re_high, re_low = split(now_ref[0, 0:1, columns])
        im_high, im_low = split(now_ref[1, 0:1, columns])
        return re_high, im_high, re_low, im_low

    for t in range(3):
        place(t)
        placed = acc[:, 0:128] + acc[:, 128:256]
        if t == 0:
            load(7).wait()
        result = left_complex(
            a_plus, jnp.concatenate([placed[b * N : (b + 1) * N] for b in range(PL)], axis=1)
        )
        for r in range(PL):
            for b in range(PL):
                send1[cell_rows(t, r * PL + b), :] = result[
                    r * S : (r + 1) * S, b * 128 : (b + 1) * 128
                ]
        if t == 0:
            pl.semaphore_wait(barrier, S - 1 + (G - 1) * LOW)
        space_send(t, part_chunk(send1, t), part_chunk(recv1, t))
        keep(send1, recv1, t * S * CELL, CELL)

    for at in range(len(later)):
        if at != 7:
            load(at).wait()

    for r in range(PL):
        re = orbit_ref[0, 0, r]
        im = orbit_ref[1, 0, r]
        pieces = []
        for t in range(3):
            pieces += [re[:, t * TILE : (t + 1) * TILE], im[:, t * TILE : (t + 1) * TILE]]
        packed[r * N : (r + 1) * N] = jnp.concatenate(pieces, axis=1)

    every_chunk = pl.ds(0, (S - 1) * CELL)
    for t in range(3):
        wait(t, 1, recv1.at[every_chunk])
        values = jnp.concatenate(
            [
                jnp.concatenate([recv1[cell_rows(t, r * PL + b), :] for r in range(PL)], axis=1)
                for b in range(PL)
            ],
            axis=0,
        )
        result = left_complex(b_plus, values)
        result = jnp.concatenate([result[:, r * 128 : (r + 1) * 128] for r in range(PL)], axis=0)
        result = right(result, lane_plus[t])
        if t == 0:
            fields[...] = result
        else:
            fields[...] += result

    def tile_at(t):
        return pl.ds(t * 128, 128)

    tails = [[] for _ in range(G)]
    for r in range(PL):
        plane = pl.ds(r * N, N)
        values = left(cas_rows, right(2.0 * fields[plane, :] * packed[plane, :], cas_in[...]))
        for g in range(G):
            row = jnp.concatenate(
                [
                    values[b * S : (b + 1) * S, g * QUART : (g + 1) * QUART]
                    for b in range(PL)
                ],
                axis=1,
            )
            w_send[g, :, tile_at(r)] = row[:, :128]
            tails[g].append(row[:, 128:])
        if r == PL - 1:
            for g in range(G):
                w_send[g, :, tile_at(PL)] = jnp.concatenate(
                    tails[g] + [jnp.zeros((S, HL - PL * THIRD), F32)], axis=1
                )
        for t in (r,) if r < PL - 1 else (r, PL):
            band_send(
                W_PHASE[t],
                lambda peer: w_send.at[peer, :, tile_at(t)],
                lambda mine: w_recv.at[mine, :, tile_at(t)],
            )

    w_recv[group] = w_send[group]
    totals = []
    for t in range(4):
        wait(W_PHASE[t], 1, w_recv.at[pl.ds(0, G - 1), :, tile_at(t)])
        parts = [w_recv[g, :, tile_at(t)] for g in range(G)]
        totals.append(parts[0] + parts[1] + parts[2] + parts[3])
        h_send1[pl.ds(t, S, stride=HROWS), :] = totals[t]
    total = jnp.concatenate(totals, axis=1)
    space_send(4, chunk(h_send1), chunk(h_recv1))
    d_all[group] = total
    band_send(5, lambda peer: d_all.at[group], lambda mine: d_all.at[mine])
    keep(h_send1, h_recv1, 0, HROWS)

    lane = lax.broadcasted_iota(jnp.int32, (N, PL * QUART), 1)
    first = signed(lax.broadcasted_iota(jnp.int32, (N, PL * QUART), 0))
    plane = jnp.where(lane >= QUART, 1, 0) + jnp.where(lane >= 2 * QUART, 1, 0)
    second = signed(plane + start)
    third = signed(lane - plane * QUART + group * QUART)
    squared = first * first + second * second + third * third
    coulomb = jnp.where(squared > 0, HARTREE / jnp.maximum(squared, 1).astype(F32), 0.0)

    wait(4, 1, h_recv1.at[pl.ds(0, (S - 1) * HROWS)])
    pieces = [h_recv1[pl.ds(t, S, stride=HROWS), :] for t in range(4)]
    tall = jnp.concatenate(
        [
            jnp.concatenate([pieces[r], pieces[PL][:, r * 16 : (r + 1) * 16]], axis=1)
            for r in range(PL)
        ],
        axis=0,
    )
    tall = left(cas_rows, coulomb * left(cas_cols, tall))
    for r in range(PL):
        h_send2[pl.ds(r, S, stride=HROWS), :] = tall[r * S : (r + 1) * S, :128]
    h_send2[pl.ds(PL, S, stride=HROWS), :] = jnp.concatenate(
        [tall[r * S : (r + 1) * S, 128:] for r in range(PL)]
        + [jnp.zeros((S, HL - PL * THIRD), F32)],
        axis=1,
    )
    space_send(6, chunk(h_send2), chunk(h_recv2))
    keep(h_send2, h_recv2, 0, HROWS)

    def grid_values(ref, r):
        rows = [
            jnp.concatenate(
                [ref[g, :, tile_at(r)], ref[g, :, tile_at(PL)][:, r * 16 : (r + 1) * 16]], axis=1
            )
            for g in range(G)
        ]
        values = jnp.concatenate(
            [
                jnp.concatenate([row[:, b * QUART : (b + 1) * QUART] for row in rows], axis=1)
                for b in range(PL)
            ],
            axis=0,
        )
        return right(left(cas_cols, values), cas_out[...])

    wait(5, 0, d_all.at[pl.ds(0, G - 1)])
    wait(5, 1, d_all.at[pl.ds(0, G - 1)])
    for r in range(PL):
        plane = pl.ds(r * N, N)
        known = grid_values(d_all, r) * doubled(xc_ref[r])
        fields[plane, :] = doubled(local_ref[r]) * fields[plane, :] + known * packed[plane, :]
        xc_part[plane, :] = known

    wait(6, 1, h_recv2.at[pl.ds(0, (S - 1) * HROWS)])
    for t in (PL, 0, 1, 2):
        h_all[group, :, tile_at(t)] = h_recv2[pl.ds(t, S, stride=HROWS), :]
        band_send(
            H_PHASE[t],
            lambda peer: h_all.at[group, :, tile_at(t)],
            lambda mine: h_all.at[mine, :, tile_at(t)],
        )
    mixed = []
    for r in range(PL):
        plane = pl.ds(r * N, N)
        for t in (PL, 0) if r == 0 else (r,):
            wait(H_PHASE[t], 0, h_all.at[pl.ds(0, G - 1), :, tile_at(t)])
            wait(H_PHASE[t], 1, h_all.at[pl.ds(0, G - 1), :, tile_at(t)])
        hartree = grid_values(h_all, r)
        mixed.append(right(fields[plane, :] + hartree * packed[plane, :], lane_minus[...]))
        xc_part[plane, :] += hartree
    parts = split(jnp.concatenate(mixed, axis=1))
    for b in range(PL):
        result = left_complex(b_minus.at[b], None, parts)
        for r in range(PL):
            for t in range(3):
                send2[cell_rows(b, r * PL + t), :] = result[
                    :, (r * 3 + t) * 128 : (r * 3 + t + 1) * 128
                ]
        space_send(8 + b, part_chunk(send2, b), part_chunk(recv2, b))
        keep(send2, recv2, b * S * CELL, CELL)
    potential = xc_part[...]
    for r in range(PL):
        pot_ref[r] = jnp.concatenate(
            [potential[r * N : (r + 1) * N, t * 128 : t * 128 + TILE] for t in range(3)], axis=1
        )

    energy = energy_ref[0:1].reshape(1, 1)

    def read_waves(b, columns):
        seen = hot[b * N : (b + 1) * N, columns]
        third = miller_ref[2:3, columns]
        upper = third >= HALF
        upper_bit = jnp.where(upper, 1.0, 0.0).astype(BF16)
        high_part = seen * upper_bit
        low_part = seen - high_part
        found = jnp.dot(
            table[...],
            jnp.concatenate([low_part, low_part, high_part, high_part], axis=0),
            preferred_element_type=F32,
        )
        mask = lax.broadcasted_iota(jnp.int32, (HALF, READ), 0) == jnp.where(
            upper, third - HALF, third
        )
        sums = [
            jnp.sum(
                jnp.where(mask, found[half * HALF : (half + 1) * HALF], 0.0),
                axis=0,
                keepdims=True,
            )
            for half in range(2)
        ]
        for half in range(2):
            lifted[group, half : half + 1, columns] += sums[half]

    blocks = WAVES // BLOCK
    per_block = BLOCK // READ

    for n in range(blocks):
        columns = pl.ds(n * BLOCK, BLOCK)
        index = [signed(miller_ref[d : d + 1, columns]) for d in range(3)]
        squared = index[0] * index[0] + index[1] * index[1] + index[2] * index[2]
        diagonal = KINETIC * squared.astype(F32) / float(N * N) - energy
        for half in range(2):
            lifted[group, half : half + 1, columns] = diagonal * now_ref[half, 0:1, columns]
        high, low = split(
            jnp.concatenate([occ_ref[0, :, columns], occ_ref[1, :, columns]], axis=0)
        )
        occ_split[0:32, columns] = high
        occ_split[32:64, columns] = low
        occ_split[64:96, columns] = high

    def block(ref, at, n):
        return ref.at[at, :, pl.ds(n * BLOCK, BLOCK)]

    for b in range(PL):
        wait(8 + b, 1, recv2.at[every_chunk])
        values = jnp.concatenate(
            [
                jnp.concatenate([recv2[cell_rows(b, r * PL + t), :] for t in range(3)], axis=1)
                for r in range(PL)
            ],
            axis=0,
        )
        turned = jnp.transpose(left_complex(a_minus, values))
        pieces = []
        for side in range(2):
            rows = []
            for half in range(2):
                whole = jnp.concatenate(
                    [
                        turned[t * 128 + half * TILE : t * 128 + (half + 1) * TILE]
                        for t in range(3)
                    ],
                    axis=0,
                )
                rows.append(whole[side * HALF : (side + 1) * HALF])
            rows = jnp.concatenate(rows, axis=0)
            high = rows.astype(BF16).astype(F32)
            pieces += [high, rows - high]
        table[...] = jnp.concatenate(pieces, axis=1).astype(BF16)

        def one(step, carry):
            read_waves(b, columns_at(step, READ))
            return carry

        for n in range(blocks):
            lax.fori_loop(n * per_block, (n + 1) * per_block, one, 0, unroll=2)
            if b == PL - 1:
                band_send(
                    11 + n,
                    lambda peer: block(lifted, group, n),
                    lambda mine: block(lifted, mine, n),
                )

    def columns_of_tile(step):
        return pl.ds(pl.multiple_of(step * 128, 128), 128)

    def overlap(step, sums):
        columns = columns_of_tile(step)
        occ_re = occ_ref[0, :, columns]
        occ_im = occ_ref[1, :, columns]
        out = []
        for v in range(G):
            re = lifted[v, 0:1, columns]
            im = lifted[v, 1:2, columns]
            out.append(sums[2 * v] + (occ_re * re + occ_im * im))
            out.append(sums[2 * v + 1] + (occ_re * im - occ_im * re))
        return tuple(out)

    def three(ref, n):
        return ref.at[pl.ds(0, G - 1), :, pl.ds(n * BLOCK, BLOCK)]

    tiles = BLOCK // 128
    sums = tuple(jnp.zeros((16, 128), F32) for _ in range(2 * G))
    for n in range(blocks):
        wait(11 + n, 0, three(lifted, n))
        wait(11 + n, 1, three(lifted, n))
        sums = lax.fori_loop(n * tiles, (n + 1) * tiles, overlap, sums, unroll=4)
    lane = lax.broadcasted_iota(jnp.int32, (16, 128), 1)
    band_of = lane // 16
    own_row = (lane % 16) == lax.broadcasted_iota(jnp.int32, (16, 128), 0)
    matrix = jnp.zeros((16, 128), F32)
    for row in range(2 * G):
        column = jnp.sum(sums[row], axis=1, keepdims=True)
        matrix = jnp.where(band_of == row, column, matrix)
    over_send[0] = jnp.sum(jnp.where(own_row, matrix, 0.0), axis=0, keepdims=True)
    space_send(15, lambda peer: over_send.at[0], lambda mine: over_recv.at[mine])
    over_recv[me] = over_send[0]
    wait(15, 1, over_recv.at[pl.ds(0, S - 1)])
    row_sum = jnp.sum(over_recv[...], axis=0)
    lane = lax.broadcasted_iota(jnp.int32, (8, 128), 1)
    line = lax.broadcasted_iota(jnp.int32, (8, 128), 0)
    spread = jnp.where(lane // 16 == line, jnp.broadcast_to(row_sum, (8, 128)), 0.0)
    for shift in (64, 32, 16):
        spread = spread + pltpu.roll(spread, shift, axis=1)
    crossed = jnp.where(
        line % 2 == 0, -pltpu.roll(spread, 7, axis=0), pltpu.roll(spread, 1, axis=0)
    )
    weights = jnp.where(lane // 16 % 2 == 0, spread, crossed)
    weights_high = weights.astype(BF16).astype(F32)
    weights = jnp.where(lane < 64, weights_high, weights - weights_high).astype(BF16)[:, :96]

    def correct(step, carry):
        columns = columns_at(step, READ)
        result = jnp.dot(weights, occ_split[:, columns], preferred_element_type=F32)
        for v in range(G):
            for part in range(2):
                corr[v, part : part + 1, columns] = result[2 * v + part : 2 * v + part + 1]
        return carry

    for n in range(blocks):
        lax.fori_loop(n * per_block, (n + 1) * per_block, correct, 0, unroll=2)
        band_send(
            16 + n, lambda peer: block(corr, peer, n), lambda mine: block(corr_recv, mine, n)
        )

    corr_recv[group] = corr[group]
    beta_old = beta_ref[0:1].reshape(1, 1)
    partial = [jnp.zeros((1, 1), F32) for _ in range(4)]
    for n in range(blocks):
        wait(16 + n, 1, three(corr_recv, n))
        columns = pl.ds(n * BLOCK, BLOCK)
        for part in range(2):
            removed = (
                corr_recv[0, part : part + 1, columns]
                + corr_recv[1, part : part + 1, columns]
                + corr_recv[2, part : part + 1, columns]
                + corr_recv[3, part : part + 1, columns]
            )
            q = now_ref[part, 0:1, columns]
            p = prev_ref[part, 0:1, columns]
            u = lifted[group, part : part + 1, columns] - removed - beta_old * p
            rest_ref[part, 0:1, columns] = u
            for slot, product in enumerate((u * u, q * u, q * p, q * q)):
                partial[slot] = partial[slot] + jnp.sum(product, axis=1, keepdims=True)
    lane = lax.broadcasted_iota(jnp.int32, (1, 128), 1)
    row = jnp.zeros((1, 128), F32)
    for slot in range(4):
        row = jnp.where(lane == slot, partial[slot], row)
    sum_send1[0] = row
    here_low = lax.rem(me, LOW)
    here_high = me // LOW
    for step in range(1, G * LOW):
        peer_band = lax.rem(group + step // LOW, G)
        peer_low = lax.rem(here_low + step % LOW, LOW)
        pltpu.make_async_remote_copy(
            src_ref=sum_send1.at[0],
            dst_ref=sum_recv1.at[group * LOW + here_low],
            send_sem=sems.at[20, 0],
            recv_sem=sems.at[20, 1],
            device_id={"band": peer_band, "space": here_high * LOW + peer_low},
            device_id_type=MESH,
        ).start()
    sum_recv1[group * LOW + here_low] = sum_send1[0]
    wait(20, 1, sum_recv1.at[pl.ds(0, G * LOW - 1)])
    sum_send2[0] = jnp.sum(sum_recv1[...], axis=0)
    for step in range(1, HIGH):
        peer_high = lax.rem(here_high + step, HIGH)
        pltpu.make_async_remote_copy(
            src_ref=sum_send2.at[0],
            dst_ref=sum_recv2.at[here_high],
            send_sem=sems.at[21, 0],
            recv_sem=sems.at[21, 1],
            device_id={"space": peer_high * LOW + here_low},
            device_id_type=MESH,
        ).start()
    sum_recv2[here_high] = sum_send2[0]

    for part in range(3):
        wait(part, 0, send1.at[every_chunk])
        wait(8 + part, 0, send2.at[every_chunk])
    for t in range(4):
        wait(W_PHASE[t], 0, w_send.at[pl.ds(0, G - 1), :, tile_at(t)])
    wait(4, 0, h_send1.at[pl.ds(0, (S - 1) * HROWS)])
    wait(6, 0, h_send2.at[pl.ds(0, (S - 1) * HROWS)])
    wait(15, 0, over_recv.at[pl.ds(0, S - 1)])
    for n in range(blocks):
        wait(16 + n, 0, three(corr, n))
    wait(20, 0, sum_recv1.at[pl.ds(0, G * LOW - 1)])

    wait(21, 0, sum_recv2.at[pl.ds(0, HIGH - 1)])
    wait(21, 1, sum_recv2.at[pl.ds(0, HIGH - 1)])
    row = jnp.sum(sum_recv2[...], axis=0)

    def pick(slot):
        return jnp.sum(jnp.where(lane == slot, row, 0.0), axis=1, keepdims=True)

    norm_u, q_u, q_p, norm_q = [pick(slot) for slot in range(4)]
    alpha = (q_u + beta_old * q_p) / ENTRIES
    square = norm_u - 2.0 * alpha * q_u + alpha * alpha * norm_q
    beta_new = jnp.sqrt(square / ENTRIES)
    scalars_ref[...] = jnp.where(lane == 0, alpha, beta_new)


def finish(rest_ref, now_ref, scalars_ref, pot_in, next_ref, coef_ref, pot_ref):
    alpha = scalars_ref[0:1, 0:1]
    beta_new = scalars_ref[0:1, 1:2]
    inverse = 1.0 / beta_new
    for part in range(2):
        next_ref[part] = (rest_ref[part] - alpha * now_ref[part]) * inverse
    coef_ref[...] = scalars_ref[0:1, 0:2]
    pot_ref[...] = pot_in[...]


def per_device(
    lanczos_now,
    lanczos_prev,
    beta_prev,
    orbitals,
    band_energy,
    occupied,
    local_pot,
    xc_kernel,
    miller,
):
    later = [lanczos_prev, orbitals, occupied, local_pot, xc_kernel]
    later += [jnp.asarray(table) for table in make_tables()]
    later += [beta_prev, band_energy]
    vmem = pl.BlockSpec(memory_space=pltpu.VMEM)
    in_hbm = pl.BlockSpec(memory_space=pltpu.HBM)
    wide = pltpu.VMEM((3 * S * CELL, 128), F32)
    narrow = pltpu.VMEM((S * HROWS, 128), F32)
    quarter = pltpu.VMEM((G, S, HL), F32)
    band_waves = pltpu.VMEM((G, 2, WAVES), F32)
    real_grid = jax.ShapeDtypeStruct((PL, N, N), F32)
    waves = jax.ShapeDtypeStruct((2, 1, WAVES), F32)
    rest, scalars, potential = pl.pallas_call(
        body,
        out_shape=(waves, jax.ShapeDtypeStruct((1, 128), F32), real_grid),
        in_specs=[vmem, vmem] + [in_hbm] * len(later),
        out_specs=(vmem, vmem, vmem),
        scratch_shapes=[pltpu.VMEM(array.shape, array.dtype) for array in later]
        + [
            pltpu.VMEM((PL * N, WAVES), BF16),
            pltpu.VMEM((PL * N, 256), F32),
            wide,
            wide,
            pltpu.VMEM((PL * N, 384), F32),
            pltpu.VMEM((PL * N, 384), F32),
            pltpu.VMEM((PL * N, 384), F32),
            quarter,
            quarter,
            quarter,
            quarter,
            narrow,
            narrow,
            narrow,
            narrow,
            wide,
            wide,
            pltpu.VMEM((N, 4 * N), BF16),
            pltpu.VMEM((96, WAVES), BF16),
            band_waves,
            pltpu.VMEM((1, 1, 128), F32),
            pltpu.VMEM((S, 1, 128), F32),
            band_waves,
            band_waves,
            pltpu.VMEM((1, 1, 128), F32),
            pltpu.VMEM((G * LOW, 1, 128), F32),
            pltpu.VMEM((1, 1, 128), F32),
            pltpu.VMEM((HIGH, 1, 128), F32),
            pltpu.SemaphoreType.DMA((28, 2)),
            pltpu.SemaphoreType.DMA((len(later),)),
        ],
        compiler_params=pltpu.CompilerParams(
            collective_id=0, has_side_effects=True, vmem_limit_bytes=60 * 1024 * 1024
        ),
    )(lanczos_now, miller, *later)
    return pl.pallas_call(
        finish,
        out_shape=(waves, jax.ShapeDtypeStruct((1, 2), F32), real_grid),
        in_specs=[vmem] * 4,
        out_specs=(vmem,) * 3,
    )(rest, lanczos_now, scalars, potential)


def solution(mesh):
    return jax.shard_map(
        per_device,
        mesh=mesh,
        in_specs=(
            P(None, "band", "space"),
            P(None, "band", "space"),
            P(),
            P(None, "band", "space", None, None),
            P("band"),
            P(None, "band", "space"),
            P("space", None, None),
            P("space", None, None),
            P(None, "space"),
        ),
        out_specs=(P(None, "band", "space"), P(), P("space", None, None)),
        check_vma=False,
    )
```

```python
import math

import jax
import jax.numpy as jnp
import ml_dtypes
import numpy as np
from jax import lax
from jax.experimental import pallas as pl
from jax.experimental.pallas import tpu as pltpu
from jax.sharding import PartitionSpec as P

MESH = pl.DeviceIdType.MESH
F32 = jnp.float32
BF16 = jnp.bfloat16
KINETIC = 8.0
HARTREE = 4.0
N = 192
S = 64
G = 4
PL = 3
CELL = 9
HROWS = 4
QUART = N // G
THIRD = PL * QUART
HL = 512
LOW = 4
HIGH = S // LOW
TILE = 64
WAVES = 16384
PLACE = 4096
READ = 2048
HALF = N // 2
BLOCK = 4096
W_PHASE = (3, 22, 23, 24)
H_PHASE = (7, 25, 26, 27)
STRIDE = 29
ENTRIES = float(2 * G * WAVES * S)


def split_np(table):
    high = table.astype(np.float32).astype(ml_dtypes.bfloat16)
    low = (table - high.astype(np.float64)).astype(np.float32).astype(ml_dtypes.bfloat16)
    return high, low


def left_table(table):
    high, low = split_np(table)
    return np.concatenate([high, low], axis=0)


def right_table(table):
    high, low = split_np(table)
    return np.concatenate([high, high, low], axis=0)


def make_tables():
    index = np.arange(N)
    angle = 2.0 * np.pi * (np.outer(index, index) % N) / N
    cosine = np.cos(angle) / math.sqrt(N)
    sine = np.sin(angle) / math.sqrt(N)
    order = np.concatenate([np.arange(S) * PL + part for part in range(PL)])
    re_lane = index // TILE * 128 + index % TILE
    im_lane = re_lane + TILE

    def lanes(sign):
        table = np.zeros((2 * N, 2 * N))
        table[np.ix_(re_lane, re_lane)] = cosine
        table[np.ix_(im_lane, re_lane)] = -sign * sine
        table[np.ix_(re_lane, im_lane)] = sign * sine
        table[np.ix_(im_lane, im_lane)] = cosine
        return table

    def rows(sign, row_order, column_order):
        both = [
            cosine[row_order][:, column_order],
            sign * sine[row_order][:, column_order],
        ]
        return left_table(np.concatenate(both, axis=0))

    cas = cosine + sine
    cas_in = np.zeros((2 * N, N))
    cas_in[re_lane] = cas
    cas_in[im_lane] = cas
    plus = lanes(1.0)
    return (
        np.stack([right_table(plus[t * 128 : (t + 1) * 128]) for t in range(3)]),
        right_table(lanes(-1.0)),
        rows(1.0, order, index),
        rows(1.0, index, order),
        np.stack([rows(-1.0, order[b * S : (b + 1) * S], index) for b in range(PL)]),
        rows(-1.0, index, order),
        right_table(cas_in),
        right_table(cas_in.T),
        left_table(cas[order]),
        left_table(cas[:, order]),
    )


def split(values):
    high = values.astype(BF16)
    low = (values - high.astype(F32)).astype(BF16)
    return high, low


def left(table_ref, values, parts=None):
    high, low = parts or split(values)
    rows = table_ref.shape[0] // 2
    by_high = jnp.dot(table_ref[...], high, preferred_element_type=F32)
    by_low = jnp.dot(table_ref[0:rows], low, preferred_element_type=F32)
    return by_high[0:rows] + (by_high[rows:] + by_low)


def right(values, table):
    high, low = split(values)
    stacked = jnp.concatenate([high, low, high], axis=1)
    return jnp.dot(stacked, table, preferred_element_type=F32)


def times_i(values):
    lane = lax.broadcasted_iota(jnp.int32, (values.shape[0], 128), 1)
    tiles = []
    for t in range(values.shape[1] // 128):
        turned = pltpu.roll(values[:, t * 128 : (t + 1) * 128], TILE, axis=1)
        tiles.append(jnp.where(lane < TILE, -turned, turned))
    return jnp.concatenate(tiles, axis=1)


def left_complex(table_ref, values, parts=None):
    both = left(table_ref, values, parts)
    rows = table_ref.shape[0] // 4
    return both[0:rows] + times_i(both[rows:])


def signed(indices):
    return jnp.where(indices < N // 2, indices, indices - N)


def doubled(values):
    tiles = []
    for t in range(3):
        part = values[:, t * TILE : (t + 1) * TILE]
        tiles += [part, part]
    return jnp.concatenate(tiles, axis=1)


def body(*refs):
    now_ref, miller_ref = refs[:2]
    later = refs[2:19]
    rest_ref, scalars_ref, pot_ref = refs[19:22]
    held = refs[22:39]
    (
        prev_ref,
        orbit_ref,
        occ_ref,
        local_ref,
        xc_ref,
        lane_plus,
        lane_minus,
        a_plus,
        b_plus,
        b_minus,
        a_minus,
        cas_in,
        cas_out,
        cas_rows,
        cas_cols,
        beta_ref,
        energy_ref,
    ) = held
    (
        hot,
        acc,
        send1,
        recv1,
        fields,
        packed,
        xc_part,
        w_send,
        w_recv,
        d_all,
        h_all,
        h_send1,
        h_recv1,
        h_send2,
        h_recv2,
        send2,
        recv2,
        table,
        occ_split,
        lifted,
        over_send,
        over_recv,
        corr,
        corr_recv,
        sum_send1,
        sum_recv1,
        sum_send2,
        sum_recv2,
        sems,
        load_sems,
    ) = refs[39:]
    me = lax.axis_index("space")
    group = lax.axis_index("band")
    start = me * PL

    def load(at):
        return pltpu.make_async_copy(later[at], held[at], load_sems.at[at])

    for at in range(len(later)):
        load(at).start()

    barrier = pltpu.get_barrier_semaphore()

    def greet(turn, carry):
        for step in range(7):
            peer = lax.rem(me + (turn * 7 + step + 1) * STRIDE, S)
            pl.semaphore_signal(barrier, inc=1, device_id={"space": peer}, device_id_type=MESH)
        return carry

    lax.fori_loop(0, (S - 1) // 7, greet, 0)
    for step in range(1, G):
        for low in range(LOW):
            peer = me // LOW * LOW + lax.rem(me + low, LOW)
            pl.semaphore_signal(
                barrier,
                inc=1,
                device_id={"band": lax.rem(group + step, G), "space": peer},
                device_id_type=MESH,
            )

    def space_send(phase, source, target):
        def one(turn, carry):
            for step in range(7):
                peer = lax.rem(me + (turn * 7 + step + 1) * STRIDE, S)
                pltpu.make_async_remote_copy(
                    src_ref=source(peer),
                    dst_ref=target(me),
                    send_sem=sems.at[phase, 0],
                    recv_sem=sems.at[phase, 1],
                    device_id={"space": peer},
                    device_id_type=MESH,
                ).start()
            return carry

        lax.fori_loop(0, (S - 1) // 7, one, 0)

    def band_send(phase, source, target):
        for step in (2, 1, 3):
            peer = lax.rem(group + step, G)
            pltpu.make_async_remote_copy(
                src_ref=source(peer),
                dst_ref=target(group),
                send_sem=sems.at[phase, 0],
                recv_sem=sems.at[phase, 1],
                device_id={"band": peer},
                device_id_type=MESH,
            ).start()

    def wait(phase, side, region):
        pltpu.make_async_copy(region, region, sems.at[phase, side]).wait()

    def part_chunk(ref, part):
        return lambda at: ref.at[pl.ds(part * S * CELL + at * CELL, CELL)]

    def chunk(ref):
        return lambda at: ref.at[pl.ds(at * HROWS, HROWS)]

    def keep(source, target, first, rows):
        own = pl.ds(first + me * rows, rows)
        target[own, :] = source[own, :]

    def cell_rows(part, m):
        return pl.ds(part * S * CELL + m, S, stride=CELL)

    def columns_at(step, size):
        return pl.ds(pl.multiple_of(step * size, size), size)

    def place(tile):
        def one(step, carry):
            columns = columns_at(step, PLACE)
            if tile == 0:
                row = (miller_ref[1:2, columns] - start) * N + miller_ref[0:1, columns]
                where = lax.broadcasted_iota(jnp.int16, (PL * N, PLACE), 0)
                seen = jnp.where(where == row.astype(jnp.int16), BF16(1), BF16(0))
                hot[:, columns] = seen
            else:
                seen = hot[:, columns]
            third = (miller_ref[2:3, columns] - tile * TILE).astype(jnp.int16)
            mask = lax.broadcasted_iota(jnp.int16, (TILE, PLACE), 0) == third
            parts = [jnp.where(mask, value, BF16(0)) for value in values_of(columns)]
            product = lax.dot_general(
                seen,
                jnp.concatenate(parts, axis=0),
                (((1,), (1,)), ((), ())),
                preferred_element_type=F32,
            )
            acc[...] += product
            return carry

        acc[...] = jnp.zeros_like(acc)
        lax.fori_loop(0, WAVES // PLACE, one, 0)

    def values_of(columns):
        re_high, re_low = split(now_ref[0, 0:1, columns])
        im_high, im_low = split(now_ref[1, 0:1, columns])
        return re_high, im_high, re_low, im_low

    for t in range(3):
        place(t)
        placed = acc[:, 0:128] + acc[:, 128:256]
        if t == 0:
            load(7).wait()
        result = left_complex(
            a_plus, jnp.concatenate([placed[b * N : (b + 1) * N] for b in range(PL)], axis=1)
        )
        for r in range(PL):
            for b in range(PL):
                send1[cell_rows(t, r * PL + b), :] = result[
                    r * S : (r + 1) * S, b * 128 : (b + 1) * 128
                ]
        if t == 0:
            pl.semaphore_wait(barrier, S - 1 + (G - 1) * LOW)
        space_send(t, part_chunk(send1, t), part_chunk(recv1, t))
        keep(send1, recv1, t * S * CELL, CELL)

    for at in range(len(later)):
        if at != 7:
            load(at).wait()

    for r in range(PL):
        re = orbit_ref[0, 0, r]
        im = orbit_ref[1, 0, r]
        pieces = []
        for t in range(3):
            pieces += [re[:, t * TILE : (t + 1) * TILE], im[:, t * TILE : (t + 1) * TILE]]
        packed[r * N : (r + 1) * N] = jnp.concatenate(pieces, axis=1)

    every_chunk = pl.ds(0, (S - 1) * CELL)
    for t in range(3):
        wait(t, 1, recv1.at[every_chunk])
        values = jnp.concatenate(
            [
                jnp.concatenate([recv1[cell_rows(t, r * PL + b), :] for r in range(PL)], axis=1)
                for b in range(PL)
            ],
            axis=0,
        )
        result = left_complex(b_plus, values)
        result = jnp.concatenate([result[:, r * 128 : (r + 1) * 128] for r in range(PL)], axis=0)
        result = right(result, lane_plus[t])
        if t == 0:
            fields[...] = result
        else:
            fields[...] += result

    def tile_at(t):
        return pl.ds(t * 128, 128)

    tails = [[] for _ in range(G)]
    for r in range(PL):
        plane = pl.ds(r * N, N)
        values = left(cas_rows, right(2.0 * fields[plane, :] * packed[plane, :], cas_in[...]))
        for g in range(G):
            row = jnp.concatenate(
                [
                    values[b * S : (b + 1) * S, g * QUART : (g + 1) * QUART]
                    for b in range(PL)
                ],
                axis=1,
            )
            w_send[g, :, tile_at(r)] = row[:, :128]
            tails[g].append(row[:, 128:])
        if r == PL - 1:
            for g in range(G):
                w_send[g, :, tile_at(PL)] = jnp.concatenate(
                    tails[g] + [jnp.zeros((S, HL - PL * THIRD), F32)], axis=1
                )
        for t in (r,) if r < PL - 1 else (r, PL):
            band_send(
                W_PHASE[t],
                lambda peer: w_send.at[peer, :, tile_at(t)],
                lambda mine: w_recv.at[mine, :, tile_at(t)],
            )

    w_recv[group] = w_send[group]
    totals = []
    for t in range(4):
        wait(W_PHASE[t], 1, w_recv.at[pl.ds(0, G - 1), :, tile_at(t)])
        parts = [w_recv[g, :, tile_at(t)] for g in range(G)]
        totals.append(parts[0] + parts[1] + parts[2] + parts[3])
        h_send1[pl.ds(t, S, stride=HROWS), :] = totals[t]
    total = jnp.concatenate(totals, axis=1)
    space_send(4, chunk(h_send1), chunk(h_recv1))
    d_all[group] = total
    band_send(5, lambda peer: d_all.at[group], lambda mine: d_all.at[mine])
    keep(h_send1, h_recv1, 0, HROWS)

    lane = lax.broadcasted_iota(jnp.int32, (N, PL * QUART), 1)
    first = signed(lax.broadcasted_iota(jnp.int32, (N, PL * QUART), 0))
    plane = jnp.where(lane >= QUART, 1, 0) + jnp.where(lane >= 2 * QUART, 1, 0)
    second = signed(plane + start)
    third = signed(lane - plane * QUART + group * QUART)
    squared = first * first + second * second + third * third
    coulomb = jnp.where(squared > 0, HARTREE / jnp.maximum(squared, 1).astype(F32), 0.0)

    wait(4, 1, h_recv1.at[pl.ds(0, (S - 1) * HROWS)])
    pieces = [h_recv1[pl.ds(t, S, stride=HROWS), :] for t in range(4)]
    tall = jnp.concatenate(
        [
            jnp.concatenate([pieces[r], pieces[PL][:, r * 16 : (r + 1) * 16]], axis=1)
            for r in range(PL)
        ],
        axis=0,
    )
    tall = left(cas_rows, coulomb * left(cas_cols, tall))
    for r in range(PL):
        h_send2[pl.ds(r, S, stride=HROWS), :] = tall[r * S : (r + 1) * S, :128]
    h_send2[pl.ds(PL, S, stride=HROWS), :] = jnp.concatenate(
        [tall[r * S : (r + 1) * S, 128:] for r in range(PL)]
        + [jnp.zeros((S, HL - PL * THIRD), F32)],
        axis=1,
    )
    space_send(6, chunk(h_send2), chunk(h_recv2))
    keep(h_send2, h_recv2, 0, HROWS)

    def grid_values(ref, r):
        rows = [
            jnp.concatenate(
                [ref[g, :, tile_at(r)], ref[g, :, tile_at(PL)][:, r * 16 : (r + 1) * 16]], axis=1
            )
            for g in range(G)
        ]
        values = jnp.concatenate(
            [
                jnp.concatenate([row[:, b * QUART : (b + 1) * QUART] for row in rows], axis=1)
                for b in range(PL)
            ],
            axis=0,
        )
        return right(left(cas_cols, values), cas_out[...])

    wait(5, 0, d_all.at[pl.ds(0, G - 1)])
    wait(5, 1, d_all.at[pl.ds(0, G - 1)])
    for r in range(PL):
        plane = pl.ds(r * N, N)
        known = grid_values(d_all, r) * doubled(xc_ref[r])
        fields[plane, :] = doubled(local_ref[r]) * fields[plane, :] + known * packed[plane, :]
        xc_part[plane, :] = known

    wait(6, 1, h_recv2.at[pl.ds(0, (S - 1) * HROWS)])
    for t in (PL, 0, 1, 2):
        h_all[group, :, tile_at(t)] = h_recv2[pl.ds(t, S, stride=HROWS), :]
        band_send(
            H_PHASE[t],
            lambda peer: h_all.at[group, :, tile_at(t)],
            lambda mine: h_all.at[mine, :, tile_at(t)],
        )
    mixed = []
    for r in range(PL):
        plane = pl.ds(r * N, N)
        for t in (PL, 0) if r == 0 else (r,):
            wait(H_PHASE[t], 0, h_all.at[pl.ds(0, G - 1), :, tile_at(t)])
            wait(H_PHASE[t], 1, h_all.at[pl.ds(0, G - 1), :, tile_at(t)])
        hartree = grid_values(h_all, r)
        mixed.append(right(fields[plane, :] + hartree * packed[plane, :], lane_minus[...]))
        xc_part[plane, :] += hartree
    parts = split(jnp.concatenate(mixed, axis=1))
    for b in range(PL):
        result = left_complex(b_minus.at[b], None, parts)
        for r in range(PL):
            for t in range(3):
                send2[cell_rows(b, r * PL + t), :] = result[
                    :, (r * 3 + t) * 128 : (r * 3 + t + 1) * 128
                ]
        space_send(8 + b, part_chunk(send2, b), part_chunk(recv2, b))
        keep(send2, recv2, b * S * CELL, CELL)
    potential = xc_part[...]
    for r in range(PL):
        pot_ref[r] = jnp.concatenate(
            [potential[r * N : (r + 1) * N, t * 128 : t * 128 + TILE] for t in range(3)], axis=1
        )

    energy = energy_ref[0:1].reshape(1, 1)

    def read_waves(b, columns):
        seen = hot[b * N : (b + 1) * N, columns]
        third = miller_ref[2:3, columns]
        upper = third >= HALF
        upper_bit = jnp.where(upper, 1.0, 0.0).astype(BF16)
        high_part = seen * upper_bit
        low_part = seen - high_part
        found = jnp.dot(
            table[...],
            jnp.concatenate([low_part, low_part, high_part, high_part], axis=0),
            preferred_element_type=F32,
        )
        mask = lax.broadcasted_iota(jnp.int32, (HALF, READ), 0) == jnp.where(
            upper, third - HALF, third
        )
        sums = [
            jnp.sum(
                jnp.where(mask, found[half * HALF : (half + 1) * HALF], 0.0),
                axis=0,
                keepdims=True,
            )
            for half in range(2)
        ]
        for half in range(2):
            lifted[group, half : half + 1, columns] += sums[half]

    blocks = WAVES // BLOCK
    per_block = BLOCK // READ

    for n in range(blocks):
        columns = pl.ds(n * BLOCK, BLOCK)
        index = [signed(miller_ref[d : d + 1, columns]) for d in range(3)]
        squared = index[0] * index[0] + index[1] * index[1] + index[2] * index[2]
        diagonal = KINETIC * squared.astype(F32) / float(N * N) - energy
        for half in range(2):
            lifted[group, half : half + 1, columns] = diagonal * now_ref[half, 0:1, columns]
        high, low = split(
            jnp.concatenate([occ_ref[0, :, columns], occ_ref[1, :, columns]], axis=0)
        )
        occ_split[0:32, columns] = high
        occ_split[32:64, columns] = low
        occ_split[64:96, columns] = high

    def block(ref, at, n):
        return ref.at[at, :, pl.ds(n * BLOCK, BLOCK)]

    for b in range(PL):
        wait(8 + b, 1, recv2.at[every_chunk])
        values = jnp.concatenate(
            [
                jnp.concatenate([recv2[cell_rows(b, r * PL + t), :] for t in range(3)], axis=1)
                for r in range(PL)
            ],
            axis=0,
        )
        turned = jnp.transpose(left_complex(a_minus, values))
        pieces = []
        for side in range(2):
            rows = []
            for half in range(2):
                whole = jnp.concatenate(
                    [
                        turned[t * 128 + half * TILE : t * 128 + (half + 1) * TILE]
                        for t in range(3)
                    ],
                    axis=0,
                )
                rows.append(whole[side * HALF : (side + 1) * HALF])
            rows = jnp.concatenate(rows, axis=0)
            high = rows.astype(BF16).astype(F32)
            pieces += [high, rows - high]
        table[...] = jnp.concatenate(pieces, axis=1).astype(BF16)

        def one(step, carry):
            read_waves(b, columns_at(step, READ))
            return carry

        for n in range(blocks):
            lax.fori_loop(n * per_block, (n + 1) * per_block, one, 0)
            if b == PL - 1:
                band_send(
                    11 + n,
                    lambda peer: block(lifted, group, n),
                    lambda mine: block(lifted, mine, n),
                )

    def columns_of_tile(step):
        return pl.ds(pl.multiple_of(step * 128, 128), 128)

    def overlap(step, sums):
        columns = columns_of_tile(step)
        occ_re = occ_ref[0, :, columns]
        occ_im = occ_ref[1, :, columns]
        out = []
        for v in range(G):
            re = lifted[v, 0:1, columns]
            im = lifted[v, 1:2, columns]
            out.append(sums[2 * v] + (occ_re * re + occ_im * im))
            out.append(sums[2 * v + 1] + (occ_re * im - occ_im * re))
        return tuple(out)

    def three(ref, n):
        return ref.at[pl.ds(0, G - 1), :, pl.ds(n * BLOCK, BLOCK)]

    tiles = BLOCK // 128
    sums = tuple(jnp.zeros((16, 128), F32) for _ in range(2 * G))
    for n in range(blocks):
        wait(11 + n, 0, three(lifted, n))
        wait(11 + n, 1, three(lifted, n))
        sums = lax.fori_loop(n * tiles, (n + 1) * tiles, overlap, sums, unroll=4)
    lane = lax.broadcasted_iota(jnp.int32, (16, 128), 1)
    band_of = lane // 16
    own_row = (lane % 16) == lax.broadcasted_iota(jnp.int32, (16, 128), 0)
    matrix = jnp.zeros((16, 128), F32)
    for row in range(2 * G):
        column = jnp.sum(sums[row], axis=1, keepdims=True)
        matrix = jnp.where(band_of == row, column, matrix)
    over_send[0] = jnp.sum(jnp.where(own_row, matrix, 0.0), axis=0, keepdims=True)
    space_send(15, lambda peer: over_send.at[0], lambda mine: over_recv.at[mine])
    over_recv[me] = over_send[0]
    wait(15, 1, over_recv.at[pl.ds(0, S - 1)])
    row_sum = jnp.sum(over_recv[...], axis=0)
    lane = lax.broadcasted_iota(jnp.int32, (8, 128), 1)
    line = lax.broadcasted_iota(jnp.int32, (8, 128), 0)
    spread = jnp.where(lane // 16 == line, jnp.broadcast_to(row_sum, (8, 128)), 0.0)
    for shift in (64, 32, 16):
        spread = spread + pltpu.roll(spread, shift, axis=1)
    crossed = jnp.where(
        line % 2 == 0, -pltpu.roll(spread, 7, axis=0), pltpu.roll(spread, 1, axis=0)
    )
    weights = jnp.where(lane // 16 % 2 == 0, spread, crossed)
    weights_high = weights.astype(BF16).astype(F32)
    weights = jnp.where(lane < 64, weights_high, weights - weights_high).astype(BF16)[:, :96]

    def correct(step, carry):
        columns = columns_at(step, READ)
        result = jnp.dot(weights, occ_split[:, columns], preferred_element_type=F32)
        for v in range(G):
            for part in range(2):
                corr[v, part : part + 1, columns] = result[2 * v + part : 2 * v + part + 1]
        return carry

    for n in range(blocks):
        lax.fori_loop(n * per_block, (n + 1) * per_block, correct, 0, unroll=2)
        band_send(
            16 + n, lambda peer: block(corr, peer, n), lambda mine: block(corr_recv, mine, n)
        )

    corr_recv[group] = corr[group]
    beta_old = beta_ref[0:1].reshape(1, 1)
    partial = [jnp.zeros((1, 1), F32) for _ in range(4)]
    for n in range(blocks):
        wait(16 + n, 1, three(corr_recv, n))
        columns = pl.ds(n * BLOCK, BLOCK)
        for part in range(2):
            removed = (
                corr_recv[0, part : part + 1, columns]
                + corr_recv[1, part : part + 1, columns]
                + corr_recv[2, part : part + 1, columns]
                + corr_recv[3, part : part + 1, columns]
            )
            q = now_ref[part, 0:1, columns]
            p = prev_ref[part, 0:1, columns]
            u = lifted[group, part : part + 1, columns] - removed - beta_old * p
            rest_ref[part, 0:1, columns] = u
            for slot, product in enumerate((u * u, q * u, q * p, q * q)):
                partial[slot] = partial[slot] + jnp.sum(product, axis=1, keepdims=True)
    lane = lax.broadcasted_iota(jnp.int32, (1, 128), 1)
    row = jnp.zeros((1, 128), F32)
    for slot in range(4):
        row = jnp.where(lane == slot, partial[slot], row)
    sum_send1[0] = row
    here_low = lax.rem(me, LOW)
    here_high = me // LOW
    for step in range(1, G * LOW):
        peer_band = lax.rem(group + step // LOW, G)
        peer_low = lax.rem(here_low + step % LOW, LOW)
        pltpu.make_async_remote_copy(
            src_ref=sum_send1.at[0],
            dst_ref=sum_recv1.at[group * LOW + here_low],
            send_sem=sems.at[20, 0],
            recv_sem=sems.at[20, 1],
            device_id={"band": peer_band, "space": here_high * LOW + peer_low},
            device_id_type=MESH,
        ).start()
    sum_recv1[group * LOW + here_low] = sum_send1[0]
    wait(20, 1, sum_recv1.at[pl.ds(0, G * LOW - 1)])
    sum_send2[0] = jnp.sum(sum_recv1[...], axis=0)
    for step in range(1, HIGH):
        peer_high = lax.rem(here_high + step, HIGH)
        pltpu.make_async_remote_copy(
            src_ref=sum_send2.at[0],
            dst_ref=sum_recv2.at[here_high],
            send_sem=sems.at[21, 0],
            recv_sem=sems.at[21, 1],
            device_id={"space": peer_high * LOW + here_low},
            device_id_type=MESH,
        ).start()
    sum_recv2[here_high] = sum_send2[0]

    for part in range(3):
        wait(part, 0, send1.at[every_chunk])
        wait(8 + part, 0, send2.at[every_chunk])
    for t in range(4):
        wait(W_PHASE[t], 0, w_send.at[pl.ds(0, G - 1), :, tile_at(t)])
    wait(4, 0, h_send1.at[pl.ds(0, (S - 1) * HROWS)])
    wait(6, 0, h_send2.at[pl.ds(0, (S - 1) * HROWS)])
    wait(15, 0, over_recv.at[pl.ds(0, S - 1)])
    for n in range(blocks):
        wait(16 + n, 0, three(corr, n))
    wait(20, 0, sum_recv1.at[pl.ds(0, G * LOW - 1)])

    wait(21, 0, sum_recv2.at[pl.ds(0, HIGH - 1)])
    wait(21, 1, sum_recv2.at[pl.ds(0, HIGH - 1)])
    row = jnp.sum(sum_recv2[...], axis=0)

    def pick(slot):
        return jnp.sum(jnp.where(lane == slot, row, 0.0), axis=1, keepdims=True)

    norm_u, q_u, q_p, norm_q = [pick(slot) for slot in range(4)]
    alpha = (q_u + beta_old * q_p) / ENTRIES
    square = norm_u - 2.0 * alpha * q_u + alpha * alpha * norm_q
    beta_new = jnp.sqrt(square / ENTRIES)
    scalars_ref[...] = jnp.where(lane == 0, alpha, beta_new)


def finish(rest_ref, now_ref, scalars_ref, pot_in, next_ref, coef_ref, pot_ref):
    alpha = scalars_ref[0:1, 0:1]
    beta_new = scalars_ref[0:1, 1:2]
    inverse = 1.0 / beta_new
    for part in range(2):
        next_ref[part] = (rest_ref[part] - alpha * now_ref[part]) * inverse
    coef_ref[...] = scalars_ref[0:1, 0:2]
    pot_ref[...] = pot_in[...]


def per_device(
    lanczos_now,
    lanczos_prev,
    beta_prev,
    orbitals,
    band_energy,
    occupied,
    local_pot,
    xc_kernel,
    miller,
):
    later = [lanczos_prev, orbitals, occupied, local_pot, xc_kernel]
    later += [jnp.asarray(table) for table in make_tables()]
    later += [beta_prev, band_energy]
    vmem = pl.BlockSpec(memory_space=pltpu.VMEM)
    in_hbm = pl.BlockSpec(memory_space=pltpu.HBM)
    wide = pltpu.VMEM((3 * S * CELL, 128), F32)
    narrow = pltpu.VMEM((S * HROWS, 128), F32)
    quarter = pltpu.VMEM((G, S, HL), F32)
    band_waves = pltpu.VMEM((G, 2, WAVES), F32)
    real_grid = jax.ShapeDtypeStruct((PL, N, N), F32)
    waves = jax.ShapeDtypeStruct((2, 1, WAVES), F32)
    rest, scalars, potential = pl.pallas_call(
        body,
        out_shape=(waves, jax.ShapeDtypeStruct((1, 128), F32), real_grid),
        in_specs=[vmem, vmem] + [in_hbm] * len(later),
        out_specs=(vmem, vmem, vmem),
        scratch_shapes=[pltpu.VMEM(array.shape, array.dtype) for array in later]
        + [
            pltpu.VMEM((PL * N, WAVES), BF16),
            pltpu.VMEM((PL * N, 256), F32),
            wide,
            wide,
            pltpu.VMEM((PL * N, 384), F32),
            pltpu.VMEM((PL * N, 384), F32),
            pltpu.VMEM((PL * N, 384), F32),
            quarter,
            quarter,
            quarter,
            quarter,
            narrow,
            narrow,
            narrow,
            narrow,
            wide,
            wide,
            pltpu.VMEM((N, 4 * N), BF16),
            pltpu.VMEM((96, WAVES), BF16),
            band_waves,
            pltpu.VMEM((1, 1, 128), F32),
            pltpu.VMEM((S, 1, 128), F32),
            band_waves,
            band_waves,
            pltpu.VMEM((1, 1, 128), F32),
            pltpu.VMEM((G * LOW, 1, 128), F32),
            pltpu.VMEM((1, 1, 128), F32),
            pltpu.VMEM((HIGH, 1, 128), F32),
            pltpu.SemaphoreType.DMA((28, 2)),
            pltpu.SemaphoreType.DMA((len(later),)),
        ],
        compiler_params=pltpu.CompilerParams(
            collective_id=0, has_side_effects=True, vmem_limit_bytes=60 * 1024 * 1024
        ),
    )(lanczos_now, miller, *later)
    return pl.pallas_call(
        finish,
        out_shape=(waves, jax.ShapeDtypeStruct((1, 2), F32), real_grid),
        in_specs=[vmem] * 4,
        out_specs=(vmem,) * 3,
    )(rest, lanczos_now, scalars, potential)


def solution(mesh):
    return jax.shard_map(
        per_device,
        mesh=mesh,
        in_specs=(
            P(None, "band", "space"),
            P(None, "band", "space"),
            P(),
            P(None, "band", "space", None, None),
            P("band"),
            P(None, "band", "space"),
            P("space", None, None),
            P("space", None, None),
            P(None, "space"),
        ),
        out_specs=(P(None, "band", "space"), P(), P("space", None, None)),
        check_vma=False,
    )
```
